256 devices in a mesh: gx: 16 (over y, z_lo, core), gy: 16 (over x, z_hi).
Axes of the slice: x: 4, y: 4, z: 8 (z_hi: 4, z_lo: 2; z = z_hi * 2 + z_lo), core: 2. Of those that a mesh axis runs over, the one named last changes fastest.
Arguments:
- load: float32 [3, 256, 256, 128], P(None, 'gx', 'gy'), may hold values from -24 to 24
- guess: float32 [3, 256, 256, 128], P(None, 'gx', 'gy'), may hold values from -1.2 to 1.2
- labels: int32 [256, 256, 128], P('gx', 'gy'), may hold values from 0 to 2
- segments: int32 [256, 256, 128], P('gx', 'gy'), may hold values from 0 to 15
- stiffness: float32 [6, 48], replicated, as said below
Outputs:
- displacement: float32 [3, 256, 256, 128], P(None, 'gx', 'gy')
- residual: float32 [3, 256, 256, 128], P(None, 'gx', 'gy')
The draws below stay inside these ranges and needn't reach their ends.
Inputs may be any that keep to these rules, and one draw needn't show every extreme that they name: `stiffness`: for each of the 48 entries the six values form a symmetric positive definite 3x3 matrix.
All inputs are finite; a program needn't handle non-finite values.
Results may differ from the reference program's by a relative error of at most 0.00018.
Values sent between devices are 32-bit elements; how exact they have to be, the bound alone decides.
A program may use at most 64 MiB of HBM per device.

```python
import jax
import jax.numpy as jnp

NZ = 128
SEGS = 16
ITERS = 2
MATERIALS = 48
NX = 256
NY = 256


def draw_stiffness(key, part):
    key = jax.random.fold_in(key, 7)
    key_diag, key_coupling = jax.random.split(key)
    diagonal = jax.random.uniform(key_diag, (3, MATERIALS), jnp.float32, 2.0, 8.0)
    coupling = jax.random.uniform(key_coupling, (3, MATERIALS), jnp.float32, -0.4, 0.4)
    entry_xy = coupling[0] * jnp.sqrt(diagonal[0] * diagonal[1])
    entry_xz = coupling[1] * jnp.sqrt(diagonal[0] * diagonal[2])
    entry_yz = coupling[2] * jnp.sqrt(diagonal[1] * diagonal[2])
    return jnp.concatenate([diagonal, jnp.stack([entry_xy, entry_xz, entry_yz])], axis=0)


def touch_ends(array, stream_key, least, high):
    longest = array.shape.index(max(array.shape))
    spots = []
    for shift in (0, 1):
        where = [jax.random.randint(jax.random.fold_in(stream_key, axis), (), 0, length) for axis, length in enumerate(array.shape)]
        where[longest] = (where[longest] + shift) % array.shape[longest]
        spots.append(tuple(where))
    return array.at[spots[0]].set(least).at[spots[1]].set(high)


def steps_of(rng, shape, shards, low, top_value):
    gain = 1.0
    for dim, blocks in shards:
        heights = jax.random.uniform(jax.random.fold_in(jax.random.fold_in(rng, 6), dim), (blocks,), jnp.float32, low / len(shards), top_value / len(shards))
        gain = gain * jnp.repeat(jnp.exp(heights), shape[dim] // blocks).reshape((-1,) + (1,) * (len(shape) - 1 - dim))
    return gain


def normal_values(rng, extent, deviation, bound, cuts=(), held_as=jnp.bfloat16):
    entries = jax.random.normal(rng, extent, jnp.float32) * deviation
    if len(cuts) > 0:
        entries = steps_of(rng, extent, cuts, -0.22, 0.18) * entries
    return jnp.clip(entries, min=-bound, max=bound).astype(held_as)


def setup_inputs(seed: int = 0) -> dict:
    key_list = jax.random.split(jax.random.key(seed), 6)
    return {
        "load": normal_values(key_list[0], (3, NX, NY, NZ), 4.0, 24.0, ((1, 16), (2, 16)), jnp.float32),
        "guess": normal_values(key_list[1], (3, NX, NY, NZ), 0.2, 1.2, ((1, 16), (2, 16)), jnp.float32),
        "labels": touch_ends(jax.random.randint(key_list[2], (NX, NY, NZ), 0, 3), jax.random.fold_in(key_list[2], 1), 0, 2).astype(jnp.int32),
        "segments": touch_ends(jax.random.randint(key_list[3], (NX, NY, NZ), 0, SEGS), jax.random.fold_in(key_list[3], 1), 0, SEGS - 1).astype(jnp.int32),
        "stiffness": draw_stiffness(jax.random.fold_in(key_list[5], 71), 0),
    }


theta_value = 1.025
delta_value = 0.975


def extend_whole(field, signs):
    wrapped = jnp.concatenate([field[:, :, -1:], field, field[:, :, :1]], axis=2)
    scaling = jnp.asarray(signs, jnp.float32).reshape(-1, 1, 1)
    low_ghost = wrapped[:, 0, ::-1] * scaling
    high_ghost = wrapped[:, -1, ::-1] * scaling
    return jnp.concatenate([low_ghost[:, None], wrapped, high_ghost[:, None]], axis=1)


def smooth(padded):
    along_x = padded[:, 1:-1] + 0.5 * (padded[:, :-2] + padded[:, 2:])
    along_y = along_x[:, :, 1:-1] + 0.5 * (along_x[:, :, :-2] + along_x[:, :, 2:])
    return along_y[..., 1:-1] + 0.5 * (along_y[..., :-2] + along_y[..., 2:])


def sym_apply(coef, vector):
    return jnp.stack([
        coef[0] * vector[0] + coef[3] * vector[1] + coef[4] * vector[2],
        coef[3] * vector[0] + coef[1] * vector[1] + coef[5] * vector[2],
        coef[4] * vector[0] + coef[5] * vector[1] + coef[2] * vector[2]])


def operate(field, coef_ext, coef_sum):
    field_ext = extend_whole(field, (-1.0, -1.0, 1.0))
    product_ext = sym_apply(coef_ext, field_ext)
    stacked = jnp.concatenate([field_ext, product_ext], axis=0)
    sums = smooth(jnp.pad(stacked, ((0, 0), (0, 0), (0, 0), (1, 1))))
    interior = coef_ext[:, 1:-1, 1:-1]
    product = product_ext[:, 1:-1, 1:-1]
    return 0.5 * (8.0 * product + sym_apply(coef_sum, field) - sym_apply(interior, sums[:3]) - sums[3:])


def reference(load, guess, labels, segments, stiffness):
    codes = (labels * SEGS + segments).astype(jnp.int32)
    coef = stiffness[:, codes]
    coef_ext = extend_whole(coef, (1.0, 1.0, 1.0, 1.0, -1.0, -1.0))
    coef_sum = smooth(jnp.pad(coef_ext, ((0, 0), (0, 0), (0, 0), (1, 1)), mode="edge"))
    interior = coef_ext[:, 1:-1, 1:-1]
    inverse = 1.0 / (0.5 * (6.0 * interior[:3] + coef_sum[:3]))
    sigma = theta_value / delta_value
    residual = load - operate(guess, coef_ext, coef_sum)
    rho_prev = 1.0 / sigma
    update = inverse * residual / theta_value
    displacement = guess + update
    for iteration in range(1, ITERS):
        residual = load - operate(displacement, coef_ext, coef_sum)
        rho_now = 1.0 / (2.0 * sigma - rho_prev)
        update = rho_now * rho_prev * update + (2.0 * rho_now / delta_value) * inverse * residual
        displacement = displacement + update
        rho_prev = rho_now
    return displacement, residual
```

```python
import functools

import jax
import jax.numpy as jnp
from jax import lax
from jax.experimental import pallas as pl
from jax.experimental.pallas import tpu as pltpu
from jax.sharding import PartitionSpec as P

SEGS = 16
MESH = pl.DeviceIdType.MESH
f32 = jnp.float32

theta_value = 1.025
delta_value = 0.975
sigma_value = theta_value / delta_value
rho_first = 1.0 / sigma_value
rho_second = 1.0 / (2.0 * sigma_value - rho_first)

W = 16
ROWS = W + 6
RING = W + 8
HI, LO, MIRROR = W + 2, 0, W + 4


def routes(gx, gy):
    nx, ny = lax.axis_size("gx"), lax.axis_size("gy")
    first, last = gx == 0, gx == nx - 1
    xl = jnp.where(first, 0, gx - 1)
    xh = jnp.where(last, nx - 1, gx + 1)
    down, up = lax.rem(gy + ny - 1, ny), lax.rem(gy + 1, ny)
    mid = ny - 1 - gy
    mid_down, mid_up = lax.rem(mid + ny - 1, ny), lax.rem(mid + 1, ny)
    pick = jnp.where
    return [
        ((gx, down), 1),
        ((gx, up), 0),
        ((xl, pick(first, mid, gy)), pick(first, 2, 3)),
        ((xh, pick(last, mid, gy)), pick(last, 3, 2)),
        ((xl, pick(first, mid_up, down)), pick(first, 4, 7)),
        ((xl, pick(first, mid_down, up)), pick(first, 5, 6)),
        ((xh, pick(last, mid_up, down)), pick(last, 6, 5)),
        ((xh, pick(last, mid_down, up)), pick(last, 7, 4)),
    ]


def pieces(width, first, last):
    xs_lo, xs_hi = pl.ds(0, width), pl.ds(W - width, width)
    whole = pl.ds(0, W)
    to_lo = jnp.where(first, MIRROR, HI)
    to_hi = jnp.where(last, MIRROR + 2 - width, LO + 2 - width)
    xd_lo, xd_hi = pl.ds(to_lo, width), pl.ds(to_hi, width)
    yd_lo, yd_hi = pl.ds(W, width), pl.ds(RING - width, width)
    block = pl.ds(2, W)
    return [
        (whole, xs_lo, block, yd_lo),
        (whole, xs_hi, block, yd_hi),
        (xs_lo, whole, xd_lo, whole),
        (xs_hi, whole, xd_hi, whole),
        (xs_lo, xs_lo, xd_lo, yd_lo),
        (xs_lo, xs_hi, xd_lo, yd_hi),
        (xs_hi, xs_lo, xd_hi, yd_lo),
        (xs_hi, xs_hi, xd_hi, yd_hi),
    ]


def sym_apply(c, u):
    return (
        c[0] * u[0] + c[3] * u[1] + c[4] * u[2],
        c[3] * u[0] + c[1] * u[1] + c[5] * u[2],
        c[4] * u[0] + c[5] * u[1] + c[2] * u[2],
    )


def ring_sum(h):
    return (h + h) + (pltpu.roll(h, 1, 0) + pltpu.roll(h, RING - 1, 0))


def depth_sum(h, repeat):
    lane = lax.broadcasted_iota(jnp.int32, h.shape, 1)
    end = h if repeat else jnp.zeros_like(h)
    below = jnp.where(lane == 0, end, pltpu.roll(h, 1, 1))
    above = jnp.where(lane == 127, end, pltpu.roll(h, 127, 1))
    return (h + h) + (below + above)


def kernel(
    load, guess, labels, segments, table, out_u, out_r,
    u_ext, l_ext, k_ext, c_ext, v_ext, d_ext, inv, cs_ext, lab, seg, local_sem, send_sem, recv_sem,
):
    gx, gy = lax.axis_index("gx"), lax.axis_index("gy")
    first, last = gx == 0, gx == lax.axis_size("gx") - 1
    own = (pl.ds(2, W), pl.ds(0, W))
    fetch = [
        pltpu.make_async_copy(labels, lab, local_sem.at[0]),
        pltpu.make_async_copy(segments, seg, local_sem.at[1]),
        pltpu.make_async_copy(guess, u_ext.at[:, *own], local_sem.at[2]),
        pltpu.make_async_copy(load, l_ext.at[:, *own], local_sem.at[3]),
    ]
    for copy in fetch:
        copy.start()
    k_ext[:, W:RING] = jnp.zeros((ROWS, 8, 128), jnp.int32)
    k_ext[0:2, 0:W] = jnp.zeros((2, W, 128), jnp.int32)
    k_ext[HI:ROWS, 0:W] = jnp.zeros((4, W, 128), jnp.int32)

    to = routes(gx, gy)
    here = [None] * 4 + [jnp.logical_and(d[0] == gx, d[1] == gy) for d, _ in to[4:]]
    barrier = pltpu.get_barrier_semaphore()
    expected = 4
    for (device, _), same in zip(to, here):
        if same is None:
            pl.semaphore_signal(barrier, inc=1, device_id=device, device_id_type=MESH)
        else:

            @pl.when(jnp.logical_not(same))
            def _():
                pl.semaphore_signal(barrier, inc=1, device_id=device, device_id_type=MESH)

            expected = expected + jnp.where(same, 0, 1)
    pl.semaphore_wait(barrier, expected)

    def view(ref, x, y):
        return ref.at[:, x, y] if len(ref.shape) == 4 else ref.at[x, y]

    def send(kind, src, dst, width, shift):
        copies = []
        for n, (xs, ys, xd, yd) in enumerate(pieces(width, first, last)):
            device, slot = to[n]
            source = view(src, pl.ds(xs.start + shift, xs.size), ys)
            target = view(dst, xd, yd)
            copy = pltpu.make_async_remote_copy(
                src_ref=source,
                dst_ref=target,
                send_sem=send_sem.at[kind, n],
                recv_sem=recv_sem.at[kind, slot],
                device_id=device,
                device_id_type=MESH,
            )
            if here[n] is None:
                copy.start()
            else:
                local = pltpu.make_async_copy(source, target, recv_sem.at[kind, slot])
                pl.when(jnp.logical_not(here[n]))(copy.start)
                pl.when(here[n])(local.start)
            copies.append(copy)
        return copies

    def receive(kind, dst, width):
        whole, block = pl.ds(0, W), pl.ds(2, W)
        xr, yr = pl.ds(0, width), pl.ds(W, width)
        for slot in range(8):
            part = (block, yr) if slot < 2 else (xr, whole) if slot < 4 else (xr, yr)
            ref = view(dst, *part)
            pltpu.make_async_copy(ref, ref, recv_sem.at[kind, slot]).wait()

    sent = send(0, guess, u_ext, 2, 0)
    fetch[0].wait()
    fetch[1].wait()
    k_ext[2:HI, 0:W] = lab[...] * SEGS + seg[...]
    sent += send(1, k_ext, k_ext, 2, 2)
    sent += send(2, load, l_ext, 1, 0)
    fetch[2].wait()
    fetch[3].wait()

    def lookup(x, rows, size, sign):
        codes = k_ext[x, pl.ds(rows, size)]
        for entry in range(6):
            line = jnp.broadcast_to(table[entry : entry + 1, :], (size, 128))
            value = jnp.take_along_axis(line, codes, axis=1, mode="promise_in_bounds")
            if entry >= 4 and sign is not None:
                value = value * sign
            c_ext[entry, x, pl.ds(rows, size)] = value

    @pl.loop(2, HI)
    def _(x):
        lookup(x, 0, W, None)

    receive(0, u_ext, 2)
    receive(1, k_ext, 2)
    receive(2, l_ext, 1)

    turn = 7 - lax.broadcasted_iota(jnp.int32, (8, 128), 0)

    def turned(tile):
        return jnp.take_along_axis(tile, turn, axis=0, mode="promise_in_bounds")

    @pl.when(jnp.logical_or(first, last))
    def _():
        base = jnp.where(first, LO, HI)
        for j in range(2):
            for to_tile, from_tile in ((0, 1), (1, 0), (2, 2)):
                dst, src = pl.ds(8 * to_tile, 8), pl.ds(8 * from_tile, 8)
                k_ext[base + j, dst] = turned(k_ext[MIRROR + 1 - j, src])
                for c, s in enumerate((-1.0, -1.0, 1.0)):
                    u_ext[c, base + j, dst] = s * turned(u_ext[c, MIRROR + 1 - j, src])
                    l_ext[c, base + j, dst] = s * turned(l_ext[c, MIRROR + 1 - j, src])

    @pl.loop(2, HI)
    def _(x):
        lookup(x, W, 8, None)

    low_sign = jnp.where(first, -1.0, 1.0)
    high_sign = jnp.where(last, -1.0, 1.0)
    for x, sign in ((0, low_sign), (1, low_sign), (HI, high_sign), (HI + 1, high_sign)):
        lookup(x, 0, RING, sign)

    @pl.loop(0, W + 4)
    def _(x):
        v = sym_apply([c_ext[e, x] for e in range(6)], [u_ext[c, x] for c in range(3)])
        for c in range(3):
            v_ext[c, x] = v[c]

    def rows_sum(ref, e, x):
        return (ref[e, x - 1] + ref[e, x + 1]) + 2.0 * ref[e, x]

    @pl.loop(1, W + 3)
    def _(x):
        c = [c_ext[e, x] for e in range(6)]
        u = [u_ext[k, x] for k in range(3)]
        c_sum = [depth_sum(ring_sum(rows_sum(c_ext, e, x)), True) for e in range(6)]
        u_sum = [depth_sum(ring_sum(rows_sum(u_ext, k, x)), False) for k in range(3)]
        v_sum = [depth_sum(ring_sum(rows_sum(v_ext, k, x)), False) for k in range(3)]
        near = sym_apply(c, [64.0 * u[k] - u_sum[k] for k in range(3)])
        far = sym_apply(c_sum, u)
        for k in range(3):
            r = l_ext[k, x] - 0.0625 * (near[k] + far[k] - v_sum[k])
            inverse = 16.0 / (48.0 * c[k] + c_sum[k])
            d_ext[k, x] = u[k] + (inverse * r) * (1.0 / theta_value)
            inv[k, x] = inverse
        for e in range(6):
            cs_ext[e, x] = c_sum[e]

    @pl.loop(1, W + 3)
    def _(x):
        v = sym_apply([c_ext[e, x] for e in range(6)], [d_ext[k, x] for k in range(3)])
        for k in range(3):
            v_ext[k, x] = v[k]

    @pl.loop(2, HI)
    def _(x):
        c = [c_ext[e, x, 0:W] for e in range(6)]
        c_sum = [cs_ext[e, x, 0:W] for e in range(6)]
        d = [d_ext[k, x, 0:W] for k in range(3)]
        u_sum = [depth_sum(ring_sum(rows_sum(d_ext, k, x))[0:W], False) for k in range(3)]
        v_sum = [depth_sum(ring_sum(rows_sum(v_ext, k, x))[0:W], False) for k in range(3)]
        near = sym_apply(c, [64.0 * d[k] - u_sum[k] for k in range(3)])
        far = sym_apply(c_sum, d)
        for k in range(3):
            r = l_ext[k, x, 0:W] - 0.0625 * (near[k] + far[k] - v_sum[k])
            step = d[k] - u_ext[k, x, 0:W]
            step = (rho_second * rho_first) * step + (2.0 * rho_second / delta_value) * inv[k, x, 0:W] * r
            out_u[k, x - 2] = d[k] + step
            out_r[k, x - 2] = r

    for n, copy in enumerate(sent):
        if here[n % 8] is None:
            copy.wait_send()
        else:
            pl.when(jnp.logical_not(here[n % 8]))(copy.wait_send)


def write(u, r, out_u, out_r, sem):
    copies = [
        pltpu.make_async_copy(u, out_u, sem.at[0]),
        pltpu.make_async_copy(r, out_r, sem.at[1]),
    ]
    for copy in copies:
        copy.start()
    for copy in copies:
        copy.wait()


def body(load, guess, labels, segments, stiffness):
    table = jnp.pad(stiffness, ((0, 2), (0, 128 - stiffness.shape[1])))
    vmem = pl.BlockSpec(memory_space=pltpu.VMEM)
    anywhere = pl.BlockSpec(memory_space=pl.ANY)
    shape = load.shape
    wide = (ROWS, RING, 128)
    results = pl.pallas_call(
        kernel,
        out_shape=[pltpu.VMEM(shape, f32)] * 2,
        in_specs=[anywhere] * 4 + [vmem],
        out_specs=[vmem] * 2,
        scratch_shapes=[
            pltpu.VMEM((3,) + wide, f32),
            pltpu.VMEM((3,) + wide, f32),
            pltpu.VMEM(wide, jnp.int32),
            pltpu.VMEM((6,) + wide, f32),
            pltpu.VMEM((3,) + wide, f32),
            pltpu.VMEM((3,) + wide, f32),
            pltpu.VMEM((3,) + wide, f32),
            pltpu.VMEM((6,) + wide, f32),
            pltpu.VMEM((W, W, 128), jnp.int32),
            pltpu.VMEM((W, W, 128), jnp.int32),
            pltpu.SemaphoreType.DMA((4,)),
            pltpu.SemaphoreType.DMA((3, 8)),
            pltpu.SemaphoreType.DMA((3, 8)),
        ],
        compiler_params=pltpu.CompilerParams(
            collective_id=0, has_side_effects=True, vmem_limit_bytes=40 * 2**20
        ),
    )(load, guess, labels, segments, table)
    results = [pltpu.with_memory_space_constraint(x, pltpu.VMEM) for x in results]
    return tuple(
        pl.pallas_call(
            write,
            out_shape=[jax.ShapeDtypeStruct(shape, f32)] * 2,
            in_specs=[vmem] * 2,
            out_specs=[anywhere] * 2,
            scratch_shapes=[pltpu.SemaphoreType.DMA((2,))],
        )(*results)
    )


def solution(mesh):
    field = P(None, "gx", "gy", None)
    voxel = P("gx", "gy", None)
    return jax.shard_map(
        body,
        mesh=mesh,
        in_specs=(field, field, voxel, voxel, P()),
        out_specs=(field, field),
        check_vma=False,
    )
```

```python
import functools

import jax
import jax.numpy as jnp
from jax import lax
from jax.experimental import pallas as pl
from jax.experimental.pallas import tpu as pltpu
from jax.sharding import PartitionSpec as P

SEGS = 16
MESH = pl.DeviceIdType.MESH
f32 = jnp.float32

theta_value = 1.025
delta_value = 0.975
sigma_value = theta_value / delta_value
rho_first = 1.0 / sigma_value
rho_second = 1.0 / (2.0 * sigma_value - rho_first)

W = 16
ROWS = W + 6
RING = W + 8
HI, LO, MIRROR = W + 2, 0, W + 4


def routes(gx, gy):
    nx, ny = lax.axis_size("gx"), lax.axis_size("gy")
    first, last = gx == 0, gx == nx - 1
    xl = jnp.where(first, 0, gx - 1)
    xh = jnp.where(last, nx - 1, gx + 1)
    down, up = lax.rem(gy + ny - 1, ny), lax.rem(gy + 1, ny)
    mid = ny - 1 - gy
    mid_down, mid_up = lax.rem(mid + ny - 1, ny), lax.rem(mid + 1, ny)
    pick = jnp.where
    return [
        ((gx, down), 1),
        ((gx, up), 0),
        ((xl, pick(first, mid, gy)), pick(first, 2, 3)),
        ((xh, pick(last, mid, gy)), pick(last, 3, 2)),
        ((xl, pick(first, mid_up, down)), pick(first, 4, 7)),
        ((xl, pick(first, mid_down, up)), pick(first, 5, 6)),
        ((xh, pick(last, mid_up, down)), pick(last, 6, 5)),
        ((xh, pick(last, mid_down, up)), pick(last, 7, 4)),
    ]


def pieces(width, first, last):
    xs_lo, xs_hi = pl.ds(0, width), pl.ds(W - width, width)
    whole = pl.ds(0, W)
    to_lo = jnp.where(first, MIRROR, HI)
    to_hi = jnp.where(last, MIRROR + 2 - width, LO + 2 - width)
    xd_lo, xd_hi = pl.ds(to_lo, width), pl.ds(to_hi, width)
    yd_lo, yd_hi = pl.ds(W, width), pl.ds(RING - width, width)
    block = pl.ds(2, W)
    return [
        (whole, xs_lo, block, yd_lo),
        (whole, xs_hi, block, yd_hi),
        (xs_lo, whole, xd_lo, whole),
        (xs_hi, whole, xd_hi, whole),
        (xs_lo, xs_lo, xd_lo, yd_lo),
        (xs_lo, xs_hi, xd_lo, yd_hi),
        (xs_hi, xs_lo, xd_hi, yd_lo),
        (xs_hi, xs_hi, xd_hi, yd_hi),
    ]


def sym_apply(c, u):
    return (
        c[0] * u[0] + c[3] * u[1] + c[4] * u[2],
        c[3] * u[0] + c[1] * u[1] + c[5] * u[2],
        c[4] * u[0] + c[5] * u[1] + c[2] * u[2],
    )


def ring_sum(h):
    return (h + h) + (pltpu.roll(h, 1, 0) + pltpu.roll(h, RING - 1, 0))


def depth_sum(h, repeat):
    lane = lax.broadcasted_iota(jnp.int32, h.shape, 1)
    end = h if repeat else jnp.zeros_like(h)
    below = jnp.where(lane == 0, end, pltpu.roll(h, 1, 1))
    above = jnp.where(lane == 127, end, pltpu.roll(h, 127, 1))
    return (h + h) + (below + above)


def kernel(
    load, guess, labels, segments, stiffness, out_u, out_r,
    blocks, table, u_ext, l_ext, k_ext, c_ext, v_ext, d_ext, inv, cs_ext, lab, seg, local_sem, send_sem, recv_sem,
):
    gx, gy = lax.axis_index("gx"), lax.axis_index("gy")
    first, last = gx == 0, gx == lax.axis_size("gx") - 1
    own = (pl.ds(2, W), pl.ds(0, W))
    fetch = [
        pltpu.make_async_copy(labels, lab, local_sem.at[0]),
        pltpu.make_async_copy(segments, seg, local_sem.at[1]),
        pltpu.make_async_copy(guess, u_ext.at[:, *own], local_sem.at[2]),
        pltpu.make_async_copy(load, l_ext.at[:, *own], local_sem.at[3]),
        pltpu.make_async_copy(stiffness, blocks, local_sem.at[4]),
    ]
    for copy in fetch:
        copy.start()
    k_ext[:, W:RING] = jnp.zeros((ROWS, 8, 128), jnp.int32)
    k_ext[0:2, 0:W] = jnp.zeros((2, W, 128), jnp.int32)
    k_ext[HI:ROWS, 0:W] = jnp.zeros((4, W, 128), jnp.int32)

    to = routes(gx, gy)
    here = [None] * 4 + [jnp.logical_and(d[0] == gx, d[1] == gy) for d, _ in to[4:]]
    barrier = pltpu.get_barrier_semaphore()
    expected = 4
    for (device, _), same in zip(to, here):
        if same is None:
            pl.semaphore_signal(barrier, inc=1, device_id=device, device_id_type=MESH)
        else:

            @pl.when(jnp.logical_not(same))
            def _():
                pl.semaphore_signal(barrier, inc=1, device_id=device, device_id_type=MESH)

            expected = expected + jnp.where(same, 0, 1)
    pl.semaphore_wait(barrier, expected)

    def view(ref, x, y):
        return ref.at[:, x, y] if len(ref.shape) == 4 else ref.at[x, y]

    def send(kind, src, dst, width, shift):
        copies = []
        for n, (xs, ys, xd, yd) in enumerate(pieces(width, first, last)):
            device, slot = to[n]
            source = view(src, pl.ds(xs.start + shift, xs.size), ys)
            target = view(dst, xd, yd)
            copy = pltpu.make_async_remote_copy(
                src_ref=source,
                dst_ref=target,
                send_sem=send_sem.at[kind, n],
                recv_sem=recv_sem.at[kind, slot],
                device_id=device,
                device_id_type=MESH,
            )
            if here[n] is None:
                copy.start()
            else:
                local = pltpu.make_async_copy(source, target, recv_sem.at[kind, slot])
                pl.when(jnp.logical_not(here[n]))(copy.start)
                pl.when(here[n])(local.start)
            copies.append(copy)
        return copies

    def receive(kind, dst, width):
        whole, block = pl.ds(0, W), pl.ds(2, W)
        xr, yr = pl.ds(0, width), pl.ds(W, width)
        for slot in range(8):
            part = (block, yr) if slot < 2 else (xr, whole) if slot < 4 else (xr, yr)
            ref = view(dst, *part)
            pltpu.make_async_copy(ref, ref, recv_sem.at[kind, slot]).wait()

    sent = send(0, guess, u_ext, 2, 0)
    fetch[0].wait()
    fetch[1].wait()
    k_ext[2:HI, 0:W] = lab[...] * SEGS + seg[...]
    sent += send(1, k_ext, k_ext, 2, 2)
    sent += send(2, load, l_ext, 1, 0)
    fetch[2].wait()
    fetch[3].wait()
    fetch[4].wait()
    table[0:6, 0 : stiffness.shape[1]] = blocks[...]

    def lookup(x, rows, size, sign):
        codes = k_ext[x, pl.ds(rows, size)]
        for entry in range(6):
            line = jnp.broadcast_to(table[entry : entry + 1, :], (size, 128))
            value = jnp.take_along_axis(line, codes, axis=1, mode="promise_in_bounds")
            if entry >= 4 and sign is not None:
                value = value * sign
            c_ext[entry, x, pl.ds(rows, size)] = value

    @pl.loop(2, HI)
    def _(x):
        lookup(x, 0, W, None)

    receive(0, u_ext, 2)
    receive(1, k_ext, 2)
    receive(2, l_ext, 1)

    turn = 7 - lax.broadcasted_iota(jnp.int32, (8, 128), 0)

    def turned(tile):
        return jnp.take_along_axis(tile, turn, axis=0, mode="promise_in_bounds")

    @pl.when(jnp.logical_or(first, last))
    def _():
        base = jnp.where(first, LO, HI)
        for j in range(2):
            for to_tile, from_tile in ((0, 1), (1, 0), (2, 2)):
                dst, src = pl.ds(8 * to_tile, 8), pl.ds(8 * from_tile, 8)
                k_ext[base + j, dst] = turned(k_ext[MIRROR + 1 - j, src])
                for c, s in enumerate((-1.0, -1.0, 1.0)):
                    u_ext[c, base + j, dst] = s * turned(u_ext[c, MIRROR + 1 - j, src])
                    l_ext[c, base + j, dst] = s * turned(l_ext[c, MIRROR + 1 - j, src])

    @pl.loop(2, HI)
    def _(x):
        lookup(x, W, 8, None)

    low_sign = jnp.where(first, -1.0, 1.0)
    high_sign = jnp.where(last, -1.0, 1.0)
    for x, sign in ((0, low_sign), (1, low_sign), (HI, high_sign), (HI + 1, high_sign)):
        lookup(x, 0, RING, sign)

    @pl.loop(0, W + 4)
    def _(x):
        v = sym_apply([c_ext[e, x] for e in range(6)], [u_ext[c, x] for c in range(3)])
        for c in range(3):
            v_ext[c, x] = v[c]

    def rows_sum(ref, e, x):
        return (ref[e, x - 1] + ref[e, x + 1]) + 2.0 * ref[e, x]

    @pl.loop(1, W + 3)
    def _(x):
        c = [c_ext[e, x] for e in range(6)]
        u = [u_ext[k, x] for k in range(3)]
        c_sum = [depth_sum(ring_sum(rows_sum(c_ext, e, x)), True) for e in range(6)]
        u_sum = [depth_sum(ring_sum(rows_sum(u_ext, k, x)), False) for k in range(3)]
        v_sum = [depth_sum(ring_sum(rows_sum(v_ext, k, x)), False) for k in range(3)]
        near = sym_apply(c, [64.0 * u[k] - u_sum[k] for k in range(3)])
        far = sym_apply(c_sum, u)
        for k in range(3):
            r = l_ext[k, x] - 0.0625 * (near[k] + far[k] - v_sum[k])
            inverse = 16.0 / (48.0 * c[k] + c_sum[k])
            d_ext[k, x] = u[k] + (inverse * r) * (1.0 / theta_value)
            inv[k, x] = inverse
        for e in range(6):
            cs_ext[e, x] = c_sum[e]

    @pl.loop(1, W + 3)
    def _(x):
        v = sym_apply([c_ext[e, x] for e in range(6)], [d_ext[k, x] for k in range(3)])
        for k in range(3):
            v_ext[k, x] = v[k]

    @pl.loop(2, HI)
    def _(x):
        c = [c_ext[e, x, 0:W] for e in range(6)]
        c_sum = [cs_ext[e, x, 0:W] for e in range(6)]
        d = [d_ext[k, x, 0:W] for k in range(3)]
        u_sum = [depth_sum(ring_sum(rows_sum(d_ext, k, x))[0:W], False) for k in range(3)]
        v_sum = [depth_sum(ring_sum(rows_sum(v_ext, k, x))[0:W], False) for k in range(3)]
        near = sym_apply(c, [64.0 * d[k] - u_sum[k] for k in range(3)])
        far = sym_apply(c_sum, d)
        for k in range(3):
            r = l_ext[k, x, 0:W] - 0.0625 * (near[k] + far[k] - v_sum[k])
            step = d[k] - u_ext[k, x, 0:W]
            step = (rho_second * rho_first) * step + (2.0 * rho_second / delta_value) * inv[k, x, 0:W] * r
            out_u[k, x - 2] = d[k] + step
            out_r[k, x - 2] = r

    for n, copy in enumerate(sent):
        if here[n % 8] is None:
            copy.wait_send()
        else:
            pl.when(jnp.logical_not(here[n % 8]))(copy.wait_send)


def write(u, r, out_u, out_r, sem):
    copies = [
        pltpu.make_async_copy(u, out_u, sem.at[0]),
        pltpu.make_async_copy(r, out_r, sem.at[1]),
    ]
    for copy in copies:
        copy.start()
    for copy in copies:
        copy.wait()


def body(load, guess, labels, segments, stiffness):
    vmem = pl.BlockSpec(memory_space=pltpu.VMEM)
    anywhere = pl.BlockSpec(memory_space=pl.ANY)
    hbm = pl.BlockSpec(memory_space=pltpu.HBM)
    shape = load.shape
    wide = (ROWS, RING, 128)
    results = pl.pallas_call(
        kernel,
        out_shape=[pltpu.VMEM(shape, f32)] * 2,
        in_specs=[hbm] * 5,
        out_specs=[vmem] * 2,
        scratch_shapes=[
            pltpu.VMEM(stiffness.shape, f32),
            pltpu.VMEM((8, 128), f32),
            pltpu.VMEM((3,) + wide, f32),
            pltpu.VMEM((3,) + wide, f32),
            pltpu.VMEM(wide, jnp.int32),
            pltpu.VMEM((6,) + wide, f32),
            pltpu.VMEM((3,) + wide, f32),
            pltpu.VMEM((3,) + wide, f32),
            pltpu.VMEM((3,) + wide, f32),
            pltpu.VMEM((6,) + wide, f32),
            pltpu.VMEM((W, W, 128), jnp.int32),
            pltpu.VMEM((W, W, 128), jnp.int32),
            pltpu.SemaphoreType.DMA((5,)),
            pltpu.SemaphoreType.DMA((3, 8)),
            pltpu.SemaphoreType.DMA((3, 8)),
        ],
        compiler_params=pltpu.CompilerParams(
            collective_id=0, has_side_effects=True, vmem_limit_bytes=40 * 2**20
        ),
    )(*[pltpu.with_memory_space_constraint(x, pltpu.HBM) for x in (load, guess, labels, segments, stiffness)])
    results = [pltpu.with_memory_space_constraint(x, pltpu.VMEM) for x in results]
    return tuple(
        pl.pallas_call(
            write,
            out_shape=[jax.ShapeDtypeStruct(shape, f32)] * 2,
            in_specs=[vmem] * 2,
            out_specs=[anywhere] * 2,
            scratch_shapes=[pltpu.SemaphoreType.DMA((2,))],
        )(*results)
    )


def solution(mesh):
    field = P(None, "gx", "gy", None)
    voxel = P("gx", "gy", None)
    return jax.shard_map(
        body,
        mesh=mesh,
        in_specs=(field, field, voxel, voxel, P()),
        out_specs=(field, field),
        check_vma=False,
    )
```

```python
import functools

import jax
import jax.numpy as jnp
from jax import lax
from jax.experimental import pallas as pl
from jax.experimental.pallas import tpu as pltpu
from jax.sharding import PartitionSpec as P

SEGS = 16
MESH = pl.DeviceIdType.MESH
f32 = jnp.float32

theta_value = 1.025
delta_value = 0.975
sigma_value = theta_value / delta_value
rho_first = 1.0 / sigma_value
rho_second = 1.0 / (2.0 * sigma_value - rho_first)

W = 16
RING = W + 8
VALUES = 11
EARLY = 8
SIGNS = (-1.0, -1.0, 1.0) * 2 + (1.0, 1.0) + (-1.0, -1.0, 1.0)


def routes(gx, gy):
    nx, ny = lax.axis_size("gx"), lax.axis_size("gy")
    first, last = gx == 0, gx == nx - 1
    xl = jnp.where(first, 0, gx - 1)
    xh = jnp.where(last, nx - 1, gx + 1)
    down, up = lax.rem(gy + ny - 1, ny), lax.rem(gy + 1, ny)
    mid = ny - 1 - gy
    mid_down, mid_up = lax.rem(mid + ny - 1, ny), lax.rem(mid + 1, ny)
    pick = jnp.where
    return [
        ((gx, down), 1),
        ((gx, up), 0),
        ((xl, pick(first, mid, gy)), pick(first, 2, 3)),
        ((xh, pick(last, mid, gy)), pick(last, 3, 2)),
        ((xl, pick(first, mid_up, down)), (7, 4)),
        ((xl, pick(first, mid_down, up)), (6, 5)),
        ((xh, pick(last, mid_up, down)), (5, 6)),
        ((xh, pick(last, mid_down, up)), (4, 7)),
    ]


def sym_apply(c, u):
    return (
        c[0] * u[0] + c[3] * u[1] + c[4] * u[2],
        c[3] * u[0] + c[1] * u[1] + c[5] * u[2],
        c[4] * u[0] + c[5] * u[1] + c[2] * u[2],
    )


def along_row(h):
    n = h.shape[0]
    return (h + h) + (pltpu.roll(h, 1, 0) + pltpu.roll(h, n - 1, 0))


def along_depth(h, repeat=False):
    lane = lax.broadcasted_iota(jnp.int32, h.shape, 1)
    end = h if repeat else jnp.zeros_like(h)
    below = jnp.where(lane == 0, end, pltpu.roll(h, 1, 1))
    above = jnp.where(lane == 127, end, pltpu.roll(h, 127, 1))
    return (h + h) + (below + above)


def weigh(h, repeat=False):
    return along_depth(along_row(h), repeat)


def line(x):
    return pl.ds(W * x, W) if isinstance(x, int) else pl.ds(pl.multiple_of(W * x, W), W)


def kernel(
    load, guess, labels, segments, stiffness, u_own, r_own, d_own, inv_own,
    blocks, table, l_own, k_own, lab, seg, c_own, v_own, cs_own, snd, rcv, t2g, t2o, c_strip,
    local_sem, send_sem, late_send_sem, recv_sem, late_recv_sem,
):
    gx, gy = lax.axis_index("gx"), lax.axis_index("gy")
    first, last = gx == 0, gx == lax.axis_size("gx") - 1
    fetch = [
        pltpu.make_async_copy(labels, lab, local_sem.at[0]),
        pltpu.make_async_copy(segments, seg, local_sem.at[1]),
        pltpu.make_async_copy(guess, u_own, local_sem.at[2]),
        pltpu.make_async_copy(load, l_own, local_sem.at[3]),
        pltpu.make_async_copy(stiffness, blocks, local_sem.at[4]),
    ]
    for copy in fetch:
        copy.start()
    t2g[...] = jnp.zeros(t2g.shape, f32)

    to = routes(gx, gy)
    here = [None] * 4 + [jnp.logical_and(d[0] == gx, d[1] == gy) for d, _ in to[4:]]
    barrier = pltpu.get_barrier_semaphore()
    expected = 4
    for (device, _), same in zip(to, here):
        if same is None:
            pl.semaphore_signal(barrier, inc=1, device_id=device, device_id_type=MESH)
        else:

            @pl.when(jnp.logical_not(same))
            def _():
                pl.semaphore_signal(barrier, inc=1, device_id=device, device_id_type=MESH)

            expected = expected + jnp.where(same, 0, 1)

    t2o[...] = jnp.zeros(t2o.shape, f32)
    fetch[0].wait()
    fetch[1].wait()
    k_own[...] = (lab[...] * SEGS + seg[...]).astype(f32)
    fetch[2].wait()
    fetch[3].wait()
    sides = ((0, 1), (W - 1, W - 2))
    for s in range(4):
        for j in range(2):
            at = sides[s % 2][j]
            rows = pl.ds(at, W, stride=W) if s < 2 else line(at)
            for c in range(3):
                snd[s, 3 * j + c] = u_own[c, rows]
                if j == 0:
                    snd[s, EARLY + c] = l_own[c, rows]
            snd[s, 6 + j] = k_own[rows]
    fetch[4].wait()
    table[0:6, 0 : stiffness.shape[1]] = blocks[...]

    pl.semaphore_wait(barrier, expected)

    sent = []

    def send_edge(n, values, out_sem, in_sem):
        device, slot = to[n]
        copy = pltpu.make_async_remote_copy(
            src_ref=snd.at[n, values],
            dst_ref=rcv.at[slot, values],
            send_sem=out_sem.at[n],
            recv_sem=in_sem.at[slot],
            device_id=device,
            device_id_type=MESH,
        )
        copy.start()
        sent.append((copy, None))

    def corner_ref(slot):
        return t2g.at[slot % 2, :, pl.ds(6 if slot < 6 else 0, 2)]

    def send_corner(n):
        device, slots = to[n]
        mirrored = first if n < 6 else last
        source = snd.at[n % 2, :, pl.ds(0 if n < 6 else W - 2, 2)]
        for slot, chosen in zip(slots, (jnp.logical_not(mirrored), mirrored)):
            copy = pltpu.make_async_remote_copy(
                src_ref=source,
                dst_ref=corner_ref(slot),
                send_sem=send_sem.at[n],
                recv_sem=recv_sem.at[slot],
                device_id=device,
                device_id_type=MESH,
            )
            pl.when(jnp.logical_and(chosen, jnp.logical_not(here[n])))(copy.start)
            if slot == slots[1]:
                local = pltpu.make_async_copy(source, corner_ref(slot), recv_sem.at[slot])
                pl.when(jnp.logical_and(chosen, here[n]))(local.start)
        sent.append((copy, here[n]))

    early, late = pl.ds(0, EARLY), pl.ds(EARLY, VALUES - EARLY)
    for n in range(2):
        send_edge(n, early, send_sem, recv_sem)
    for n in range(4, 8):
        send_corner(n)
    for n in range(2, 4):
        send_edge(n, early, send_sem, recv_sem)
    for n in range(4):
        send_edge(n, late, late_send_sem, late_recv_sem)

    def receive(ref, sem):
        pltpu.make_async_copy(ref, ref, sem).wait()

    def lookup(codes, entry):
        rows = jnp.broadcast_to(table[entry : entry + 1, :], codes.shape)
        return jnp.take_along_axis(rows, codes, axis=1, mode="promise_in_bounds")

    inner_row = lax.broadcasted_iota(jnp.int32, (W, 128), 0)
    inner_row = jnp.logical_and(inner_row > 0, inner_row < W - 1)
    none = jnp.zeros((W, 128), f32)
    for x in (0, W - 1):
        for c in range(3):
            d_own[c, line(x)] = none
        for e in range(6):
            cs_own[e, line(x)] = none

    @pl.loop(0, W, unroll=4)
    def _(x):
        codes = k_own[line(x)].astype(jnp.int32)
        c = [lookup(codes, e) for e in range(6)]
        for e in range(6):
            c_own[e, line(x)] = c[e]
        v = sym_apply(c, [u_own[k, line(x)] for k in range(3)])
        for k in range(3):
            v_own[k, line(x)] = v[k]

    for s in range(4):
        for j in range(2):
            codes = snd[s, 6 + j].astype(jnp.int32)
            for e in range(6):
                c_strip[s, 2 + j, e, 0:W] = lookup(codes, e)

    def three(ref, e, x):
        return (ref[e, line(x - 1)] + ref[e, line(x + 1)]) + 2.0 * ref[e, line(x)]

    @pl.loop(1, W - 1, unroll=2)
    def _(x):
        c = [c_own[e, line(x)] for e in range(6)]
        u = [u_own[k, line(x)] for k in range(3)]
        c_sum = [weigh(three(c_own, e, x), True) for e in range(6)]
        u_sum = [weigh(three(u_own, k, x)) for k in range(3)]
        v_sum = [weigh(three(v_own, k, x)) for k in range(3)]
        near = sym_apply(c, [64.0 * u[k] - u_sum[k] for k in range(3)])
        far = sym_apply(c_sum, u)
        for k in range(3):
            r = l_own[k, line(x)] - 0.0625 * (near[k] + far[k] - v_sum[k])
            inverse = 16.0 / (48.0 * c[k] + c_sum[k])
            d = u[k] + (inverse * r) * (1.0 / theta_value)
            inv_own[k, line(x)] = inverse
            d_own[k, line(x)] = jnp.where(inner_row, d, 0.0)
        for e in range(6):
            cs_own[e, line(x)] = c_sum[e]

    @pl.loop(0, W, unroll=4)
    def _(x):
        v = sym_apply([c_own[e, line(x)] for e in range(6)], [d_own[k, line(x)] for k in range(3)])
        for k in range(3):
            v_own[k, line(x)] = v[k]

    def three_within(ref, e, x):
        below, above = jnp.maximum(x - 1, 0), jnp.minimum(x + 1, W - 1)
        return (ref[e, line(below)] + ref[e, line(above)]) + 2.0 * ref[e, line(x)]

    @pl.loop(0, W, unroll=2)
    def _(x):
        c = [c_own[e, line(x)] for e in range(6)]
        c_sum = [cs_own[e, line(x)] for e in range(6)]
        d = [d_own[k, line(x)] for k in range(3)]
        d_sum = [weigh(three_within(d_own, k, x)) for k in range(3)]
        v_sum = [weigh(three_within(v_own, k, x)) for k in range(3)]
        near = sym_apply(c, [64.0 * d[k] - d_sum[k] for k in range(3)])
        far = sym_apply(c_sum, d)
        for k in range(3):
            r_own[k, line(x)] = l_own[k, line(x)] - 0.0625 * (near[k] + far[k] - v_sum[k])

    turn = 7 - lax.broadcasted_iota(jnp.int32, (8, 128), 0)

    def turned(tile):
        return jnp.take_along_axis(tile, turn, axis=0, mode="promise_in_bounds")

    eight = lax.broadcasted_iota(jnp.int32, (8, 128), 0)
    low_sign = jnp.where(first, -1.0, 1.0)
    high_sign = jnp.where(last, -1.0, 1.0)
    end_sign = jnp.where(eight > 5, low_sign, jnp.where(eight < 2, high_sign, 1.0))

    def strip(s):
        ring = s < 2
        n = RING if ring else W

        def value(row, index):
            own = row > 1
            if not ring:
                return (snd if own else rcv)[s, index]
            ends = t2o if own else t2g
            return jnp.concatenate([(snd if own else rcv)[s, index], ends[s, index]], axis=0)

        def layer(row):
            return (1, 0, 0, 1)[row]

        for row in range(4):
            codes = value(row, 6 + layer(row)).astype(jnp.int32)
            if row < 2:
                for e in range(6):
                    entry = lookup(codes[0:W], e)
                    if e > 3 and not ring:
                        entry = entry * (low_sign if s == 2 else high_sign)
                    c_strip[s, row, e, 0:W] = entry
            if ring:
                for e in range(6):
                    entry = lookup(codes[W:RING], e)
                    c_strip[s, row, e, W:RING] = entry * end_sign if e > 3 else entry
        c = [[c_strip[s, row, e, 0:n] for e in range(6)] for row in range(4)]
        u = [[value(row, 3 * layer(row) + k) for k in range(3)] for row in range(4)]
        v = [sym_apply(c[row], u[row]) for row in range(4)]

        def three_rows(f, row, k):
            return (f[row - 1][k] + f[row + 1][k]) + 2.0 * f[row][k]

        part, inverse, c_sum = {}, {}, {}
        for row in (1, 2):
            c_sum[row] = [weigh(three_rows(c, row, e), True) for e in range(6)]
            u_sum = [weigh(three_rows(u, row, k)) for k in range(3)]
            v_sum = [weigh(three_rows(v, row, k)) for k in range(3)]
            near = sym_apply(c[row], [64.0 * u[row][k] - u_sum[k] for k in range(3)])
            far = sym_apply(c_sum[row], u[row])
            part[row] = [0.0625 * (near[k] + far[k] - v_sum[k]) for k in range(3)]
            inverse[row] = [16.0 / (48.0 * c[row][k] + c_sum[row][k]) for k in range(3)]

        receive(rcv.at[s, late], late_recv_sem.at[s])
        if not ring:
            turn_strip(s, range(EARLY, VALUES))
        d = {}
        for row in (1, 2):
            d[row] = []
            for k in range(3):
                r = value(row, EARLY + k) - part[row][k]
                step = u[row][k] + (inverse[row][k] * r) * (1.0 / theta_value)
                d[row].append(step if ring else jnp.where(inner_row, step, 0.0))
        v = {row: sym_apply(c[row], d[row]) for row in (1, 2)}
        d_sum = [weigh(d[1][k] + 2.0 * d[2][k])[0:W] for k in range(3)]
        v_sum = [weigh(v[1][k] + 2.0 * v[2][k])[0:W] for k in range(3)]
        c2 = [t[0:W] for t in c[2]]
        c3 = [t[0:W] for t in c[3]]
        d2 = [t[0:W] for t in d[2]]
        near = sym_apply(c2, [64.0 * d2[k] - d_sum[k] for k in range(3)])
        far = sym_apply([t[0:W] for t in c_sum[2]], d2)
        outer = [near[k] + far[k] - v_sum[k] for k in range(3)]
        d_sum = [weigh(d[2][k])[0:W] for k in range(3)]
        v_sum = [weigh(v[2][k])[0:W] for k in range(3)]
        near = sym_apply(c3, d_sum)
        nearer, farther = sides[s % 2]
        if ring:
            rows_0, rows_1 = pl.ds(nearer, W, stride=W), pl.ds(farther, W, stride=W)
        else:
            rows_0, rows_1 = line(nearer), line(farther)
        for k in range(3):
            r_own[k, rows_0] = r_own[k, rows_0] - 0.0625 * outer[k]
            r_own[k, rows_1] = r_own[k, rows_1] + 0.0625 * (near[k] + v_sum[k])
            d_own[k, rows_0] = d2[k]
            inv_own[k, rows_0] = inverse[2][k][0:W]

    def turn_strip(s, indices):
        @pl.when(first if s == 2 else last)
        def _():
            for i in indices:
                head, tail = rcv[s, i, 0:8], rcv[s, i, 8:W]
                rcv[s, i, 0:8] = SIGNS[i] * turned(tail)
                rcv[s, i, 8:W] = SIGNS[i] * turned(head)

    for s in (2, 3):
        receive(rcv.at[s, early], recv_sem.at[s])
        turn_strip(s, range(EARLY))
        strip(s)

    for s in range(2):
        for j in range(2):
            at = sides[s][j]
            for side, spot in ((2, (7, 6)), (3, (0, 1))):
                for i in range(2):
                    for c in range(3):
                        t2o[s, 3 * j + c, spot[i]] = rcv[side, 3 * i + c, at]
                    t2o[s, 6 + j, spot[i]] = rcv[side, 6 + i, at]
                if j == 0:
                    for c in range(3):
                        t2o[s, EARLY + c, spot[0]] = rcv[side, EARLY + c, at]

    for s in (1, 0):
        receive(rcv.at[s, early], recv_sem.at[s])
        for slot in (4 + s, 6 + s):
            receive(corner_ref(slot), recv_sem.at[slot])
        for mirrored, base in ((first, 6), (last, 0)):

            @pl.when(mirrored)
            def _():
                for i in range(VALUES):
                    one, two = t2g[s, i, base], t2g[s, i, base + 1]
                    t2g[s, i, base] = SIGNS[i] * two
                    t2g[s, i, base + 1] = SIGNS[i] * one

        strip(s)

    for copy, same in sent:
        if same is None:
            copy.wait_send()
        else:
            pl.when(jnp.logical_not(same))(copy.wait_send)


def finish(u, r, d, inv, out_u, out_r, result, sem):
    copies = [pltpu.make_async_copy(r, out_r, sem.at[3])]
    copies[0].start()
    for k in range(3):
        copies.append(pltpu.make_async_copy(result.at[k], out_u.at[k], sem.at[k]))

        @pl.loop(0, W, unroll=8)
        def _(x):
            step = d[k, line(x)] - u[k, line(x)]
            step = (rho_second * rho_first) * step
            step += (2.0 * rho_second / delta_value) * (inv[k, line(x)] * r[k, line(x)])
            result[k, line(x)] = d[k, line(x)] + step

        copies[-1].start()
    for copy in copies:
        copy.wait()


def body(load, guess, labels, segments, stiffness):
    vmem = pl.BlockSpec(memory_space=pltpu.VMEM)
    hbm = pl.BlockSpec(memory_space=pltpu.HBM)
    shape = load.shape
    field = (3, W * W, 128)
    inputs = (
        load.reshape(field),
        guess.reshape(field),
        labels.reshape(field[1:]),
        segments.reshape(field[1:]),
        stiffness,
    )
    results = pl.pallas_call(
        kernel,
        out_shape=[pltpu.VMEM(field, f32)] * 4,
        in_specs=[hbm] * 5,
        out_specs=[vmem] * 4,
        scratch_shapes=[
            pltpu.VMEM(stiffness.shape, f32),
            pltpu.VMEM((8, 128), f32),
            pltpu.VMEM(field, f32),
            pltpu.VMEM(field[1:], f32),
            pltpu.VMEM(field[1:], jnp.int32),
            pltpu.VMEM(field[1:], jnp.int32),
            pltpu.VMEM((6,) + field[1:], f32),
            pltpu.VMEM(field, f32),
            pltpu.VMEM((6,) + field[1:], f32),
            pltpu.VMEM((4, VALUES, W, 128), f32),
            pltpu.VMEM((4, VALUES, W, 128), f32),
            pltpu.VMEM((2, VALUES, 8, 128), f32),
            pltpu.VMEM((2, VALUES, 8, 128), f32),
            pltpu.VMEM((4, 4, 6, RING, 128), f32),
            pltpu.SemaphoreType.DMA((5,)),
            pltpu.SemaphoreType.DMA((8,)),
            pltpu.SemaphoreType.DMA((4,)),
            pltpu.SemaphoreType.DMA((8,)),
            pltpu.SemaphoreType.DMA((4,)),
        ],
        compiler_params=pltpu.CompilerParams(
            collective_id=0, has_side_effects=True, vmem_limit_bytes=40 * 2**20
        ),
    )(*[pltpu.with_memory_space_constraint(x, pltpu.HBM) for x in inputs])
    out_u, out_r = pl.pallas_call(
        finish,
        out_shape=[jax.ShapeDtypeStruct(field, f32)] * 2,
        in_specs=[vmem] * 4,
        out_specs=[hbm] * 2,
        scratch_shapes=[pltpu.VMEM(field, f32), pltpu.SemaphoreType.DMA((4,))],
    )(*[pltpu.with_memory_space_constraint(x, pltpu.VMEM) for x in results])
    return out_u.reshape(shape), out_r.reshape(shape)


def solution(mesh):
    field = P(None, "gx", "gy", None)
    voxel = P("gx", "gy", None)
    return jax.shard_map(
        body,
        mesh=mesh,
        in_specs=(field, field, voxel, voxel, P()),
        out_specs=(field, field),
        check_vma=False,
    )
```

```python
import functools

import jax
import jax.numpy as jnp
from jax import lax
from jax.experimental import pallas as pl
from jax.experimental.pallas import tpu as pltpu
from jax.sharding import PartitionSpec as P

SEGS = 16
MESH = pl.DeviceIdType.MESH
f32 = jnp.float32

theta_value = 1.025
delta_value = 0.975
sigma_value = theta_value / delta_value
rho_first = 1.0 / sigma_value
rho_second = 1.0 / (2.0 * sigma_value - rho_first)

W = 16
RING = W + 8
VALUES = 11
EARLY = 8
SIGNS = (-1.0, -1.0, 1.0) * 2 + (1.0, 1.0) + (-1.0, -1.0, 1.0)


def routes(gx, gy):
    nx, ny = lax.axis_size("gx"), lax.axis_size("gy")
    first, last = gx == 0, gx == nx - 1
    xl = jnp.where(first, 0, gx - 1)
    xh = jnp.where(last, nx - 1, gx + 1)
    down, up = lax.rem(gy + ny - 1, ny), lax.rem(gy + 1, ny)
    mid = ny - 1 - gy
    mid_down, mid_up = lax.rem(mid + ny - 1, ny), lax.rem(mid + 1, ny)
    pick = jnp.where
    return [
        ((gx, down), 1),
        ((gx, up), 0),
        ((xl, pick(first, mid, gy)), pick(first, 2, 3)),
        ((xh, pick(last, mid, gy)), pick(last, 3, 2)),
        ((xl, pick(first, mid_up, down)), (7, 4)),
        ((xl, pick(first, mid_down, up)), (6, 5)),
        ((xh, pick(last, mid_up, down)), (5, 6)),
        ((xh, pick(last, mid_down, up)), (4, 7)),
    ]


def sym_apply(c, u):
    return (
        c[0] * u[0] + c[3] * u[1] + c[4] * u[2],
        c[3] * u[0] + c[1] * u[1] + c[5] * u[2],
        c[4] * u[0] + c[5] * u[1] + c[2] * u[2],
    )


def along_row(h):
    n = h.shape[0]
    return (h + h) + (pltpu.roll(h, 1, 0) + pltpu.roll(h, n - 1, 0))


def along_depth(h, repeat=False):
    lane = lax.broadcasted_iota(jnp.int32, h.shape, 1)
    end = h if repeat else jnp.zeros_like(h)
    below = jnp.where(lane == 0, end, pltpu.roll(h, 1, 1))
    above = jnp.where(lane == 127, end, pltpu.roll(h, 127, 1))
    return (h + h) + (below + above)


def weigh(h, repeat=False):
    return along_depth(along_row(h), repeat)


def line(x):
    return pl.ds(W * x, W) if isinstance(x, int) else pl.ds(pl.multiple_of(W * x, W), W)


def kernel(
    load, guess, labels, segments, stiffness, u_own, r_own, d_own, inv_own,
    blocks, table, l_own, k_own, lab, seg, c_own, v_own, cs_own, snd, rcv, t2g, t2o, c_strip,
    local_sem, send_sem, late_send_sem, recv_sem, late_recv_sem,
):
    gx, gy = lax.axis_index("gx"), lax.axis_index("gy")
    first, last = gx == 0, gx == lax.axis_size("gx") - 1
    fetch = [
        pltpu.make_async_copy(labels, lab, local_sem.at[0]),
        pltpu.make_async_copy(segments, seg, local_sem.at[1]),
        pltpu.make_async_copy(guess, u_own, local_sem.at[2]),
        pltpu.make_async_copy(load, l_own, local_sem.at[3]),
        pltpu.make_async_copy(stiffness, blocks, local_sem.at[4]),
    ]
    for copy in fetch:
        copy.start()
    t2g[...] = jnp.zeros(t2g.shape, f32)

    to = routes(gx, gy)
    here = [None] * 4 + [jnp.logical_and(d[0] == gx, d[1] == gy) for d, _ in to[4:]]
    barrier = pltpu.get_barrier_semaphore()
    expected = 4
    for (device, _), same in zip(to, here):
        if same is None:
            pl.semaphore_signal(barrier, inc=1, device_id=device, device_id_type=MESH)
        else:

            @pl.when(jnp.logical_not(same))
            def _():
                pl.semaphore_signal(barrier, inc=1, device_id=device, device_id_type=MESH)

            expected = expected + jnp.where(same, 0, 1)

    t2o[...] = jnp.zeros(t2o.shape, f32)
    fetch[0].wait()
    fetch[1].wait()
    k_own[...] = (lab[...] * SEGS + seg[...]).astype(f32)
    fetch[2].wait()
    fetch[3].wait()
    sides = ((0, 1), (W - 1, W - 2))
    for s in range(4):
        for j in range(2):
            at = sides[s % 2][j]
            rows = pl.ds(at, W, stride=W) if s < 2 else line(at)
            for c in range(3):
                snd[s, 3 * j + c] = u_own[c, rows]
                if j == 0:
                    snd[s, EARLY + c] = l_own[c, rows]
            snd[s, 6 + j] = k_own[rows]
    fetch[4].wait()
    table[0:6, 0 : stiffness.shape[1]] = blocks[...]

    pl.semaphore_wait(barrier, expected)

    early, late = pl.ds(0, EARLY), pl.ds(EARLY, VALUES - EARLY)
    parts = ((early, send_sem, recv_sem), (late, late_send_sem, late_recv_sem))

    def edge(n, device, slot):
        return [
            pltpu.make_async_remote_copy(
                src_ref=snd.at[n, values],
                dst_ref=rcv.at[slot, values],
                send_sem=out_sem.at[n],
                recv_sem=in_sem.at[slot],
                device_id=device,
                device_id_type=MESH,
            )
            for values, out_sem, in_sem in parts
        ]

    def corner_ref(side, end):
        return t2g.at[side, :, pl.ds(0 if end else 6, 2)]

    def send_x(n):
        for copy in edge(n, *to[n]):
            copy.start()

    def send_y(side):
        for copy in edge(side, (gx, jnp.where(side == 0, to[0][0][1], to[1][0][1])), 1 - side):
            copy.start()

    def send_corners(side):
        for end in range(2):
            low, high = to[4 + 2 * end][0], to[5 + 2 * end][0]
            device = (low[0], jnp.where(side == 0, low[1], high[1]))
            same = jnp.where(side == 0, here[4 + 2 * end], here[5 + 2 * end])
            mirrored = (first, last)[end]
            n = 4 + 2 * end + side
            source = snd.at[side, :, pl.ds(end * (W - 2), 2)]

            def remote(target, slot):
                return pltpu.make_async_remote_copy(
                    src_ref=source,
                    dst_ref=target,
                    send_sem=send_sem.at[n],
                    recv_sem=recv_sem.at[slot],
                    device_id=device,
                    device_id_type=MESH,
                )

            ahead = remote(corner_ref(1 - side, 1 - end), 4 + 2 * (1 - end) + (1 - side))
            back = remote(corner_ref(side, end), n)
            local = pltpu.make_async_copy(source, corner_ref(side, end), recv_sem.at[n])
            pl.when(jnp.logical_not(mirrored))(ahead.start)
            pl.when(jnp.logical_and(mirrored, jnp.logical_not(same)))(back.start)
            pl.when(same)(local.start)

    group = lax.rem(gy, 4)
    odd = lax.rem(lax.div(gx, 2), 2)
    hasty = jnp.where(group == 0, odd, jnp.where(group == 3, 1, 0))
    mirrors = ((2, first), (3, last))

    @pl.when(group == 0)
    def _():
        for n, mirrored in mirrors:
            pl.when(jnp.logical_not(mirrored))(lambda: send_x(n))

    send_corners(hasty)
    send_corners(1 - hasty)

    @pl.when(group == 3)
    def _():
        for n, mirrored in mirrors:
            pl.when(mirrored)(lambda: send_x(n))
    send_y(hasty)

    @pl.when(group == 2)
    def _():
        for n, mirrored in mirrors:
            pl.when(mirrored)(lambda: send_x(n))

    @pl.when(group != 0)
    def _():
        for n, mirrored in mirrors:
            pl.when(jnp.logical_not(mirrored))(lambda: send_x(n))

    send_y(1 - hasty)

    @pl.when(group < 2)
    def _():
        for n, mirrored in mirrors:
            pl.when(mirrored)(lambda: send_x(n))

    def receive(ref, sem):
        pltpu.make_async_copy(ref, ref, sem).wait()

    def lookup(codes, entry):
        rows = jnp.broadcast_to(table[entry : entry + 1, :], codes.shape)
        return jnp.take_along_axis(rows, codes, axis=1, mode="promise_in_bounds")

    inner_row = lax.broadcasted_iota(jnp.int32, (W, 128), 0)
    inner_row = jnp.logical_and(inner_row > 0, inner_row < W - 1)
    none = jnp.zeros((W, 128), f32)
    for x in (0, W - 1):
        for c in range(3):
            d_own[c, line(x)] = none
        for e in range(6):
            cs_own[e, line(x)] = none

    @pl.loop(0, W, unroll=4)
    def _(x):
        codes = k_own[line(x)].astype(jnp.int32)
        c = [lookup(codes, e) for e in range(6)]
        for e in range(6):
            c_own[e, line(x)] = c[e]
        v = sym_apply(c, [u_own[k, line(x)] for k in range(3)])
        for k in range(3):
            v_own[k, line(x)] = v[k]

    for s in range(4):
        for j in range(2):
            codes = snd[s, 6 + j].astype(jnp.int32)
            for e in range(6):
                c_strip[s, 2 + j, e, 0:W] = lookup(codes, e)

    def three(ref, e, x):
        return (ref[e, line(x - 1)] + ref[e, line(x + 1)]) + 2.0 * ref[e, line(x)]

    @pl.loop(1, W - 1, unroll=2)
    def _(x):
        c = [c_own[e, line(x)] for e in range(6)]
        u = [u_own[k, line(x)] for k in range(3)]
        c_sum = [weigh(three(c_own, e, x), True) for e in range(6)]
        u_sum = [weigh(three(u_own, k, x)) for k in range(3)]
        v_sum = [weigh(three(v_own, k, x)) for k in range(3)]
        near = sym_apply(c, [64.0 * u[k] - u_sum[k] for k in range(3)])
        far = sym_apply(c_sum, u)
        for k in range(3):
            r = l_own[k, line(x)] - 0.0625 * (near[k] + far[k] - v_sum[k])
            inverse = 16.0 / (48.0 * c[k] + c_sum[k])
            d = u[k] + (inverse * r) * (1.0 / theta_value)
            inv_own[k, line(x)] = inverse
            d_own[k, line(x)] = jnp.where(inner_row, d, 0.0)
        for e in range(6):
            cs_own[e, line(x)] = c_sum[e]

    @pl.loop(0, W, unroll=4)
    def _(x):
        v = sym_apply([c_own[e, line(x)] for e in range(6)], [d_own[k, line(x)] for k in range(3)])
        for k in range(3):
            v_own[k, line(x)] = v[k]

    def three_within(ref, e, x):
        below, above = jnp.maximum(x - 1, 0), jnp.minimum(x + 1, W - 1)
        return (ref[e, line(below)] + ref[e, line(above)]) + 2.0 * ref[e, line(x)]

    @pl.loop(0, W, unroll=2)
    def _(x):
        c = [c_own[e, line(x)] for e in range(6)]
        c_sum = [cs_own[e, line(x)] for e in range(6)]
        d = [d_own[k, line(x)] for k in range(3)]
        d_sum = [weigh(three_within(d_own, k, x)) for k in range(3)]
        v_sum = [weigh(three_within(v_own, k, x)) for k in range(3)]
        near = sym_apply(c, [64.0 * d[k] - d_sum[k] for k in range(3)])
        far = sym_apply(c_sum, d)
        for k in range(3):
            r_own[k, line(x)] = l_own[k, line(x)] - 0.0625 * (near[k] + far[k] - v_sum[k])

    turn = 7 - lax.broadcasted_iota(jnp.int32, (8, 128), 0)

    def turned(tile):
        return jnp.take_along_axis(tile, turn, axis=0, mode="promise_in_bounds")

    eight = lax.broadcasted_iota(jnp.int32, (8, 128), 0)
    low_sign = jnp.where(first, -1.0, 1.0)
    high_sign = jnp.where(last, -1.0, 1.0)
    end_sign = jnp.where(eight > 5, low_sign, jnp.where(eight < 2, high_sign, 1.0))

    def strip(s):
        ring = isinstance(s, int)
        n = RING if ring else W

        def value(row, index):
            own = row > 1
            if not ring:
                return (snd if own else rcv)[s, index]
            ends = t2o if own else t2g
            return jnp.concatenate([(snd if own else rcv)[s, index], ends[s, index]], axis=0)

        def layer(row):
            return (1, 0, 0, 1)[row]

        for row in range(4):
            codes = value(row, 6 + layer(row)).astype(jnp.int32)
            if row < 2:
                for e in range(6):
                    entry = lookup(codes[0:W], e)
                    if e > 3 and not ring:
                        entry = entry * jnp.where(s == 2, low_sign, high_sign)
                    c_strip[s, row, e, 0:W] = entry
            if ring:
                for e in range(6):
                    entry = lookup(codes[W:RING], e)
                    c_strip[s, row, e, W:RING] = entry * end_sign if e > 3 else entry
        c = [[c_strip[s, row, e, 0:n] for e in range(6)] for row in range(4)]
        u = [[value(row, 3 * layer(row) + k) for k in range(3)] for row in range(4)]
        v = [sym_apply(c[row], u[row]) for row in range(4)]

        def three_rows(f, row, k):
            return (f[row - 1][k] + f[row + 1][k]) + 2.0 * f[row][k]

        part, inverse, c_sum = {}, {}, {}
        for row in (1, 2):
            c_sum[row] = [weigh(three_rows(c, row, e), True) for e in range(6)]
            u_sum = [weigh(three_rows(u, row, k)) for k in range(3)]
            v_sum = [weigh(three_rows(v, row, k)) for k in range(3)]
            near = sym_apply(c[row], [64.0 * u[row][k] - u_sum[k] for k in range(3)])
            far = sym_apply(c_sum[row], u[row])
            part[row] = [0.0625 * (near[k] + far[k] - v_sum[k]) for k in range(3)]
            inverse[row] = [16.0 / (48.0 * c[row][k] + c_sum[row][k]) for k in range(3)]

        d = {}
        for row in (1, 2):
            d[row] = []
            for k in range(3):
                r = value(row, EARLY + k) - part[row][k]
                step = u[row][k] + (inverse[row][k] * r) * (1.0 / theta_value)
                d[row].append(step if ring else jnp.where(inner_row, step, 0.0))
        v = {row: sym_apply(c[row], d[row]) for row in (1, 2)}
        d_sum = [weigh(d[1][k] + 2.0 * d[2][k])[0:W] for k in range(3)]
        v_sum = [weigh(v[1][k] + 2.0 * v[2][k])[0:W] for k in range(3)]
        c2 = [t[0:W] for t in c[2]]
        c3 = [t[0:W] for t in c[3]]
        d2 = [t[0:W] for t in d[2]]
        near = sym_apply(c2, [64.0 * d2[k] - d_sum[k] for k in range(3)])
        far = sym_apply([t[0:W] for t in c_sum[2]], d2)
        outer = [near[k] + far[k] - v_sum[k] for k in range(3)]
        d_sum = [weigh(d[2][k])[0:W] for k in range(3)]
        v_sum = [weigh(v[2][k])[0:W] for k in range(3)]
        near = sym_apply(c3, d_sum)
        if ring:
            nearer, farther = sides[s]
            rows_0, rows_1 = pl.ds(nearer, W, stride=W), pl.ds(farther, W, stride=W)
        else:
            nearer = jnp.where(s == 2, 0, W - 1)
            rows_0, rows_1 = line(nearer), line(jnp.where(s == 2, 1, W - 2))
        for k in range(3):
            r_own[k, rows_0] = r_own[k, rows_0] - 0.0625 * outer[k]
            r_own[k, rows_1] = r_own[k, rows_1] + 0.0625 * (near[k] + v_sum[k])
            d_own[k, rows_0] = d2[k]
            inv_own[k, rows_0] = inverse[2][k][0:W]

    def turn_strip(s):
        @pl.when(jnp.logical_or(first, last))
        def _():
            for i in range(VALUES):
                head, tail = rcv[s, i, 0:8], rcv[s, i, 8:W]
                rcv[s, i, 0:8] = SIGNS[i] * turned(tail)
                rcv[s, i, 8:W] = SIGNS[i] * turned(head)

    def receive_edge(s):
        receive(rcv.at[s, early], recv_sem.at[s])
        receive(rcv.at[s, late], late_recv_sem.at[s])

    side_a = jnp.where(first, 3, 2)
    side_b = 5 - side_a
    receive_edge(side_a)
    strip(side_a)
    receive_edge(side_b)
    turn_strip(side_b)

    for s in range(2):
        for j in range(2):
            at = sides[s][j]
            for side, spot in ((2, (7, 6)), (3, (0, 1))):
                for i in range(2):
                    for c in range(3):
                        t2o[s, 3 * j + c, spot[i]] = rcv[side, 3 * i + c, at]
                    t2o[s, 6 + j, spot[i]] = rcv[side, 6 + i, at]
                if j == 0:
                    for c in range(3):
                        t2o[s, EARLY + c, spot[0]] = rcv[side, EARLY + c, at]

    def receive_y(s):
        receive_edge(s)
        for end in range(2):
            receive(corner_ref(s, end), recv_sem.at[4 + 2 * end + s])
        for mirrored, base in ((first, 6), (last, 0)):

            @pl.when(mirrored)
            def _():
                for i in range(VALUES):
                    one, two = t2g[s, i, base], t2g[s, i, base + 1]
                    t2g[s, i, base] = SIGNS[i] * two
                    t2g[s, i, base + 1] = SIGNS[i] * one

    receive_y(1)
    strip(side_b)
    strip(1)
    receive_y(0)
    strip(0)

    for n in range(4):
        for copy in edge(n, *to[n]):
            copy.wait_send()
    for n in range(4, 8):

        @pl.when(jnp.logical_not(here[n]))
        def _():
            source = snd.at[n % 2, :, pl.ds(0 if n < 6 else W - 2, 2)]
            pltpu.make_async_copy(source, source, send_sem.at[n]).wait()


def finish(u, r, d, inv, out_u, out_r, result, sem):
    copies = [pltpu.make_async_copy(r, out_r, sem.at[3])]
    copies[0].start()
    for k in range(3):
        copies.append(pltpu.make_async_copy(result.at[k], out_u.at[k], sem.at[k]))

        @pl.loop(0, W, unroll=8)
        def _(x):
            step = d[k, line(x)] - u[k, line(x)]
            step = (rho_second * rho_first) * step
            step += (2.0 * rho_second / delta_value) * (inv[k, line(x)] * r[k, line(x)])
            result[k, line(x)] = d[k, line(x)] + step

        copies[-1].start()
    for copy in copies:
        copy.wait()


def body(load, guess, labels, segments, stiffness):
    vmem = pl.BlockSpec(memory_space=pltpu.VMEM)
    hbm = pl.BlockSpec(memory_space=pltpu.HBM)
    shape = load.shape
    field = (3, W * W, 128)
    inputs = (
        load.reshape(field),
        guess.reshape(field),
        labels.reshape(field[1:]),
        segments.reshape(field[1:]),
        stiffness,
    )
    results = pl.pallas_call(
        kernel,
        out_shape=[pltpu.VMEM(field, f32)] * 4,
        in_specs=[hbm] * 5,
        out_specs=[vmem] * 4,
        scratch_shapes=[
            pltpu.VMEM(stiffness.shape, f32),
            pltpu.VMEM((8, 128), f32),
            pltpu.VMEM(field, f32),
            pltpu.VMEM(field[1:], f32),
            pltpu.VMEM(field[1:], jnp.int32),
            pltpu.VMEM(field[1:], jnp.int32),
            pltpu.VMEM((6,) + field[1:], f32),
            pltpu.VMEM(field, f32),
            pltpu.VMEM((6,) + field[1:], f32),
            pltpu.VMEM((4, VALUES, W, 128), f32),
            pltpu.VMEM((4, VALUES, W, 128), f32),
            pltpu.VMEM((2, VALUES, 8, 128), f32),
            pltpu.VMEM((2, VALUES, 8, 128), f32),
            pltpu.VMEM((4, 4, 6, RING, 128), f32),
            pltpu.SemaphoreType.DMA((5,)),
            pltpu.SemaphoreType.DMA((8,)),
            pltpu.SemaphoreType.DMA((4,)),
            pltpu.SemaphoreType.DMA((8,)),
            pltpu.SemaphoreType.DMA((4,)),
        ],
        compiler_params=pltpu.CompilerParams(
            collective_id=0, has_side_effects=True, vmem_limit_bytes=40 * 2**20
        ),
    )(*[pltpu.with_memory_space_constraint(x, pltpu.HBM) for x in inputs])
    out_u, out_r = pl.pallas_call(
        finish,
        out_shape=[jax.ShapeDtypeStruct(field, f32)] * 2,
        in_specs=[vmem] * 4,
        out_specs=[hbm] * 2,
        scratch_shapes=[pltpu.VMEM(field, f32), pltpu.SemaphoreType.DMA((4,))],
    )(*[pltpu.with_memory_space_constraint(x, pltpu.VMEM) for x in results])
    return out_u.reshape(shape), out_r.reshape(shape)


def solution(mesh):
    field = P(None, "gx", "gy", None)
    voxel = P("gx", "gy", None)
    return jax.shard_map(
        body,
        mesh=mesh,
        in_specs=(field, field, voxel, voxel, P()),
        out_specs=(field, field),
        check_vma=False,
    )
```

```python
import functools

import jax
import jax.numpy as jnp
from jax import lax
from jax.experimental import pallas as pl
from jax.experimental.pallas import tpu as pltpu
from jax.sharding import PartitionSpec as P

SEGS = 16
MESH = pl.DeviceIdType.MESH
f32 = jnp.float32

theta_value = 1.025
delta_value = 0.975
sigma_value = theta_value / delta_value
rho_first = 1.0 / sigma_value
rho_second = 1.0 / (2.0 * sigma_value - rho_first)

W = 16
RING = W + 8
CODES, ENDS, PART, LINES = 3 * W, 5 * W, 5 * W + 8, 8 * W + 8
VALUES = 11
VECTOR = (-1.0, -1.0, 1.0)
SIGNS = VECTOR * 2 + (1.0, 1.0) + VECTOR


def routes(gx, gy):
    nx, ny = lax.axis_size("gx"), lax.axis_size("gy")
    first, last = gx == 0, gx == nx - 1
    xl = jnp.where(first, 0, gx - 1)
    xh = jnp.where(last, nx - 1, gx + 1)
    down, up = lax.rem(gy + ny - 1, ny), lax.rem(gy + 1, ny)
    mid = ny - 1 - gy
    mid_down, mid_up = lax.rem(mid + ny - 1, ny), lax.rem(mid + 1, ny)
    pick = jnp.where
    return [
        ((gx, down), 1),
        ((gx, up), 0),
        ((xl, pick(first, mid, gy)), pick(first, 2, 3)),
        ((xh, pick(last, mid, gy)), pick(last, 3, 2)),
        ((xl, pick(first, mid_up, down)), (7, 4)),
        ((xl, pick(first, mid_down, up)), (6, 5)),
        ((xh, pick(last, mid_up, down)), (5, 6)),
        ((xh, pick(last, mid_down, up)), (4, 7)),
    ]


def sym_apply(c, u):
    return (
        c[0] * u[0] + c[3] * u[1] + c[4] * u[2],
        c[3] * u[0] + c[1] * u[1] + c[5] * u[2],
        c[4] * u[0] + c[5] * u[1] + c[2] * u[2],
    )


def along_row(h):
    n = h.shape[0]
    return (h + h) + (pltpu.roll(h, 1, 0) + pltpu.roll(h, n - 1, 0))


def along_depth(h, repeat=False):
    lane = lax.broadcasted_iota(jnp.int32, h.shape, 1)
    end = h if repeat else jnp.zeros_like(h)
    below = jnp.where(lane == 0, end, pltpu.roll(h, 1, 1))
    above = jnp.where(lane == 127, end, pltpu.roll(h, 127, 1))
    return (h + h) + (below + above)


def along_open_row(h):
    place = lax.broadcasted_iota(jnp.int32, h.shape, 0)
    n = h.shape[0]
    below = jnp.where(place == 0, 0.0, pltpu.roll(h, 1, 0))
    above = jnp.where(place == n - 1, 0.0, pltpu.roll(h, n - 1, 0))
    return (h + h) + (below + above)


def weigh(h, repeat=False):
    return along_depth(along_row(h), repeat)


def line(x):
    return pl.ds(W * x, W) if isinstance(x, int) else pl.ds(pl.multiple_of(W * x, W), W)


def kernel(
    load, guess, labels, segments, stiffness, u_own, r_own, d_own, inv_own,
    blocks, table, l_own, k_own, lab, seg, c_own, v_own, cs_own, snd, csnd, rcv, t2g, t2o, c_strip,
    local_sem, send_sem, late_send_sem, recv_sem, late_recv_sem,
):
    gx, gy = lax.axis_index("gx"), lax.axis_index("gy")
    first, last = gx == 0, gx == lax.axis_size("gx") - 1
    fetch = [
        pltpu.make_async_copy(labels, lab, local_sem.at[0]),
        pltpu.make_async_copy(segments, seg, local_sem.at[1]),
        pltpu.make_async_copy(guess, u_own, local_sem.at[2]),
        pltpu.make_async_copy(load, l_own, local_sem.at[3]),
        pltpu.make_async_copy(stiffness, blocks, local_sem.at[4]),
    ]
    for copy in fetch:
        copy.start()
    t2g[...] = jnp.zeros(t2g.shape, f32)

    to = routes(gx, gy)
    here = [None] * 4 + [jnp.logical_and(d[0] == gx, d[1] == gy) for d, _ in to[4:]]
    barrier = pltpu.get_barrier_semaphore()
    expected = 4
    for (device, _), same in zip(to, here):
        if same is None:
            pl.semaphore_signal(barrier, inc=1, device_id=device, device_id_type=MESH)
        else:

            @pl.when(jnp.logical_not(same))
            def _():
                pl.semaphore_signal(barrier, inc=1, device_id=device, device_id_type=MESH)

            expected = expected + jnp.where(same, 0, 1)

    t2o[...] = jnp.zeros(t2o.shape, f32)
    fetch[0].wait()
    fetch[1].wait()
    k_own[...] = (lab[...] * SEGS + seg[...]).astype(f32)
    fetch[2].wait()
    fetch[3].wait()
    sides = ((0, 1), (W - 1, W - 2))

    def own_rows(s, j):
        if isinstance(s, int):
            return pl.ds(sides[s % 2][j], W, stride=W) if s < 2 else line(sides[s % 2][j])
        return line(jnp.where(s == 2, sides[0][j], sides[1][j]))

    for s in range(4):
        for c in range(3):
            snd[s, line(c)] = u_own[c, own_rows(s, 0)]
            for end in range(2):
                at = sides[s % 2][1]
                at = (W * (W - 1) * end + at) if s < 2 else (W * at + (W - 1) * end)
                snd[s, ENDS + 3 * end + c] = u_own[c, at]
        for j in range(2):
            snd[s, line(3 + j)] = k_own[own_rows(s, j)]
    for s in range(2):
        for end in range(2):
            for j in range(2):
                at = sides[s][j] + W * (W - 2) * end
                for i in range(2):
                    for c in range(3):
                        csnd[s, end, 3 * j + c, i] = u_own[c, at + W * i]
                        if j == 0:
                            csnd[s, end, 8 + c, i] = l_own[c, at + W * i]
                    csnd[s, end, 6 + j, i] = k_own[at + W * i]
    fetch[4].wait()
    table[0:6, 0 : stiffness.shape[1]] = blocks[...]

    def lookup(codes, entry):
        rows = jnp.broadcast_to(table[entry : entry + 1, :], codes.shape)
        return jnp.take_along_axis(rows, codes, axis=1, mode="promise_in_bounds")

    for s in range(4):
        c, u = [], []
        for j in range(2):
            codes = snd[s, line(3 + j)].astype(jnp.int32)
            c.append([lookup(codes, e) for e in range(6)])
            u.append([u_own[k, own_rows(s, j)] for k in range(3)])
            for e in range(6):
                c_strip[s, 2 + j, e, 0:W] = c[j][e]
        v = [sym_apply(c[j], u[j]) for j in range(2)]
        u_sum = [along_depth(along_open_row(2.0 * u[0][k] + u[1][k])) for k in range(3)]
        v_sum = [along_depth(along_open_row(2.0 * v[0][k] + v[1][k])) for k in range(3)]
        near = sym_apply(c[0], [64.0 * u[0][k] - u_sum[k] for k in range(3)])
        for k in range(3):
            part = l_own[k, own_rows(s, 0)] - 0.0625 * (near[k] - v_sum[k])
            snd[s, pl.ds(PART + W * k, W)] = part

    pl.semaphore_wait(barrier, expected)

    early, late = pl.ds(0, PART), pl.ds(PART, LINES - PART)
    parts = ((early, send_sem, recv_sem), (late, late_send_sem, late_recv_sem))

    def edge(n, device, slot):
        return [
            pltpu.make_async_remote_copy(
                src_ref=snd.at[n, values],
                dst_ref=rcv.at[slot, values],
                send_sem=out_sem.at[n],
                recv_sem=in_sem.at[slot],
                device_id=device,
                device_id_type=MESH,
            )
            for values, out_sem, in_sem in parts
        ]

    def corner_ref(side, end):
        return t2g.at[side, :, pl.ds(0 if end else 6, 2)]

    def send_x(n):
        for copy in edge(n, *to[n]):
            copy.start()

    def send_y(side):
        for copy in edge(side, (gx, jnp.where(side == 0, to[0][0][1], to[1][0][1])), 1 - side):
            copy.start()

    def send_corners(side):
        for end in range(2):
            low, high = to[4 + 2 * end][0], to[5 + 2 * end][0]
            device = (low[0], jnp.where(side == 0, low[1], high[1]))
            same = jnp.where(side == 0, here[4 + 2 * end], here[5 + 2 * end])
            mirrored = (first, last)[end]
            n = 4 + 2 * end + side
            source = csnd.at[side, end]

            def remote(target, slot):
                return pltpu.make_async_remote_copy(
                    src_ref=source,
                    dst_ref=target,
                    send_sem=send_sem.at[n],
                    recv_sem=recv_sem.at[slot],
                    device_id=device,
                    device_id_type=MESH,
                )

            ahead = remote(corner_ref(1 - side, 1 - end), 4 + 2 * (1 - end) + (1 - side))
            back = remote(corner_ref(side, end), n)
            local = pltpu.make_async_copy(source, corner_ref(side, end), recv_sem.at[n])
            pl.when(jnp.logical_not(mirrored))(ahead.start)
            pl.when(jnp.logical_and(mirrored, jnp.logical_not(same)))(back.start)
            pl.when(same)(local.start)

    group = lax.rem(gy, 4)
    odd = lax.rem(lax.div(gx, 2), 2)
    hasty = jnp.where(group == 0, odd, jnp.where(group == 3, 1, 0))
    mirrors = ((2, first), (3, last))

    @pl.when(group == 0)
    def _():
        for n, mirrored in mirrors:
            pl.when(jnp.logical_not(mirrored))(lambda: send_x(n))

    send_corners(hasty)
    send_corners(1 - hasty)

    @pl.when(group == 3)
    def _():
        for n, mirrored in mirrors:
            pl.when(mirrored)(lambda: send_x(n))
    send_y(hasty)

    @pl.when(group == 2)
    def _():
        for n, mirrored in mirrors:
            pl.when(mirrored)(lambda: send_x(n))

    @pl.when(group != 0)
    def _():
        for n, mirrored in mirrors:
            pl.when(jnp.logical_not(mirrored))(lambda: send_x(n))

    send_y(1 - hasty)

    @pl.when(group < 2)
    def _():
        for n, mirrored in mirrors:
            pl.when(mirrored)(lambda: send_x(n))

    def receive(ref, sem):
        pltpu.make_async_copy(ref, ref, sem).wait()

    inner_row = lax.broadcasted_iota(jnp.int32, (W, 128), 0)
    inner_row = jnp.logical_and(inner_row > 0, inner_row < W - 1)
    none = jnp.zeros((W, 128), f32)
    for x in (0, W - 1):
        for c in range(3):
            d_own[c, line(x)] = none
        for e in range(6):
            cs_own[e, line(x)] = none

    @pl.loop(0, W, unroll=4)
    def _(x):
        codes = k_own[line(x)].astype(jnp.int32)
        c = [lookup(codes, e) for e in range(6)]
        for e in range(6):
            c_own[e, line(x)] = c[e]
        v = sym_apply(c, [u_own[k, line(x)] for k in range(3)])
        for k in range(3):
            v_own[k, line(x)] = v[k]

    def three(ref, e, x):
        return (ref[e, line(x - 1)] + ref[e, line(x + 1)]) + 2.0 * ref[e, line(x)]

    @pl.loop(1, W - 1, unroll=2)
    def _(x):
        c = [c_own[e, line(x)] for e in range(6)]
        u = [u_own[k, line(x)] for k in range(3)]
        c_sum = [weigh(three(c_own, e, x), True) for e in range(6)]
        u_sum = [weigh(three(u_own, k, x)) for k in range(3)]
        v_sum = [weigh(three(v_own, k, x)) for k in range(3)]
        near = sym_apply(c, [64.0 * u[k] - u_sum[k] for k in range(3)])
        far = sym_apply(c_sum, u)
        for k in range(3):
            r = l_own[k, line(x)] - 0.0625 * (near[k] + far[k] - v_sum[k])
            inverse = 16.0 / (48.0 * c[k] + c_sum[k])
            d = u[k] + (inverse * r) * (1.0 / theta_value)
            inv_own[k, line(x)] = inverse
            d_own[k, line(x)] = jnp.where(inner_row, d, 0.0)
        for e in range(6):
            cs_own[e, line(x)] = c_sum[e]

    @pl.loop(0, W, unroll=4)
    def _(x):
        v = sym_apply([c_own[e, line(x)] for e in range(6)], [d_own[k, line(x)] for k in range(3)])
        for k in range(3):
            v_own[k, line(x)] = v[k]

    def three_within(ref, e, x):
        below, above = jnp.maximum(x - 1, 0), jnp.minimum(x + 1, W - 1)
        return (ref[e, line(below)] + ref[e, line(above)]) + 2.0 * ref[e, line(x)]

    @pl.loop(0, W, unroll=2)
    def _(x):
        c = [c_own[e, line(x)] for e in range(6)]
        c_sum = [cs_own[e, line(x)] for e in range(6)]
        d = [d_own[k, line(x)] for k in range(3)]
        d_sum = [weigh(three_within(d_own, k, x)) for k in range(3)]
        v_sum = [weigh(three_within(v_own, k, x)) for k in range(3)]
        near = sym_apply(c, [64.0 * d[k] - d_sum[k] for k in range(3)])
        far = sym_apply(c_sum, d)
        for k in range(3):
            r_own[k, line(x)] = l_own[k, line(x)] - 0.0625 * (near[k] + far[k] - v_sum[k])

    turn = 7 - lax.broadcasted_iota(jnp.int32, (8, 128), 0)

    def turned(tile):
        return jnp.take_along_axis(tile, turn, axis=0, mode="promise_in_bounds")

    eight = lax.broadcasted_iota(jnp.int32, (8, 128), 0)
    low_sign = jnp.where(first, -1.0, 1.0)
    high_sign = jnp.where(last, -1.0, 1.0)
    end_sign = jnp.where(eight > 5, low_sign, jnp.where(eight < 2, high_sign, 1.0))

    def strip(s):
        ring = isinstance(s, int)
        n = RING if ring else W

        def ringed(row, index, middle):
            return jnp.concatenate([middle, (t2g if row < 2 else t2o)[s, index]], axis=0)

        place = lax.broadcasted_iota(jnp.int32, (W, 128), 0)
        c, u = [], []
        for row in range(4):
            layer = (1, 0, 0, 1)[row]
            codes = (rcv if row < 2 else snd)[s, line(3 + layer)].astype(jnp.int32)
            if row < 2:
                for e in range(6):
                    entry = lookup(codes, e)
                    if e > 3 and not ring:
                        entry = entry * jnp.where(s == 2, low_sign, high_sign)
                    c_strip[s, row, e, 0:W] = entry
            if ring:
                codes = (t2g if row < 2 else t2o)[s, 6 + layer].astype(jnp.int32)
                for e in range(6):
                    entry = lookup(codes, e)
                    c_strip[s, row, e, W:RING] = entry * end_sign if e > 3 else entry
            c.append([c_strip[s, row, e, 0:n] for e in range(6)])
            u.append([])
            for k in range(3):
                if row == 0:
                    low_end = jnp.broadcast_to(rcv[s, pl.ds(ENDS + k, 1)], (W, 128))
                    high_end = jnp.broadcast_to(rcv[s, pl.ds(ENDS + 3 + k, 1)], (W, 128))
                    middle = jnp.where(place == 0, low_end, 0.0)
                    middle = jnp.where(place == W - 1, high_end, middle)
                elif row == 1:
                    middle = rcv[s, line(k)]
                else:
                    middle = u_own[k, own_rows(s, layer)]
                u[row].append(ringed(row, 3 * layer + k, middle) if ring else middle)
        v = [sym_apply(c[row], u[row]) if ring or row > 0 else None for row in range(4)]

        def three_rows(f, row, k):
            return (f[row - 1][k] + f[row + 1][k]) + 2.0 * f[row][k]

        def sums(f, row, k):
            if not ring:
                return weigh(f[2][k] if row == 1 else three_rows(f, row, k))
            whole = three_rows(f, row, k)
            rest = jnp.concatenate(
                [f[2][k][0:W], whole[W:RING]] if row == 1 else [whole[0:W], f[1][k][W:RING]],
                axis=0,
            )
            middle, ends = (rest, whole) if row == 1 else (whole, rest)
            h = jnp.concatenate([along_row(middle)[0:W], along_row(ends)[W:RING]], axis=0)
            return along_depth(h)

        tail = (lax.broadcasted_iota(jnp.int32, (n, 128), 0) >= W) if ring else None
        raw = {1: jnp.where(tail, 64.0, 0.0) if ring else 0.0, 2: jnp.where(tail, 0.0, 64.0) if ring else 64.0}
        part, inverse, c_sum = {}, {}, {}
        for row in (1, 2):
            c_sum[row] = [weigh(three_rows(c, row, e), True) for e in range(6)]
            u_sum = [sums(u, row, k) for k in range(3)]
            v_sum = [sums(v, row, k) for k in range(3)]
            near = sym_apply(c[row], [raw[row] * u[row][k] - u_sum[k] for k in range(3)])
            far = sym_apply(c_sum[row], u[row])
            part[row] = [0.0625 * (near[k] + far[k] - v_sum[k]) for k in range(3)]
            inverse[row] = [16.0 / (48.0 * c[row][k] + c_sum[row][k]) for k in range(3)]

        def start_of(row, k):
            if row == 1:
                middle = rcv[s, pl.ds(PART + W * k, W)]
            else:
                middle = l_own[k, own_rows(s, 0)]
            return ringed(row, 8 + k, middle) if ring else middle

        d = {}
        for row in (1, 2):
            d[row] = []
            for k in range(3):
                r = start_of(row, k) - part[row][k]
                step = u[row][k] + (inverse[row][k] * r) * (1.0 / theta_value)
                d[row].append(step if ring else jnp.where(inner_row, step, 0.0))
        v = {row: sym_apply(c[row], d[row]) for row in (1, 2)}
        d_sum = [weigh(d[1][k] + 2.0 * d[2][k])[0:W] for k in range(3)]
        v_sum = [weigh(v[1][k] + 2.0 * v[2][k])[0:W] for k in range(3)]
        c2 = [t[0:W] for t in c[2]]
        c3 = [t[0:W] for t in c[3]]
        d2 = [t[0:W] for t in d[2]]
        near = sym_apply(c2, [64.0 * d2[k] - d_sum[k] for k in range(3)])
        far = sym_apply([t[0:W] for t in c_sum[2]], d2)
        outer = [near[k] + far[k] - v_sum[k] for k in range(3)]
        d_sum = [weigh(d[2][k])[0:W] for k in range(3)]
        v_sum = [weigh(v[2][k])[0:W] for k in range(3)]
        near = sym_apply(c3, d_sum)
        if ring:
            nearer, farther = sides[s]
            rows_0, rows_1 = pl.ds(nearer, W, stride=W), pl.ds(farther, W, stride=W)
        else:
            nearer = jnp.where(s == 2, 0, W - 1)
            rows_0, rows_1 = line(nearer), line(jnp.where(s == 2, 1, W - 2))
        for k in range(3):
            r_own[k, rows_0] = r_own[k, rows_0] - 0.0625 * outer[k]
            r_own[k, rows_1] = r_own[k, rows_1] + 0.0625 * (near[k] + v_sum[k])
            d_own[k, rows_0] = d2[k]
            inv_own[k, rows_0] = inverse[2][k][0:W]

    def turn_strip(s):
        @pl.when(jnp.logical_or(first, last))
        def _():
            lines = [W * i for i in range(5)] + [PART + W * k for k in range(3)]
            for at, sign in zip(lines, VECTOR + (1.0, 1.0) + VECTOR):
                head, tail = rcv[s, at : at + 8], rcv[s, at + 8 : at + W]
                rcv[s, at : at + 8] = sign * turned(tail)
                rcv[s, at + 8 : at + W] = sign * turned(head)
            for k in range(3):
                one, two = rcv[s, ENDS + k], rcv[s, ENDS + 3 + k]
                rcv[s, ENDS + k] = VECTOR[k] * two
                rcv[s, ENDS + 3 + k] = VECTOR[k] * one

    def receive_edge(s):
        receive(rcv.at[s, early], recv_sem.at[s])
        receive(rcv.at[s, late], late_recv_sem.at[s])

    side_a = jnp.where(first, 3, 2)
    side_b = 5 - side_a
    receive_edge(side_a)
    strip(side_a)
    receive_edge(side_b)
    turn_strip(side_b)

    for s in range(2):
        for j in range(2):
            at = sides[s][j]
            for side, spot in ((2, (7, 6)), (3, (0, 1))):
                for c in range(3):
                    t2o[s, 3 * j + c, spot[0]] = rcv[side, W * c + at]
                    if j == 0:
                        t2o[s, c, spot[1]] = rcv[side, ENDS + 3 * s + c]
                        t2o[s, 8 + c, spot[0]] = rcv[side, PART + W * c + at]
                for i in range(2):
                    t2o[s, 6 + j, spot[i]] = rcv[side, CODES + W * i + at]

    def receive_y(s):
        receive_edge(s)
        for end in range(2):
            receive(corner_ref(s, end), recv_sem.at[4 + 2 * end + s])
        for mirrored, base in ((first, 6), (last, 0)):

            @pl.when(mirrored)
            def _():
                for i in range(VALUES):
                    one, two = t2g[s, i, base], t2g[s, i, base + 1]
                    t2g[s, i, base] = SIGNS[i] * two
                    t2g[s, i, base + 1] = SIGNS[i] * one

    receive_y(1)
    strip(side_b)
    strip(1)
    receive_y(0)
    strip(0)

    for n in range(4):
        for copy in edge(n, *to[n]):
            copy.wait_send()
    for n in range(4, 8):

        @pl.when(jnp.logical_not(here[n]))
        def _():
            source = csnd.at[n % 2, n // 6]
            pltpu.make_async_copy(source, source, send_sem.at[n]).wait()


def finish(u, r, d, inv, out_u, out_r, result, sem):
    copies = [pltpu.make_async_copy(r, out_r, sem.at[3])]
    copies[0].start()
    for k in range(3):
        copies.append(pltpu.make_async_copy(result.at[k], out_u.at[k], sem.at[k]))

        @pl.loop(0, W, unroll=8)
        def _(x):
            step = d[k, line(x)] - u[k, line(x)]
            step = (rho_second * rho_first) * step
            step += (2.0 * rho_second / delta_value) * (inv[k, line(x)] * r[k, line(x)])
            result[k, line(x)] = d[k, line(x)] + step

        copies[-1].start()
    for copy in copies:
        copy.wait()


def body(load, guess, labels, segments, stiffness):
    vmem = pl.BlockSpec(memory_space=pltpu.VMEM)
    hbm = pl.BlockSpec(memory_space=pltpu.HBM)
    shape = load.shape
    field = (3, W * W, 128)
    inputs = (
        load.reshape(field),
        guess.reshape(field),
        labels.reshape(field[1:]),
        segments.reshape(field[1:]),
        stiffness,
    )
    results = pl.pallas_call(
        kernel,
        out_shape=[pltpu.VMEM(field, f32)] * 4,
        in_specs=[hbm] * 5,
        out_specs=[vmem] * 4,
        scratch_shapes=[
            pltpu.VMEM(stiffness.shape, f32),
            pltpu.VMEM((8, 128), f32),
            pltpu.VMEM(field, f32),
            pltpu.VMEM(field[1:], f32),
            pltpu.VMEM(field[1:], jnp.int32),
            pltpu.VMEM(field[1:], jnp.int32),
            pltpu.VMEM((6,) + field[1:], f32),
            pltpu.VMEM(field, f32),
            pltpu.VMEM((6,) + field[1:], f32),
            pltpu.VMEM((4, LINES, 128), f32),
            pltpu.VMEM((2, 2, VALUES, 2, 128), f32),
            pltpu.VMEM((4, LINES, 128), f32),
            pltpu.VMEM((2, VALUES, 8, 128), f32),
            pltpu.VMEM((2, VALUES, 8, 128), f32),
            pltpu.VMEM((4, 4, 6, RING, 128), f32),
            pltpu.SemaphoreType.DMA((5,)),
            pltpu.SemaphoreType.DMA((8,)),
            pltpu.SemaphoreType.DMA((4,)),
            pltpu.SemaphoreType.DMA((8,)),
            pltpu.SemaphoreType.DMA((4,)),
        ],
        compiler_params=pltpu.CompilerParams(
            collective_id=0, has_side_effects=True, vmem_limit_bytes=40 * 2**20
        ),
    )(*[pltpu.with_memory_space_constraint(x, pltpu.HBM) for x in inputs])
    out_u, out_r = pl.pallas_call(
        finish,
        out_shape=[jax.ShapeDtypeStruct(field, f32)] * 2,
        in_specs=[vmem] * 4,
        out_specs=[hbm] * 2,
        scratch_shapes=[pltpu.VMEM(field, f32), pltpu.SemaphoreType.DMA((4,))],
    )(*[pltpu.with_memory_space_constraint(x, pltpu.VMEM) for x in results])
    return out_u.reshape(shape), out_r.reshape(shape)


def solution(mesh):
    field = P(None, "gx", "gy", None)
    voxel = P("gx", "gy", None)
    return jax.shard_map(
        body,
        mesh=mesh,
        in_specs=(field, field, voxel, voxel, P()),
        out_specs=(field, field),
        check_vma=False,
    )
```

```python
import functools

import jax
import jax.numpy as jnp
from jax import lax
from jax.experimental import pallas as pl
from jax.experimental.pallas import tpu as pltpu
from jax.sharding import PartitionSpec as P

SEGS = 16
MESH = pl.DeviceIdType.MESH
f32 = jnp.float32

theta_value = 1.025
delta_value = 0.975
sigma_value = theta_value / delta_value
rho_first = 1.0 / sigma_value
rho_second = 1.0 / (2.0 * sigma_value - rho_first)

W = 16
RING = W + 8
CODES, ENDS, PART, LINES = 3 * W, 5 * W, 5 * W + 8, 8 * W + 8
VALUES = 11
VECTOR = (-1.0, -1.0, 1.0)
SIGNS = VECTOR * 2 + (1.0, 1.0) + VECTOR


def routes(gx, gy):
    nx, ny = lax.axis_size("gx"), lax.axis_size("gy")
    first, last = gx == 0, gx == nx - 1
    xl = jnp.where(first, 0, gx - 1)
    xh = jnp.where(last, nx - 1, gx + 1)
    down, up = lax.rem(gy + ny - 1, ny), lax.rem(gy + 1, ny)
    mid = ny - 1 - gy
    mid_down, mid_up = lax.rem(mid + ny - 1, ny), lax.rem(mid + 1, ny)
    pick = jnp.where
    return [
        ((gx, down), 1),
        ((gx, up), 0),
        ((xl, pick(first, mid, gy)), pick(first, 2, 3)),
        ((xh, pick(last, mid, gy)), pick(last, 3, 2)),
        ((xl, pick(first, mid_up, down)), (7, 4)),
        ((xl, pick(first, mid_down, up)), (6, 5)),
        ((xh, pick(last, mid_up, down)), (5, 6)),
        ((xh, pick(last, mid_down, up)), (4, 7)),
    ]


def sym_apply(c, u):
    return (
        c[0] * u[0] + c[3] * u[1] + c[4] * u[2],
        c[3] * u[0] + c[1] * u[1] + c[5] * u[2],
        c[4] * u[0] + c[5] * u[1] + c[2] * u[2],
    )


def along_row(h):
    n = h.shape[0]
    return (h + h) + (pltpu.roll(h, 1, 0) + pltpu.roll(h, n - 1, 0))


def along_depth(h, repeat=False):
    lane = lax.broadcasted_iota(jnp.int32, h.shape, 1)
    end = h if repeat else jnp.zeros_like(h)
    below = jnp.where(lane == 0, end, pltpu.roll(h, 1, 1))
    above = jnp.where(lane == 127, end, pltpu.roll(h, 127, 1))
    return (h + h) + (below + above)


def along_open_row(h):
    place = lax.broadcasted_iota(jnp.int32, h.shape, 0)
    n = h.shape[0]
    below = jnp.where(place == 0, 0.0, pltpu.roll(h, 1, 0))
    above = jnp.where(place == n - 1, 0.0, pltpu.roll(h, n - 1, 0))
    return (h + h) + (below + above)


def weigh(h, repeat=False):
    return along_depth(along_row(h), repeat)


def line(x):
    return pl.ds(W * x, W) if isinstance(x, int) else pl.ds(pl.multiple_of(W * x, W), W)


def kernel(
    load, guess, labels, segments, stiffness, u_own, r_own, d_own, inv_own,
    blocks, table, l_own, k_own, lab, seg, c_own, v_own, cs_own, snd, csnd, rcv, t2g, t2o, c_strip,
    local_sem, send_sem, late_send_sem, recv_sem, late_recv_sem,
):
    gx, gy = lax.axis_index("gx"), lax.axis_index("gy")
    first, last = gx == 0, gx == lax.axis_size("gx") - 1
    fetch = [
        pltpu.make_async_copy(labels, lab, local_sem.at[0]),
        pltpu.make_async_copy(segments, seg, local_sem.at[1]),
        pltpu.make_async_copy(stiffness, blocks, local_sem.at[4]),
        pltpu.make_async_copy(guess, u_own, local_sem.at[2]),
        pltpu.make_async_copy(load, l_own, local_sem.at[3]),
    ]
    for copy in fetch:
        copy.start()
    t2g[...] = jnp.zeros(t2g.shape, f32)

    to = routes(gx, gy)
    here = [None] * 4 + [jnp.logical_and(d[0] == gx, d[1] == gy) for d, _ in to[4:]]
    barrier = pltpu.get_barrier_semaphore()
    expected = 4
    for (device, _), same in zip(to, here):
        if same is None:
            pl.semaphore_signal(barrier, inc=1, device_id=device, device_id_type=MESH)
        else:

            @pl.when(jnp.logical_not(same))
            def _():
                pl.semaphore_signal(barrier, inc=1, device_id=device, device_id_type=MESH)

            expected = expected + jnp.where(same, 0, 1)

    t2o[...] = jnp.zeros(t2o.shape, f32)
    fetch[0].wait()
    fetch[1].wait()
    k_own[...] = (lab[...] * SEGS + seg[...]).astype(f32)
    fetch[3].wait()
    fetch[4].wait()
    sides = ((0, 1), (W - 1, W - 2))

    def own_rows(s, j):
        if isinstance(s, int):
            return pl.ds(sides[s % 2][j], W, stride=W) if s < 2 else line(sides[s % 2][j])
        return line(jnp.where(s == 2, sides[0][j], sides[1][j]))

    for s in range(4):
        for c in range(3):
            snd[s, line(c)] = u_own[c, own_rows(s, 0)]
            for end in range(2):
                at = sides[s % 2][1]
                at = (W * (W - 1) * end + at) if s < 2 else (W * at + (W - 1) * end)
                snd[s, ENDS + 3 * end + c] = u_own[c, at]
        for j in range(2):
            snd[s, line(3 + j)] = k_own[own_rows(s, j)]
    for s in range(2):
        for end in range(2):
            for j in range(2):
                at = sides[s][j] + W * (W - 2) * end
                for i in range(2):
                    for c in range(3):
                        csnd[s, end, 3 * j + c, i] = u_own[c, at + W * i]
                        if j == 0:
                            csnd[s, end, 8 + c, i] = l_own[c, at + W * i]
                    csnd[s, end, 6 + j, i] = k_own[at + W * i]
    fetch[2].wait()
    table[0:6, 0 : stiffness.shape[1]] = blocks[...]

    def lookup(codes, entry):
        rows = jnp.broadcast_to(table[entry : entry + 1, :], codes.shape)
        return jnp.take_along_axis(rows, codes, axis=1, mode="promise_in_bounds")

    for s in range(4):
        c, u = [], []
        for j in range(2):
            codes = snd[s, line(3 + j)].astype(jnp.int32)
            c.append([lookup(codes, e) for e in range(6)])
            u.append([u_own[k, own_rows(s, j)] for k in range(3)])
            for e in range(6):
                c_strip[s, 2 + j, e, 0:W] = c[j][e]
        v = [sym_apply(c[j], u[j]) for j in range(2)]
        u_sum = [along_depth(along_open_row(2.0 * u[0][k] + u[1][k])) for k in range(3)]
        v_sum = [along_depth(along_open_row(2.0 * v[0][k] + v[1][k])) for k in range(3)]
        near = sym_apply(c[0], [64.0 * u[0][k] - u_sum[k] for k in range(3)])
        for k in range(3):
            part = l_own[k, own_rows(s, 0)] - 0.0625 * (near[k] - v_sum[k])
            snd[s, pl.ds(PART + W * k, W)] = part

    pl.semaphore_wait(barrier, expected)

    early, late = pl.ds(0, PART), pl.ds(PART, LINES - PART)
    parts = ((early, send_sem, recv_sem), (late, late_send_sem, late_recv_sem))

    def edge(n, device, slot):
        return [
            pltpu.make_async_remote_copy(
                src_ref=snd.at[n, values],
                dst_ref=rcv.at[slot, values],
                send_sem=out_sem.at[n],
                recv_sem=in_sem.at[slot],
                device_id=device,
                device_id_type=MESH,
            )
            for values, out_sem, in_sem in parts
        ]

    def corner_ref(side, end):
        return t2g.at[side, :, pl.ds(0 if end else 6, 2)]

    def send_x(n):
        for copy in edge(n, *to[n]):
            copy.start()

    def send_y(side):
        for copy in edge(side, (gx, jnp.where(side == 0, to[0][0][1], to[1][0][1])), 1 - side):
            copy.start()

    def send_corners(side):
        for end in range(2):
            low, high = to[4 + 2 * end][0], to[5 + 2 * end][0]
            device = (low[0], jnp.where(side == 0, low[1], high[1]))
            same = jnp.where(side == 0, here[4 + 2 * end], here[5 + 2 * end])
            mirrored = (first, last)[end]
            n = 4 + 2 * end + side
            source = csnd.at[side, end]

            def remote(target, slot):
                return pltpu.make_async_remote_copy(
                    src_ref=source,
                    dst_ref=target,
                    send_sem=send_sem.at[n],
                    recv_sem=recv_sem.at[slot],
                    device_id=device,
                    device_id_type=MESH,
                )

            ahead = remote(corner_ref(1 - side, 1 - end), 4 + 2 * (1 - end) + (1 - side))
            back = remote(corner_ref(side, end), n)
            local = pltpu.make_async_copy(source, corner_ref(side, end), recv_sem.at[n])
            pl.when(jnp.logical_not(mirrored))(ahead.start)
            pl.when(jnp.logical_and(mirrored, jnp.logical_not(same)))(back.start)
            pl.when(same)(local.start)

    group = lax.rem(gy, 4)
    odd = lax.rem(lax.div(gx, 2), 2)
    hasty = jnp.where(group == 0, odd, jnp.where(group == 3, 1, 0))
    mirrors = ((2, first), (3, last))

    @pl.when(group == 0)
    def _():
        for n, mirrored in mirrors:
            pl.when(jnp.logical_not(mirrored))(lambda: send_x(n))

    send_corners(hasty)
    send_corners(1 - hasty)

    @pl.when(group == 3)
    def _():
        for n, mirrored in mirrors:
            pl.when(mirrored)(lambda: send_x(n))
    send_y(hasty)

    @pl.when(group == 2)
    def _():
        for n, mirrored in mirrors:
            pl.when(mirrored)(lambda: send_x(n))

    @pl.when(group != 0)
    def _():
        for n, mirrored in mirrors:
            pl.when(jnp.logical_not(mirrored))(lambda: send_x(n))

    send_y(1 - hasty)

    @pl.when(group < 2)
    def _():
        for n, mirrored in mirrors:
            pl.when(mirrored)(lambda: send_x(n))

    def receive(ref, sem):
        pltpu.make_async_copy(ref, ref, sem).wait()

    inner_row = lax.broadcasted_iota(jnp.int32, (W, 128), 0)
    inner_row = jnp.logical_and(inner_row > 0, inner_row < W - 1)
    none = jnp.zeros((W, 128), f32)
    for x in (0, W - 1):
        for c in range(3):
            d_own[c, line(x)] = none
        for e in range(6):
            cs_own[e, line(x)] = none

    @pl.loop(0, W, unroll=4)
    def _(x):
        codes = k_own[line(x)].astype(jnp.int32)
        c = [lookup(codes, e) for e in range(6)]
        for e in range(6):
            c_own[e, line(x)] = c[e]
        v = sym_apply(c, [u_own[k, line(x)] for k in range(3)])
        for k in range(3):
            v_own[k, line(x)] = v[k]

    def three(ref, e, x):
        return (ref[e, line(x - 1)] + ref[e, line(x + 1)]) + 2.0 * ref[e, line(x)]

    @pl.loop(1, W - 1, unroll=2)
    def _(x):
        c = [c_own[e, line(x)] for e in range(6)]
        u = [u_own[k, line(x)] for k in range(3)]
        c_sum = [weigh(three(c_own, e, x), True) for e in range(6)]
        u_sum = [weigh(three(u_own, k, x)) for k in range(3)]
        v_sum = [weigh(three(v_own, k, x)) for k in range(3)]
        near = sym_apply(c, [64.0 * u[k] - u_sum[k] for k in range(3)])
        far = sym_apply(c_sum, u)
        for k in range(3):
            r = l_own[k, line(x)] - 0.0625 * (near[k] + far[k] - v_sum[k])
            inverse = 16.0 / (48.0 * c[k] + c_sum[k])
            d = u[k] + (inverse * r) * (1.0 / theta_value)
            inv_own[k, line(x)] = inverse
            d_own[k, line(x)] = jnp.where(inner_row, d, 0.0)
        for e in range(6):
            cs_own[e, line(x)] = c_sum[e]

    @pl.loop(0, W, unroll=4)
    def _(x):
        v = sym_apply([c_own[e, line(x)] for e in range(6)], [d_own[k, line(x)] for k in range(3)])
        for k in range(3):
            v_own[k, line(x)] = v[k]

    def three_within(ref, e, x):
        below, above = jnp.maximum(x - 1, 0), jnp.minimum(x + 1, W - 1)
        return (ref[e, line(below)] + ref[e, line(above)]) + 2.0 * ref[e, line(x)]

    @pl.loop(0, W, unroll=2)
    def _(x):
        c = [c_own[e, line(x)] for e in range(6)]
        c_sum = [cs_own[e, line(x)] for e in range(6)]
        d = [d_own[k, line(x)] for k in range(3)]
        d_sum = [weigh(three_within(d_own, k, x)) for k in range(3)]
        v_sum = [weigh(three_within(v_own, k, x)) for k in range(3)]
        near = sym_apply(c, [64.0 * d[k] - d_sum[k] for k in range(3)])
        far = sym_apply(c_sum, d)
        for k in range(3):
            r_own[k, line(x)] = l_own[k, line(x)] - 0.0625 * (near[k] + far[k] - v_sum[k])

    turn = 7 - lax.broadcasted_iota(jnp.int32, (8, 128), 0)

    def turned(tile):
        return jnp.take_along_axis(tile, turn, axis=0, mode="promise_in_bounds")

    eight = lax.broadcasted_iota(jnp.int32, (8, 128), 0)
    low_sign = jnp.where(first, -1.0, 1.0)
    high_sign = jnp.where(last, -1.0, 1.0)
    end_sign = jnp.where(eight > 5, low_sign, jnp.where(eight < 2, high_sign, 1.0))

    def strip(s):
        ring = isinstance(s, int)
        n = RING if ring else W

        def ringed(row, index, middle):
            return jnp.concatenate([middle, (t2g if row < 2 else t2o)[s, index]], axis=0)

        place = lax.broadcasted_iota(jnp.int32, (W, 128), 0)
        c, u = [], []
        for row in range(4):
            layer = (1, 0, 0, 1)[row]
            codes = (rcv if row < 2 else snd)[s, line(3 + layer)].astype(jnp.int32)
            if row < 2:
                for e in range(6):
                    entry = lookup(codes, e)
                    if e > 3 and not ring:
                        entry = entry * jnp.where(s == 2, low_sign, high_sign)
                    c_strip[s, row, e, 0:W] = entry
            if ring:
                codes = (t2g if row < 2 else t2o)[s, 6 + layer].astype(jnp.int32)
                for e in range(6):
                    entry = lookup(codes, e)
                    c_strip[s, row, e, W:RING] = entry * end_sign if e > 3 else entry
            c.append([c_strip[s, row, e, 0:n] for e in range(6)])
            u.append([])
            for k in range(3):
                if row == 0:
                    low_end = jnp.broadcast_to(rcv[s, pl.ds(ENDS + k, 1)], (W, 128))
                    high_end = jnp.broadcast_to(rcv[s, pl.ds(ENDS + 3 + k, 1)], (W, 128))
                    middle = jnp.where(place == 0, low_end, 0.0)
                    middle = jnp.where(place == W - 1, high_end, middle)
                elif row == 1:
                    middle = rcv[s, line(k)]
                else:
                    middle = u_own[k, own_rows(s, layer)]
                u[row].append(ringed(row, 3 * layer + k, middle) if ring else middle)
        v = [sym_apply(c[row], u[row]) if ring or row > 0 else None for row in range(4)]

        def three_rows(f, row, k):
            return (f[row - 1][k] + f[row + 1][k]) + 2.0 * f[row][k]

        def sums(f, row, k):
            if not ring:
                return weigh(f[2][k] if row == 1 else three_rows(f, row, k))
            whole = three_rows(f, row, k)
            rest = jnp.concatenate(
                [f[2][k][0:W], whole[W:RING]] if row == 1 else [whole[0:W], f[1][k][W:RING]],
                axis=0,
            )
            middle, ends = (rest, whole) if row == 1 else (whole, rest)
            h = jnp.concatenate([along_row(middle)[0:W], along_row(ends)[W:RING]], axis=0)
            return along_depth(h)

        tail = (lax.broadcasted_iota(jnp.int32, (n, 128), 0) >= W) if ring else None
        raw = {1: jnp.where(tail, 64.0, 0.0) if ring else 0.0, 2: jnp.where(tail, 0.0, 64.0) if ring else 64.0}
        part, inverse, c_sum = {}, {}, {}
        for row in (1, 2):
            c_sum[row] = [weigh(three_rows(c, row, e), True) for e in range(6)]
            u_sum = [sums(u, row, k) for k in range(3)]
            v_sum = [sums(v, row, k) for k in range(3)]
            near = sym_apply(c[row], [raw[row] * u[row][k] - u_sum[k] for k in range(3)])
            far = sym_apply(c_sum[row], u[row])
            part[row] = [0.0625 * (near[k] + far[k] - v_sum[k]) for k in range(3)]
            inverse[row] = [16.0 / (48.0 * c[row][k] + c_sum[row][k]) for k in range(3)]

        def start_of(row, k):
            if row == 1:
                middle = rcv[s, pl.ds(PART + W * k, W)]
            else:
                middle = l_own[k, own_rows(s, 0)]
            return ringed(row, 8 + k, middle) if ring else middle

        if ring:
            receive(rcv.at[s, late], late_recv_sem.at[s])
        d = {}
        for row in (1, 2):
            d[row] = []
            for k in range(3):
                r = start_of(row, k) - part[row][k]
                step = u[row][k] + (inverse[row][k] * r) * (1.0 / theta_value)
                d[row].append(step if ring else jnp.where(inner_row, step, 0.0))
        v = {row: sym_apply(c[row], d[row]) for row in (1, 2)}
        d_sum = [weigh(d[1][k] + 2.0 * d[2][k])[0:W] for k in range(3)]
        v_sum = [weigh(v[1][k] + 2.0 * v[2][k])[0:W] for k in range(3)]
        c2 = [t[0:W] for t in c[2]]
        c3 = [t[0:W] for t in c[3]]
        d2 = [t[0:W] for t in d[2]]
        near = sym_apply(c2, [64.0 * d2[k] - d_sum[k] for k in range(3)])
        far = sym_apply([t[0:W] for t in c_sum[2]], d2)
        outer = [near[k] + far[k] - v_sum[k] for k in range(3)]
        d_sum = [weigh(d[2][k])[0:W] for k in range(3)]
        v_sum = [weigh(v[2][k])[0:W] for k in range(3)]
        near = sym_apply(c3, d_sum)
        if ring:
            nearer, farther = sides[s]
            rows_0, rows_1 = pl.ds(nearer, W, stride=W), pl.ds(farther, W, stride=W)
        else:
            nearer = jnp.where(s == 2, 0, W - 1)
            rows_0, rows_1 = line(nearer), line(jnp.where(s == 2, 1, W - 2))
        for k in range(3):
            r_own[k, rows_0] = r_own[k, rows_0] - 0.0625 * outer[k]
            r_own[k, rows_1] = r_own[k, rows_1] + 0.0625 * (near[k] + v_sum[k])
            d_own[k, rows_0] = d2[k]
            inv_own[k, rows_0] = inverse[2][k][0:W]

    def turn_strip(s):
        @pl.when(jnp.logical_or(first, last))
        def _():
            lines = [W * i for i in range(5)] + [PART + W * k for k in range(3)]
            for at, sign in zip(lines, VECTOR + (1.0, 1.0) + VECTOR):
                head, tail = rcv[s, at : at + 8], rcv[s, at + 8 : at + W]
                rcv[s, at : at + 8] = sign * turned(tail)
                rcv[s, at + 8 : at + W] = sign * turned(head)
            for k in range(3):
                one, two = rcv[s, ENDS + k], rcv[s, ENDS + 3 + k]
                rcv[s, ENDS + k] = VECTOR[k] * two
                rcv[s, ENDS + 3 + k] = VECTOR[k] * one

    def receive_edge(s):
        receive(rcv.at[s, early], recv_sem.at[s])
        receive(rcv.at[s, late], late_recv_sem.at[s])

    side_a = jnp.where(first, 3, 2)
    side_b = 5 - side_a
    receive_edge(side_a)
    strip(side_a)
    receive_edge(side_b)
    turn_strip(side_b)

    for s in range(2):
        for j in range(2):
            at = sides[s][j]
            for side, spot in ((2, (7, 6)), (3, (0, 1))):
                for c in range(3):
                    t2o[s, 3 * j + c, spot[0]] = rcv[side, W * c + at]
                    if j == 0:
                        t2o[s, c, spot[1]] = rcv[side, ENDS + 3 * s + c]
                        t2o[s, 8 + c, spot[0]] = rcv[side, PART + W * c + at]
                for i in range(2):
                    t2o[s, 6 + j, spot[i]] = rcv[side, CODES + W * i + at]

    def receive_y(s):
        receive(rcv.at[s, early], recv_sem.at[s])
        for end in range(2):
            receive(corner_ref(s, end), recv_sem.at[4 + 2 * end + s])
        for mirrored, base in ((first, 6), (last, 0)):

            @pl.when(mirrored)
            def _():
                for i in range(VALUES):
                    one, two = t2g[s, i, base], t2g[s, i, base + 1]
                    t2g[s, i, base] = SIGNS[i] * two
                    t2g[s, i, base + 1] = SIGNS[i] * one

    receive_y(1)
    strip(side_b)
    strip(1)
    receive_y(0)
    strip(0)

    for n in range(4):
        for copy in edge(n, *to[n]):
            copy.wait_send()
    for n in range(4, 8):

        @pl.when(jnp.logical_not(here[n]))
        def _():
            source = csnd.at[n % 2, n // 6]
            pltpu.make_async_copy(source, source, send_sem.at[n]).wait()


def finish(u, r, d, inv, out_u, out_r, result, sem):
    copies = [pltpu.make_async_copy(r, out_r, sem.at[3])]
    copies[0].start()
    for k in range(3):
        copies.append(pltpu.make_async_copy(result.at[k], out_u.at[k], sem.at[k]))

        @pl.loop(0, W, unroll=8)
        def _(x):
            step = d[k, line(x)] - u[k, line(x)]
            step = (rho_second * rho_first) * step
            step += (2.0 * rho_second / delta_value) * (inv[k, line(x)] * r[k, line(x)])
            result[k, line(x)] = d[k, line(x)] + step

        copies[-1].start()
    for copy in copies:
        copy.wait()


def body(load, guess, labels, segments, stiffness):
    vmem = pl.BlockSpec(memory_space=pltpu.VMEM)
    hbm = pl.BlockSpec(memory_space=pltpu.HBM)
    shape = load.shape
    field = (3, W * W, 128)
    inputs = (
        load.reshape(field),
        guess.reshape(field),
        labels.reshape(field[1:]),
        segments.reshape(field[1:]),
        stiffness,
    )
    results = pl.pallas_call(
        kernel,
        out_shape=[pltpu.VMEM(field, f32)] * 4,
        in_specs=[hbm] * 5,
        out_specs=[vmem] * 4,
        scratch_shapes=[
            pltpu.VMEM(stiffness.shape, f32),
            pltpu.VMEM((8, 128), f32),
            pltpu.VMEM(field, f32),
            pltpu.VMEM(field[1:], f32),
            pltpu.VMEM(field[1:], jnp.int32),
            pltpu.VMEM(field[1:], jnp.int32),
            pltpu.VMEM((6,) + field[1:], f32),
            pltpu.VMEM(field, f32),
            pltpu.VMEM((6,) + field[1:], f32),
            pltpu.VMEM((4, LINES, 128), f32),
            pltpu.VMEM((2, 2, VALUES, 2, 128), f32),
            pltpu.VMEM((4, LINES, 128), f32),
            pltpu.VMEM((2, VALUES, 8, 128), f32),
            pltpu.VMEM((2, VALUES, 8, 128), f32),
            pltpu.VMEM((4, 4, 6, RING, 128), f32),
            pltpu.SemaphoreType.DMA((5,)),
            pltpu.SemaphoreType.DMA((8,)),
            pltpu.SemaphoreType.DMA((4,)),
            pltpu.SemaphoreType.DMA((8,)),
            pltpu.SemaphoreType.DMA((4,)),
        ],
        compiler_params=pltpu.CompilerParams(
            collective_id=0, has_side_effects=True, vmem_limit_bytes=40 * 2**20
        ),
    )(*[pltpu.with_memory_space_constraint(x, pltpu.HBM) for x in inputs])
    out_u, out_r = pl.pallas_call(
        finish,
        out_shape=[jax.ShapeDtypeStruct(field, f32)] * 2,
        in_specs=[vmem] * 4,
        out_specs=[hbm] * 2,
        scratch_shapes=[pltpu.VMEM(field, f32), pltpu.SemaphoreType.DMA((4,))],
    )(*[pltpu.with_memory_space_constraint(x, pltpu.VMEM) for x in results])
    return out_u.reshape(shape), out_r.reshape(shape)


def solution(mesh):
    field = P(None, "gx", "gy", None)
    voxel = P("gx", "gy", None)
    return jax.shard_map(
        body,
        mesh=mesh,
        in_specs=(field, field, voxel, voxel, P()),
        out_specs=(field, field),
        check_vma=False,
    )
```

```python
import functools

import jax
import jax.numpy as jnp
from jax import lax
from jax.experimental import pallas as pl
from jax.experimental.pallas import tpu as pltpu
from jax.sharding import PartitionSpec as P

SEGS = 16
MESH = pl.DeviceIdType.MESH
f32 = jnp.float32

theta_value = 1.025
delta_value = 0.975
sigma_value = theta_value / delta_value
rho_first = 1.0 / sigma_value
rho_second = 1.0 / (2.0 * sigma_value - rho_first)

W = 16
RING = W + 8
CODES, ENDS, PART, LINES = 3 * W, 5 * W, 5 * W + 8, 8 * W + 8
VALUES = 11
VECTOR = (-1.0, -1.0, 1.0)
SIGNS = VECTOR * 2 + (1.0, 1.0) + VECTOR


def routes(gx, gy):
    nx, ny = lax.axis_size("gx"), lax.axis_size("gy")
    first, last = gx == 0, gx == nx - 1
    xl = jnp.where(first, 0, gx - 1)
    xh = jnp.where(last, nx - 1, gx + 1)
    down, up = lax.rem(gy + ny - 1, ny), lax.rem(gy + 1, ny)
    mid = ny - 1 - gy
    mid_down, mid_up = lax.rem(mid + ny - 1, ny), lax.rem(mid + 1, ny)
    pick = jnp.where
    return [
        ((gx, down), 1),
        ((gx, up), 0),
        ((xl, pick(first, mid, gy)), pick(first, 2, 3)),
        ((xh, pick(last, mid, gy)), pick(last, 3, 2)),
        ((xl, pick(first, mid_up, down)), (7, 4)),
        ((xl, pick(first, mid_down, up)), (6, 5)),
        ((xh, pick(last, mid_up, down)), (5, 6)),
        ((xh, pick(last, mid_down, up)), (4, 7)),
    ]


def sym_apply(c, u):
    return (
        c[0] * u[0] + c[3] * u[1] + c[4] * u[2],
        c[3] * u[0] + c[1] * u[1] + c[5] * u[2],
        c[4] * u[0] + c[5] * u[1] + c[2] * u[2],
    )


def along_row(h):
    n = h.shape[0]
    return (h + h) + (pltpu.roll(h, 1, 0) + pltpu.roll(h, n - 1, 0))


def along_depth(h, repeat=False):
    lane = lax.broadcasted_iota(jnp.int32, h.shape, 1)
    end = h if repeat else jnp.zeros_like(h)
    below = jnp.where(lane == 0, end, pltpu.roll(h, 1, 1))
    above = jnp.where(lane == 127, end, pltpu.roll(h, 127, 1))
    return (h + h) + (below + above)


def along_open_row(h):
    place = lax.broadcasted_iota(jnp.int32, h.shape, 0)
    n = h.shape[0]
    below = jnp.where(place == 0, 0.0, pltpu.roll(h, 1, 0))
    above = jnp.where(place == n - 1, 0.0, pltpu.roll(h, n - 1, 0))
    return (h + h) + (below + above)


def weigh(h, repeat=False):
    return along_depth(along_row(h), repeat)


def line(x):
    return pl.ds(W * x, W) if isinstance(x, int) else pl.ds(pl.multiple_of(W * x, W), W)


def kernel(
    load, guess, labels, segments, stiffness, u_own, r_own, d_own, inv_own,
    blocks, table, l_own, k_own, lab, seg, c_own, v_own, cs_own, snd, csnd, rcv, t2g, t2o, c_strip,
    local_sem, send_sem, late_send_sem, recv_sem, late_recv_sem,
):
    gx, gy = lax.axis_index("gx"), lax.axis_index("gy")
    first, last = gx == 0, gx == lax.axis_size("gx") - 1
    fetch = [
        pltpu.make_async_copy(labels, lab, local_sem.at[0]),
        pltpu.make_async_copy(segments, seg, local_sem.at[1]),
        pltpu.make_async_copy(stiffness, blocks, local_sem.at[4]),
        pltpu.make_async_copy(guess, u_own, local_sem.at[2]),
        pltpu.make_async_copy(load, l_own, local_sem.at[3]),
    ]
    for copy in fetch:
        copy.start()
    t2g[...] = jnp.zeros(t2g.shape, f32)

    to = routes(gx, gy)
    here = [None] * 4 + [jnp.logical_and(d[0] == gx, d[1] == gy) for d, _ in to[4:]]
    barrier = pltpu.get_barrier_semaphore()
    expected = 4
    for (device, _), same in zip(to, here):
        if same is None:
            pl.semaphore_signal(barrier, inc=1, device_id=device, device_id_type=MESH)
        else:

            @pl.when(jnp.logical_not(same))
            def _():
                pl.semaphore_signal(barrier, inc=1, device_id=device, device_id_type=MESH)

            expected = expected + jnp.where(same, 0, 1)

    t2o[...] = jnp.zeros(t2o.shape, f32)
    fetch[0].wait()
    fetch[1].wait()
    k_own[...] = (lab[...] * SEGS + seg[...]).astype(f32)
    fetch[3].wait()
    fetch[4].wait()
    sides = ((0, 1), (W - 1, W - 2))

    def own_rows(s, j):
        if isinstance(s, int):
            return pl.ds(sides[s % 2][j], W, stride=W) if s < 2 else line(sides[s % 2][j])
        return line(jnp.where(s == 2, sides[0][j], sides[1][j]))

    for s in range(4):
        for c in range(3):
            snd[s, line(c)] = u_own[c, own_rows(s, 0)]
            for end in range(2):
                at = sides[s % 2][1]
                at = (W * (W - 1) * end + at) if s < 2 else (W * at + (W - 1) * end)
                snd[s, ENDS + 3 * end + c] = u_own[c, at]
        for j in range(2):
            snd[s, line(3 + j)] = k_own[own_rows(s, j)]
    for s in range(2):
        for end in range(2):
            for j in range(2):
                at = sides[s][j] + W * (W - 2) * end
                for i in range(2):
                    for c in range(3):
                        csnd[s, end, 3 * j + c, i] = u_own[c, at + W * i]
                        if j == 0:
                            csnd[s, end, 8 + c, i] = l_own[c, at + W * i]
                    csnd[s, end, 6 + j, i] = k_own[at + W * i]
    fetch[2].wait()
    table[0:6, 0 : stiffness.shape[1]] = blocks[...]

    def lookup(codes, entry):
        rows = jnp.broadcast_to(table[entry : entry + 1, :], codes.shape)
        return jnp.take_along_axis(rows, codes, axis=1, mode="promise_in_bounds")

    for s in range(4):
        c, u = [], []
        for j in range(2):
            codes = snd[s, line(3 + j)].astype(jnp.int32)
            c.append([lookup(codes, e) for e in range(6)])
            u.append([u_own[k, own_rows(s, j)] for k in range(3)])
            for e in range(6):
                c_strip[s, 2 + j, e, 0:W] = c[j][e]
        v = [sym_apply(c[j], u[j]) for j in range(2)]
        u_sum = [along_depth(along_open_row(2.0 * u[0][k] + u[1][k])) for k in range(3)]
        v_sum = [along_depth(along_open_row(2.0 * v[0][k] + v[1][k])) for k in range(3)]
        near = sym_apply(c[0], [64.0 * u[0][k] - u_sum[k] for k in range(3)])
        for k in range(3):
            part = l_own[k, own_rows(s, 0)] - 0.0625 * (near[k] - v_sum[k])
            snd[s, pl.ds(PART + W * k, W)] = part

    pl.semaphore_wait(barrier, expected)

    early, late = pl.ds(0, PART), pl.ds(PART, LINES - PART)
    parts = ((early, send_sem, recv_sem), (late, late_send_sem, late_recv_sem))

    whole = ((pl.ds(0, LINES), send_sem, recv_sem),)

    def n_is_y(n):
        return not isinstance(n, int) or n < 2

    def edge(n, device, slot):
        return [
            pltpu.make_async_remote_copy(
                src_ref=snd.at[n, values],
                dst_ref=rcv.at[slot, values],
                send_sem=out_sem.at[n],
                recv_sem=in_sem.at[slot],
                device_id=device,
                device_id_type=MESH,
            )
            for values, out_sem, in_sem in (parts if n_is_y(n) else whole)
        ]

    def corner_ref(side, end):
        return t2g.at[side, :, pl.ds(0 if end else 6, 2)]

    def send_x(n):
        for copy in edge(n, *to[n]):
            copy.start()

    def send_y(side):
        for copy in edge(side, (gx, jnp.where(side == 0, to[0][0][1], to[1][0][1])), 1 - side):
            copy.start()

    def send_corners(side):
        for end in range(2):
            low, high = to[4 + 2 * end][0], to[5 + 2 * end][0]
            device = (low[0], jnp.where(side == 0, low[1], high[1]))
            same = jnp.where(side == 0, here[4 + 2 * end], here[5 + 2 * end])
            mirrored = (first, last)[end]
            n = 4 + 2 * end + side
            source = csnd.at[side, end]

            def remote(target, slot):
                return pltpu.make_async_remote_copy(
                    src_ref=source,
                    dst_ref=target,
                    send_sem=send_sem.at[n],
                    recv_sem=recv_sem.at[slot],
                    device_id=device,
                    device_id_type=MESH,
                )

            ahead = remote(corner_ref(1 - side, 1 - end), 4 + 2 * (1 - end) + (1 - side))
            back = remote(corner_ref(side, end), n)
            local = pltpu.make_async_copy(source, corner_ref(side, end), recv_sem.at[n])
            pl.when(jnp.logical_not(mirrored))(ahead.start)
            pl.when(jnp.logical_and(mirrored, jnp.logical_not(same)))(back.start)
            pl.when(same)(local.start)

    group = lax.rem(gy, 4)
    odd = lax.rem(lax.div(gx, 2), 2)
    hasty = jnp.where(group == 0, odd, jnp.where(group == 3, 1, 0))
    mirrors = ((2, first), (3, last))

    @pl.when(group == 0)
    def _():
        upper = lax.rem(gx, 2) == 1
        pl.when(jnp.logical_and(upper, jnp.logical_not(last)))(lambda: send_x(3))
        pl.when(jnp.logical_not(first))(lambda: send_x(2))
        pl.when(jnp.logical_not(jnp.logical_or(upper, last)))(lambda: send_x(3))

    send_corners(hasty)
    send_corners(1 - hasty)

    @pl.when(group == 3)
    def _():
        for n, mirrored in mirrors:
            pl.when(mirrored)(lambda: send_x(n))
    send_y(hasty)

    @pl.when(group == 2)
    def _():
        for n, mirrored in mirrors:
            pl.when(mirrored)(lambda: send_x(n))

    @pl.when(group != 0)
    def _():
        for n, mirrored in mirrors:
            pl.when(jnp.logical_not(mirrored))(lambda: send_x(n))

    send_y(1 - hasty)

    @pl.when(group < 2)
    def _():
        for n, mirrored in mirrors:
            pl.when(mirrored)(lambda: send_x(n))

    def receive(ref, sem):
        pltpu.make_async_copy(ref, ref, sem).wait()

    inner_row = lax.broadcasted_iota(jnp.int32, (W, 128), 0)
    inner_row = jnp.logical_and(inner_row > 0, inner_row < W - 1)
    none = jnp.zeros((W, 128), f32)
    for x in (0, W - 1):
        for c in range(3):
            d_own[c, line(x)] = none
        for e in range(6):
            cs_own[e, line(x)] = none

    @pl.loop(0, W, unroll=4)
    def _(x):
        codes = k_own[line(x)].astype(jnp.int32)
        c = [lookup(codes, e) for e in range(6)]
        for e in range(6):
            c_own[e, line(x)] = c[e]
        v = sym_apply(c, [u_own[k, line(x)] for k in range(3)])
        for k in range(3):
            v_own[k, line(x)] = v[k]

    def three(ref, e, x):
        return (ref[e, line(x - 1)] + ref[e, line(x + 1)]) + 2.0 * ref[e, line(x)]

    @pl.loop(1, W - 1, unroll=2)
    def _(x):
        c = [c_own[e, line(x)] for e in range(6)]
        u = [u_own[k, line(x)] for k in range(3)]
        c_sum = [weigh(three(c_own, e, x), True) for e in range(6)]
        u_sum = [weigh(three(u_own, k, x)) for k in range(3)]
        v_sum = [weigh(three(v_own, k, x)) for k in range(3)]
        near = sym_apply(c, [64.0 * u[k] - u_sum[k] for k in range(3)])
        far = sym_apply(c_sum, u)
        for k in range(3):
            r = l_own[k, line(x)] - 0.0625 * (near[k] + far[k] - v_sum[k])
            inverse = 16.0 / (48.0 * c[k] + c_sum[k])
            d = u[k] + (inverse * r) * (1.0 / theta_value)
            inv_own[k, line(x)] = inverse
            d_own[k, line(x)] = jnp.where(inner_row, d, 0.0)
        for e in range(6):
            cs_own[e, line(x)] = c_sum[e]

    @pl.loop(0, W, unroll=4)
    def _(x):
        v = sym_apply([c_own[e, line(x)] for e in range(6)], [d_own[k, line(x)] for k in range(3)])
        for k in range(3):
            v_own[k, line(x)] = v[k]

    def three_within(ref, e, x):
        below, above = jnp.maximum(x - 1, 0), jnp.minimum(x + 1, W - 1)
        return (ref[e, line(below)] + ref[e, line(above)]) + 2.0 * ref[e, line(x)]

    @pl.loop(0, W, unroll=2)
    def _(x):
        c = [c_own[e, line(x)] for e in range(6)]
        c_sum = [cs_own[e, line(x)] for e in range(6)]
        d = [d_own[k, line(x)] for k in range(3)]
        d_sum = [weigh(three_within(d_own, k, x)) for k in range(3)]
        v_sum = [weigh(three_within(v_own, k, x)) for k in range(3)]
        near = sym_apply(c, [64.0 * d[k] - d_sum[k] for k in range(3)])
        far = sym_apply(c_sum, d)
        for k in range(3):
            r_own[k, line(x)] = l_own[k, line(x)] - 0.0625 * (near[k] + far[k] - v_sum[k])

    turn = 7 - lax.broadcasted_iota(jnp.int32, (8, 128), 0)

    def turned(tile):
        return jnp.take_along_axis(tile, turn, axis=0, mode="promise_in_bounds")

    eight = lax.broadcasted_iota(jnp.int32, (8, 128), 0)
    low_sign = jnp.where(first, -1.0, 1.0)
    high_sign = jnp.where(last, -1.0, 1.0)
    end_sign = jnp.where(eight > 5, low_sign, jnp.where(eight < 2, high_sign, 1.0))

    def strip(s):
        ring = isinstance(s, int)
        n = RING if ring else W

        def ringed(row, index, middle):
            return jnp.concatenate([middle, (t2g if row < 2 else t2o)[s, index]], axis=0)

        place = lax.broadcasted_iota(jnp.int32, (W, 128), 0)
        c, u = [], []
        for row in range(4):
            layer = (1, 0, 0, 1)[row]
            codes = (rcv if row < 2 else snd)[s, line(3 + layer)].astype(jnp.int32)
            if row < 2:
                for e in range(6):
                    entry = lookup(codes, e)
                    if e > 3 and not ring:
                        entry = entry * jnp.where(s == 2, low_sign, high_sign)
                    c_strip[s, row, e, 0:W] = entry
            if ring:
                codes = (t2g if row < 2 else t2o)[s, 6 + layer].astype(jnp.int32)
                for e in range(6):
                    entry = lookup(codes, e)
                    c_strip[s, row, e, W:RING] = entry * end_sign if e > 3 else entry
            c.append([c_strip[s, row, e, 0:n] for e in range(6)])
            u.append([])
            for k in range(3):
                if row == 0:
                    low_end = jnp.broadcast_to(rcv[s, pl.ds(ENDS + k, 1)], (W, 128))
                    high_end = jnp.broadcast_to(rcv[s, pl.ds(ENDS + 3 + k, 1)], (W, 128))
                    middle = jnp.where(place == 0, low_end, 0.0)
                    middle = jnp.where(place == W - 1, high_end, middle)
                elif row == 1:
                    middle = rcv[s, line(k)]
                else:
                    middle = u_own[k, own_rows(s, layer)]
                u[row].append(ringed(row, 3 * layer + k, middle) if ring else middle)
        v = [sym_apply(c[row], u[row]) if ring or row > 0 else None for row in range(4)]

        def three_rows(f, row, k):
            return (f[row - 1][k] + f[row + 1][k]) + 2.0 * f[row][k]

        def sums(f, row, k):
            if not ring:
                return weigh(f[2][k] if row == 1 else three_rows(f, row, k))
            whole = three_rows(f, row, k)
            rest = jnp.concatenate(
                [f[2][k][0:W], whole[W:RING]] if row == 1 else [whole[0:W], f[1][k][W:RING]],
                axis=0,
            )
            middle, ends = (rest, whole) if row == 1 else (whole, rest)
            h = jnp.concatenate([along_row(middle)[0:W], along_row(ends)[W:RING]], axis=0)
            return along_depth(h)

        tail = (lax.broadcasted_iota(jnp.int32, (n, 128), 0) >= W) if ring else None
        raw = {1: jnp.where(tail, 64.0, 0.0) if ring else 0.0, 2: jnp.where(tail, 0.0, 64.0) if ring else 64.0}
        part, inverse, c_sum = {}, {}, {}
        for row in (1, 2):
            c_sum[row] = [weigh(three_rows(c, row, e), True) for e in range(6)]
            u_sum = [sums(u, row, k) for k in range(3)]
            v_sum = [sums(v, row, k) for k in range(3)]
            near = sym_apply(c[row], [raw[row] * u[row][k] - u_sum[k] for k in range(3)])
            far = sym_apply(c_sum[row], u[row])
            part[row] = [0.0625 * (near[k] + far[k] - v_sum[k]) for k in range(3)]
            inverse[row] = [16.0 / (48.0 * c[row][k] + c_sum[row][k]) for k in range(3)]

        def start_of(row, k):
            if row == 1:
                middle = rcv[s, pl.ds(PART + W * k, W)]
            else:
                middle = l_own[k, own_rows(s, 0)]
            return ringed(row, 8 + k, middle) if ring else middle

        if ring:
            receive(rcv.at[s, late], late_recv_sem.at[s])
        d = {}
        for row in (1, 2):
            d[row] = []
            for k in range(3):
                r = start_of(row, k) - part[row][k]
                step = u[row][k] + (inverse[row][k] * r) * (1.0 / theta_value)
                d[row].append(step if ring else jnp.where(inner_row, step, 0.0))
        v = {row: sym_apply(c[row], d[row]) for row in (1, 2)}
        d_sum = [weigh(d[1][k] + 2.0 * d[2][k])[0:W] for k in range(3)]
        v_sum = [weigh(v[1][k] + 2.0 * v[2][k])[0:W] for k in range(3)]
        c2 = [t[0:W] for t in c[2]]
        c3 = [t[0:W] for t in c[3]]
        d2 = [t[0:W] for t in d[2]]
        near = sym_apply(c2, [64.0 * d2[k] - d_sum[k] for k in range(3)])
        far = sym_apply([t[0:W] for t in c_sum[2]], d2)
        outer = [near[k] + far[k] - v_sum[k] for k in range(3)]
        d_sum = [weigh(d[2][k])[0:W] for k in range(3)]
        v_sum = [weigh(v[2][k])[0:W] for k in range(3)]
        near = sym_apply(c3, d_sum)
        if ring:
            nearer, farther = sides[s]
            rows_0, rows_1 = pl.ds(nearer, W, stride=W), pl.ds(farther, W, stride=W)
        else:
            nearer = jnp.where(s == 2, 0, W - 1)
            rows_0, rows_1 = line(nearer), line(jnp.where(s == 2, 1, W - 2))
        for k in range(3):
            r_own[k, rows_0] = r_own[k, rows_0] - 0.0625 * outer[k]
            r_own[k, rows_1] = r_own[k, rows_1] + 0.0625 * (near[k] + v_sum[k])
            d_own[k, rows_0] = d2[k]
            inv_own[k, rows_0] = inverse[2][k][0:W]

    def turn_strip(s):
        @pl.when(jnp.logical_or(first, last))
        def _():
            lines = [W * i for i in range(5)] + [PART + W * k for k in range(3)]
            for at, sign in zip(lines, VECTOR + (1.0, 1.0) + VECTOR):
                head, tail = rcv[s, at : at + 8], rcv[s, at + 8 : at + W]
                rcv[s, at : at + 8] = sign * turned(tail)
                rcv[s, at + 8 : at + W] = sign * turned(head)
            for k in range(3):
                one, two = rcv[s, ENDS + k], rcv[s, ENDS + 3 + k]
                rcv[s, ENDS + k] = VECTOR[k] * two
                rcv[s, ENDS + 3 + k] = VECTOR[k] * one

    def receive_edge(s):
        receive(rcv.at[s], recv_sem.at[s])

    side_a = jnp.where(lax.rem(gx, 2) == 0, 3, 2)
    side_b = 5 - side_a
    receive_edge(side_a)
    strip(side_a)
    receive_edge(side_b)
    turn_strip(side_b)

    for s in range(2):
        for j in range(2):
            at = sides[s][j]
            for side, spot in ((2, (7, 6)), (3, (0, 1))):
                for c in range(3):
                    t2o[s, 3 * j + c, spot[0]] = rcv[side, W * c + at]
                    if j == 0:
                        t2o[s, c, spot[1]] = rcv[side, ENDS + 3 * s + c]
                        t2o[s, 8 + c, spot[0]] = rcv[side, PART + W * c + at]
                for i in range(2):
                    t2o[s, 6 + j, spot[i]] = rcv[side, CODES + W * i + at]

    def receive_y(s):
        receive(rcv.at[s, early], recv_sem.at[s])
        for end in range(2):
            receive(corner_ref(s, end), recv_sem.at[4 + 2 * end + s])
        for mirrored, base in ((first, 6), (last, 0)):

            @pl.when(mirrored)
            def _():
                for i in range(VALUES):
                    one, two = t2g[s, i, base], t2g[s, i, base + 1]
                    t2g[s, i, base] = SIGNS[i] * two
                    t2g[s, i, base + 1] = SIGNS[i] * one

    receive_y(1)
    strip(side_b)
    strip(1)
    receive_y(0)
    strip(0)

    for n in range(4):
        for copy in edge(n, *to[n]):
            copy.wait_send()
    for n in range(4, 8):

        @pl.when(jnp.logical_not(here[n]))
        def _():
            source = csnd.at[n % 2, n // 6]
            pltpu.make_async_copy(source, source, send_sem.at[n]).wait()


def finish(u, r, d, inv, out_u, out_r, result, sem):
    copies = [pltpu.make_async_copy(r, out_r, sem.at[3])]
    copies[0].start()
    for k in range(3):
        copies.append(pltpu.make_async_copy(result.at[k], out_u.at[k], sem.at[k]))

        @pl.loop(0, W, unroll=8)
        def _(x):
            step = d[k, line(x)] - u[k, line(x)]
            step = (rho_second * rho_first) * step
            step += (2.0 * rho_second / delta_value) * (inv[k, line(x)] * r[k, line(x)])
            result[k, line(x)] = d[k, line(x)] + step

        copies[-1].start()
    for copy in copies:
        copy.wait()


def body(load, guess, labels, segments, stiffness):
    vmem = pl.BlockSpec(memory_space=pltpu.VMEM)
    hbm = pl.BlockSpec(memory_space=pltpu.HBM)
    shape = load.shape
    field = (3, W * W, 128)
    inputs = (
        load.reshape(field),
        guess.reshape(field),
        labels.reshape(field[1:]),
        segments.reshape(field[1:]),
        stiffness,
    )
    results = pl.pallas_call(
        kernel,
        out_shape=[pltpu.VMEM(field, f32)] * 4,
        in_specs=[hbm] * 5,
        out_specs=[vmem] * 4,
        scratch_shapes=[
            pltpu.VMEM(stiffness.shape, f32),
            pltpu.VMEM((8, 128), f32),
            pltpu.VMEM(field, f32),
            pltpu.VMEM(field[1:], f32),
            pltpu.VMEM(field[1:], jnp.int32),
            pltpu.VMEM(field[1:], jnp.int32),
            pltpu.VMEM((6,) + field[1:], f32),
            pltpu.VMEM(field, f32),
            pltpu.VMEM((6,) + field[1:], f32),
            pltpu.VMEM((4, LINES, 128), f32),
            pltpu.VMEM((2, 2, VALUES, 2, 128), f32),
            pltpu.VMEM((4, LINES, 128), f32),
            pltpu.VMEM((2, VALUES, 8, 128), f32),
            pltpu.VMEM((2, VALUES, 8, 128), f32),
            pltpu.VMEM((4, 4, 6, RING, 128), f32),
            pltpu.SemaphoreType.DMA((5,)),
            pltpu.SemaphoreType.DMA((8,)),
            pltpu.SemaphoreType.DMA((4,)),
            pltpu.SemaphoreType.DMA((8,)),
            pltpu.SemaphoreType.DMA((4,)),
        ],
        compiler_params=pltpu.CompilerParams(
            collective_id=0, has_side_effects=True, vmem_limit_bytes=40 * 2**20
        ),
    )(*[pltpu.with_memory_space_constraint(x, pltpu.HBM) for x in inputs])
    out_u, out_r = pl.pallas_call(
        finish,
        out_shape=[jax.ShapeDtypeStruct(field, f32)] * 2,
        in_specs=[vmem] * 4,
        out_specs=[hbm] * 2,
        scratch_shapes=[pltpu.VMEM(field, f32), pltpu.SemaphoreType.DMA((4,))],
    )(*[pltpu.with_memory_space_constraint(x, pltpu.VMEM) for x in results])
    return out_u.reshape(shape), out_r.reshape(shape)


def solution(mesh):
    field = P(None, "gx", "gy", None)
    voxel = P("gx", "gy", None)
    return jax.shard_map(
        body,
        mesh=mesh,
        in_specs=(field, field, voxel, voxel, P()),
        out_specs=(field, field),
        check_vma=False,
    )
```

```python
import functools

import jax
import jax.numpy as jnp
from jax import lax
from jax.experimental import pallas as pl
from jax.experimental.pallas import tpu as pltpu
from jax.sharding import PartitionSpec as P

SEGS = 16
MESH = pl.DeviceIdType.MESH
f32 = jnp.float32

theta_value = 1.025
delta_value = 0.975
sigma_value = theta_value / delta_value
rho_first = 1.0 / sigma_value
rho_second = 1.0 / (2.0 * sigma_value - rho_first)

W = 16
RING = W + 8
CELLS = W * W
ROOM = CELLS + W
CODES, ENDS, PART, LINES = 3 * W, 5 * W, 5 * W + 8, 8 * W + 8
VALUES = 11
VECTOR = (-1.0, -1.0, 1.0)
SIGNS = VECTOR * 2 + (1.0, 1.0) + VECTOR


def routes(gx, gy):
    nx, ny = lax.axis_size("gx"), lax.axis_size("gy")
    first, last = gx == 0, gx == nx - 1
    xl = jnp.where(first, 0, gx - 1)
    xh = jnp.where(last, nx - 1, gx + 1)
    down, up = lax.rem(gy + ny - 1, ny), lax.rem(gy + 1, ny)
    mid = ny - 1 - gy
    mid_down, mid_up = lax.rem(mid + ny - 1, ny), lax.rem(mid + 1, ny)
    pick = jnp.where
    return [
        ((gx, down), 1),
        ((gx, up), 0),
        ((xl, pick(first, mid, gy)), pick(first, 2, 3)),
        ((xh, pick(last, mid, gy)), pick(last, 3, 2)),
        ((xl, pick(first, mid_up, down)), (7, 4)),
        ((xl, pick(first, mid_down, up)), (6, 5)),
        ((xh, pick(last, mid_up, down)), (5, 6)),
        ((xh, pick(last, mid_down, up)), (4, 7)),
    ]


def sym_apply(c, u):
    return (
        c[0] * u[0] + c[3] * u[1] + c[4] * u[2],
        c[3] * u[0] + c[1] * u[1] + c[5] * u[2],
        c[4] * u[0] + c[5] * u[1] + c[2] * u[2],
    )


def along_row(h):
    n = h.shape[0]
    return (h + h) + (pltpu.roll(h, 1, 0) + pltpu.roll(h, n - 1, 0))


def along_depth(h, repeat=False):
    lane = lax.broadcasted_iota(jnp.int32, h.shape, 1)
    end = h if repeat else jnp.zeros_like(h)
    below = jnp.where(lane == 0, end, pltpu.roll(h, 1, 1))
    above = jnp.where(lane == 127, end, pltpu.roll(h, 127, 1))
    return (h + h) + (below + above)


def along_open_row(h):
    place = lax.broadcasted_iota(jnp.int32, h.shape, 0)
    n = h.shape[0]
    below = jnp.where(place == 0, 0.0, pltpu.roll(h, 1, 0))
    above = jnp.where(place == n - 1, 0.0, pltpu.roll(h, n - 1, 0))
    return (h + h) + (below + above)


def weigh(h, repeat=False):
    return along_depth(along_row(h), repeat)


def line(x):
    return pl.ds(W * x, W) if isinstance(x, int) else pl.ds(pl.multiple_of(W * x, W), W)


def kernel(
    load, guess, labels, segments, stiffness, u_own, r_own, d_own, inv_own,
    blocks, table, l_own, k_own, lab, seg, c_own, v_own, cs_own, snd, csnd, rcv, t2g, t2o, c_strip,
    local_sem, send_sem, late_send_sem, recv_sem, late_recv_sem,
):
    gx, gy = lax.axis_index("gx"), lax.axis_index("gy")
    first, last = gx == 0, gx == lax.axis_size("gx") - 1
    fetch = [
        pltpu.make_async_copy(labels, lab, local_sem.at[0]),
        pltpu.make_async_copy(segments, seg, local_sem.at[1]),
        pltpu.make_async_copy(stiffness, blocks, local_sem.at[4]),
        pltpu.make_async_copy(guess, u_own.at[:, pl.ds(0, CELLS)], local_sem.at[2]),
        pltpu.make_async_copy(load, l_own.at[:, pl.ds(0, CELLS)], local_sem.at[3]),
    ]
    for copy in fetch:
        copy.start()
    t2g[...] = jnp.zeros(t2g.shape, f32)

    to = routes(gx, gy)
    here = [None] * 4 + [jnp.logical_and(d[0] == gx, d[1] == gy) for d, _ in to[4:]]
    barrier = pltpu.get_barrier_semaphore()
    expected = 4
    for (device, _), same in zip(to, here):
        if same is None:
            pl.semaphore_signal(barrier, inc=1, device_id=device, device_id_type=MESH)
        else:

            @pl.when(jnp.logical_not(same))
            def _():
                pl.semaphore_signal(barrier, inc=1, device_id=device, device_id_type=MESH)

            expected = expected + jnp.where(same, 0, 1)

    t2o[...] = jnp.zeros(t2o.shape, f32)
    fetch[0].wait()
    fetch[1].wait()
    k_own[0:CELLS] = (lab[...] * SEGS + seg[...]).astype(f32)
    fetch[3].wait()
    fetch[4].wait()
    sides = ((0, 1), (W - 1, W - 2))

    def own_rows(s, j):
        if isinstance(s, int):
            return pl.ds(sides[s % 2][j], W, stride=W) if s < 2 else line(sides[s % 2][j])
        return line(jnp.where(s == 2, sides[0][j], sides[1][j]))

    for s in range(4):
        for c in range(3):
            snd[s, line(c)] = u_own[c, own_rows(s, 0)]
            for end in range(2):
                at = sides[s % 2][1]
                at = (W * (W - 1) * end + at) if s < 2 else (W * at + (W - 1) * end)
                snd[s, ENDS + 3 * end + c] = u_own[c, at]
        for j in range(2):
            snd[s, line(3 + j)] = k_own[own_rows(s, j)]
    for s in range(2):
        for end in range(2):
            for j in range(2):
                at = sides[s][j] + W * (W - 2) * end
                for i in range(2):
                    for c in range(3):
                        csnd[s, end, 3 * j + c, i] = u_own[c, at + W * i]
                        if j == 0:
                            csnd[s, end, 8 + c, i] = l_own[c, at + W * i]
                    csnd[s, end, 6 + j, i] = k_own[at + W * i]
    fetch[2].wait()
    table[0:6, 0 : stiffness.shape[1]] = blocks[...]

    def lookup(codes, entry):
        rows = jnp.broadcast_to(table[entry : entry + 1, :], codes.shape)
        return jnp.take_along_axis(rows, codes, axis=1, mode="promise_in_bounds")

    for s in range(4):
        c, u = [], []
        for j in range(2):
            codes = snd[s, line(3 + j)].astype(jnp.int32)
            c.append([lookup(codes, e) for e in range(6)])
            u.append([u_own[k, own_rows(s, j)] for k in range(3)])
            for e in range(6):
                c_strip[s, 2 + j, e, 0:W] = c[j][e]
        v = [sym_apply(c[j], u[j]) for j in range(2)]
        u_sum = [along_depth(along_open_row(2.0 * u[0][k] + u[1][k])) for k in range(3)]
        v_sum = [along_depth(along_open_row(2.0 * v[0][k] + v[1][k])) for k in range(3)]
        near = sym_apply(c[0], [64.0 * u[0][k] - u_sum[k] for k in range(3)])
        for k in range(3):
            part = l_own[k, own_rows(s, 0)] - 0.0625 * (near[k] - v_sum[k])
            snd[s, pl.ds(PART + W * k, W)] = part

    pl.semaphore_wait(barrier, expected)

    early, late = pl.ds(0, PART), pl.ds(PART, LINES - PART)
    parts = ((early, send_sem, recv_sem), (late, late_send_sem, late_recv_sem))

    whole = ((pl.ds(0, LINES), send_sem, recv_sem),)

    def n_is_y(n):
        return not isinstance(n, int) or n < 2

    def edge(n, device, slot):
        return [
            pltpu.make_async_remote_copy(
                src_ref=snd.at[n, values],
                dst_ref=rcv.at[slot, values],
                send_sem=out_sem.at[n],
                recv_sem=in_sem.at[slot],
                device_id=device,
                device_id_type=MESH,
            )
            for values, out_sem, in_sem in (parts if n_is_y(n) else whole)
        ]

    def corner_ref(side, end):
        return t2g.at[side, :, pl.ds(0 if end else 6, 2)]

    def send_x(n):
        for copy in edge(n, *to[n]):
            copy.start()

    def send_y(side):
        for copy in edge(side, (gx, jnp.where(side == 0, to[0][0][1], to[1][0][1])), 1 - side):
            copy.start()

    def send_corners(side):
        for end in range(2):
            low, high = to[4 + 2 * end][0], to[5 + 2 * end][0]
            device = (low[0], jnp.where(side == 0, low[1], high[1]))
            same = jnp.where(side == 0, here[4 + 2 * end], here[5 + 2 * end])
            mirrored = (first, last)[end]
            n = 4 + 2 * end + side
            source = csnd.at[side, end]

            def remote(target, slot):
                return pltpu.make_async_remote_copy(
                    src_ref=source,
                    dst_ref=target,
                    send_sem=send_sem.at[n],
                    recv_sem=recv_sem.at[slot],
                    device_id=device,
                    device_id_type=MESH,
                )

            ahead = remote(corner_ref(1 - side, 1 - end), 4 + 2 * (1 - end) + (1 - side))
            back = remote(corner_ref(side, end), n)
            local = pltpu.make_async_copy(source, corner_ref(side, end), recv_sem.at[n])
            pl.when(jnp.logical_not(mirrored))(ahead.start)
            pl.when(jnp.logical_and(mirrored, jnp.logical_not(same)))(back.start)
            pl.when(same)(local.start)

    group = lax.rem(gy, 4)
    odd = lax.rem(lax.div(gx, 2), 2)
    hasty = jnp.where(group == 0, odd, jnp.where(group == 3, 1, 0))
    mirrors = ((2, first), (3, last))

    @pl.when(group == 0)
    def _():
        upper = lax.rem(gx, 2) == 1
        pl.when(jnp.logical_and(upper, jnp.logical_not(last)))(lambda: send_x(3))
        pl.when(jnp.logical_not(first))(lambda: send_x(2))
        pl.when(jnp.logical_not(jnp.logical_or(upper, last)))(lambda: send_x(3))

    send_corners(hasty)
    send_corners(1 - hasty)

    @pl.when(group == 3)
    def _():
        for n, mirrored in mirrors:
            pl.when(mirrored)(lambda: send_x(n))
    send_y(hasty)

    @pl.when(group == 2)
    def _():
        for n, mirrored in mirrors:
            pl.when(mirrored)(lambda: send_x(n))

    @pl.when(group != 0)
    def _():
        for n, mirrored in mirrors:
            pl.when(jnp.logical_not(mirrored))(lambda: send_x(n))

    send_y(1 - hasty)

    @pl.when(group < 2)
    def _():
        for n, mirrored in mirrors:
            pl.when(mirrored)(lambda: send_x(n))

    def receive(ref, sem):
        pltpu.make_async_copy(ref, ref, sem).wait()

    inner_row = lax.broadcasted_iota(jnp.int32, (W, 128), 0)
    inner_row = jnp.logical_and(inner_row > 0, inner_row < W - 1)
    none = jnp.zeros((W, 128), f32)
    for x in (0, W - 1):
        for c in range(3):
            d_own[c, line(x)] = none
        for e in range(6):
            cs_own[e, line(x)] = none

    @pl.loop(0, W, unroll=4)
    def _(x):
        codes = k_own[line(x)].astype(jnp.int32)
        c = [lookup(codes, e) for e in range(6)]
        for e in range(6):
            c_own[e, line(x)] = c[e]
        v = sym_apply(c, [u_own[k, line(x)] for k in range(3)])
        for k in range(3):
            v_own[k, line(x)] = v[k]

    def three(ref, e, x):
        return (ref[e, line(x - 1)] + ref[e, line(x + 1)]) + 2.0 * ref[e, line(x)]

    @pl.loop(1, W - 1, unroll=2)
    def _(x):
        c = [c_own[e, line(x)] for e in range(6)]
        u = [u_own[k, line(x)] for k in range(3)]
        c_sum = [weigh(three(c_own, e, x), True) for e in range(6)]
        u_sum = [weigh(three(u_own, k, x)) for k in range(3)]
        v_sum = [weigh(three(v_own, k, x)) for k in range(3)]
        near = sym_apply(c, [64.0 * u[k] - u_sum[k] for k in range(3)])
        far = sym_apply(c_sum, u)
        for k in range(3):
            r = l_own[k, line(x)] - 0.0625 * (near[k] + far[k] - v_sum[k])
            inverse = 16.0 / (48.0 * c[k] + c_sum[k])
            d = u[k] + (inverse * r) * (1.0 / theta_value)
            inv_own[k, line(x)] = inverse
            d_own[k, line(x)] = jnp.where(inner_row, d, 0.0)
        for e in range(6):
            cs_own[e, line(x)] = c_sum[e]

    @pl.loop(0, W, unroll=4)
    def _(x):
        v = sym_apply([c_own[e, line(x)] for e in range(6)], [d_own[k, line(x)] for k in range(3)])
        for k in range(3):
            v_own[k, line(x)] = v[k]

    def three_within(ref, e, x):
        below, above = jnp.maximum(x - 1, 0), jnp.minimum(x + 1, W - 1)
        return (ref[e, line(below)] + ref[e, line(above)]) + 2.0 * ref[e, line(x)]

    @pl.loop(0, W, unroll=2)
    def _(x):
        c = [c_own[e, line(x)] for e in range(6)]
        c_sum = [cs_own[e, line(x)] for e in range(6)]
        d = [d_own[k, line(x)] for k in range(3)]
        d_sum = [weigh(three_within(d_own, k, x)) for k in range(3)]
        v_sum = [weigh(three_within(v_own, k, x)) for k in range(3)]
        near = sym_apply(c, [64.0 * d[k] - d_sum[k] for k in range(3)])
        far = sym_apply(c_sum, d)
        for k in range(3):
            r_own[k, line(x)] = l_own[k, line(x)] - 0.0625 * (near[k] + far[k] - v_sum[k])

    turn = 7 - lax.broadcasted_iota(jnp.int32, (8, 128), 0)

    def turned(tile):
        return jnp.take_along_axis(tile, turn, axis=0, mode="promise_in_bounds")

    eight = lax.broadcasted_iota(jnp.int32, (8, 128), 0)
    low_sign = jnp.where(first, -1.0, 1.0)
    high_sign = jnp.where(last, -1.0, 1.0)
    end_sign = jnp.where(eight > 5, low_sign, jnp.where(eight < 2, high_sign, 1.0))

    def strip(s):
        ring = isinstance(s, int)
        n = RING if ring else W

        def ringed(row, index, middle):
            return jnp.concatenate([middle, (t2g if row < 2 else t2o)[s, index]], axis=0)

        place = lax.broadcasted_iota(jnp.int32, (W, 128), 0)
        c, u = [], []
        for row in range(4):
            layer = (1, 0, 0, 1)[row]
            codes = (rcv if row < 2 else snd)[s, line(3 + layer)].astype(jnp.int32)
            if row < 2:
                for e in range(6):
                    entry = lookup(codes, e)
                    if e > 3 and not ring:
                        entry = entry * jnp.where(s == 2, low_sign, high_sign)
                    c_strip[s, row, e, 0:W] = entry
            if ring:
                codes = (t2g if row < 2 else t2o)[s, 6 + layer].astype(jnp.int32)
                for e in range(6):
                    entry = lookup(codes, e)
                    c_strip[s, row, e, W:RING] = entry * end_sign if e > 3 else entry
            c.append([c_strip[s, row, e, 0:n] for e in range(6)])
            u.append([])
            for k in range(3):
                if row == 0:
                    low_end = jnp.broadcast_to(rcv[s, pl.ds(ENDS + k, 1)], (W, 128))
                    high_end = jnp.broadcast_to(rcv[s, pl.ds(ENDS + 3 + k, 1)], (W, 128))
                    middle = jnp.where(place == 0, low_end, 0.0)
                    middle = jnp.where(place == W - 1, high_end, middle)
                elif row == 1:
                    middle = rcv[s, line(k)]
                else:
                    middle = u_own[k, own_rows(s, layer)]
                u[row].append(ringed(row, 3 * layer + k, middle) if ring else middle)
        v = [sym_apply(c[row], u[row]) if ring or row > 0 else None for row in range(4)]

        def three_rows(f, row, k):
            return (f[row - 1][k] + f[row + 1][k]) + 2.0 * f[row][k]

        def sums(f, row, k):
            if not ring:
                return weigh(f[2][k] if row == 1 else three_rows(f, row, k))
            whole = three_rows(f, row, k)
            rest = jnp.concatenate(
                [f[2][k][0:W], whole[W:RING]] if row == 1 else [whole[0:W], f[1][k][W:RING]],
                axis=0,
            )
            middle, ends = (rest, whole) if row == 1 else (whole, rest)
            h = jnp.concatenate([along_row(middle)[0:W], along_row(ends)[W:RING]], axis=0)
            return along_depth(h)

        tail = (lax.broadcasted_iota(jnp.int32, (n, 128), 0) >= W) if ring else None
        raw = {1: jnp.where(tail, 64.0, 0.0) if ring else 0.0, 2: jnp.where(tail, 0.0, 64.0) if ring else 64.0}
        part, inverse, c_sum = {}, {}, {}
        for row in (1, 2):
            c_sum[row] = [weigh(three_rows(c, row, e), True) for e in range(6)]
            u_sum = [sums(u, row, k) for k in range(3)]
            v_sum = [sums(v, row, k) for k in range(3)]
            near = sym_apply(c[row], [raw[row] * u[row][k] - u_sum[k] for k in range(3)])
            far = sym_apply(c_sum[row], u[row])
            part[row] = [0.0625 * (near[k] + far[k] - v_sum[k]) for k in range(3)]
            inverse[row] = [16.0 / (48.0 * c[row][k] + c_sum[row][k]) for k in range(3)]

        def start_of(row, k):
            if row == 1:
                middle = rcv[s, pl.ds(PART + W * k, W)]
            else:
                middle = l_own[k, own_rows(s, 0)]
            return ringed(row, 8 + k, middle) if ring else middle

        if ring:
            receive(rcv.at[s, late], late_recv_sem.at[s])
        d = {}
        for row in (1, 2):
            d[row] = []
            for k in range(3):
                r = start_of(row, k) - part[row][k]
                step = u[row][k] + (inverse[row][k] * r) * (1.0 / theta_value)
                d[row].append(step if ring else jnp.where(inner_row, step, 0.0))
        v = {row: sym_apply(c[row], d[row]) for row in (1, 2)}
        d_sum = [weigh(d[1][k] + 2.0 * d[2][k])[0:W] for k in range(3)]
        v_sum = [weigh(v[1][k] + 2.0 * v[2][k])[0:W] for k in range(3)]
        c2 = [t[0:W] for t in c[2]]
        c3 = [t[0:W] for t in c[3]]
        d2 = [t[0:W] for t in d[2]]
        near = sym_apply(c2, [64.0 * d2[k] - d_sum[k] for k in range(3)])
        far = sym_apply([t[0:W] for t in c_sum[2]], d2)
        outer = [near[k] + far[k] - v_sum[k] for k in range(3)]
        d_sum = [weigh(d[2][k])[0:W] for k in range(3)]
        v_sum = [weigh(v[2][k])[0:W] for k in range(3)]
        near = sym_apply(c3, d_sum)
        if ring:
            nearer, farther = sides[s]
            rows_0, rows_1 = pl.ds(nearer, W, stride=W), pl.ds(farther, W, stride=W)
        else:
            nearer = jnp.where(s == 2, 0, W - 1)
            rows_0, rows_1 = line(nearer), line(jnp.where(s == 2, 1, W - 2))
        for k in range(3):
            r_own[k, rows_0] = r_own[k, rows_0] - 0.0625 * outer[k]
            r_own[k, rows_1] = r_own[k, rows_1] + 0.0625 * (near[k] + v_sum[k])
            d_own[k, rows_0] = d2[k]
            inv_own[k, rows_0] = inverse[2][k][0:W]

    def turn_strip(s):
        @pl.when(jnp.logical_or(first, last))
        def _():
            lines = [W * i for i in range(5)] + [PART + W * k for k in range(3)]
            for at, sign in zip(lines, VECTOR + (1.0, 1.0) + VECTOR):
                head, tail = rcv[s, at : at + 8], rcv[s, at + 8 : at + W]
                rcv[s, at : at + 8] = sign * turned(tail)
                rcv[s, at + 8 : at + W] = sign * turned(head)
            for k in range(3):
                one, two = rcv[s, ENDS + k], rcv[s, ENDS + 3 + k]
                rcv[s, ENDS + k] = VECTOR[k] * two
                rcv[s, ENDS + 3 + k] = VECTOR[k] * one

    def receive_edge(s):
        receive(rcv.at[s], recv_sem.at[s])

    side_a = jnp.where(lax.rem(gx, 2) == 0, 3, 2)
    side_b = 5 - side_a
    receive_edge(side_a)
    strip(side_a)
    receive_edge(side_b)
    turn_strip(side_b)

    for s in range(2):
        for j in range(2):
            at = sides[s][j]
            for side, spot in ((2, (7, 6)), (3, (0, 1))):
                for c in range(3):
                    t2o[s, 3 * j + c, spot[0]] = rcv[side, W * c + at]
                    if j == 0:
                        t2o[s, c, spot[1]] = rcv[side, ENDS + 3 * s + c]
                        t2o[s, 8 + c, spot[0]] = rcv[side, PART + W * c + at]
                for i in range(2):
                    t2o[s, 6 + j, spot[i]] = rcv[side, CODES + W * i + at]

    def receive_y(s):
        receive(rcv.at[s, early], recv_sem.at[s])
        for end in range(2):
            receive(corner_ref(s, end), recv_sem.at[4 + 2 * end + s])
        for mirrored, base in ((first, 6), (last, 0)):

            @pl.when(mirrored)
            def _():
                for i in range(VALUES):
                    one, two = t2g[s, i, base], t2g[s, i, base + 1]
                    t2g[s, i, base] = SIGNS[i] * two
                    t2g[s, i, base + 1] = SIGNS[i] * one

    receive_y(1)
    strip(side_b)
    strip(1)
    receive_y(0)
    strip(0)

    for n in range(4):
        for copy in edge(n, *to[n]):
            copy.wait_send()
    for n in range(4, 8):

        @pl.when(jnp.logical_not(here[n]))
        def _():
            source = csnd.at[n % 2, n // 6]
            pltpu.make_async_copy(source, source, send_sem.at[n]).wait()


def finish(u, r, d, inv, out_u, out_r, result, sem):
    copies = [pltpu.make_async_copy(r.at[:, pl.ds(0, CELLS)], out_r, sem.at[3])]
    copies[0].start()
    for k in range(3):
        copies.append(pltpu.make_async_copy(result.at[k], out_u.at[k], sem.at[k]))

        @pl.loop(0, W, unroll=8)
        def _(x):
            step = d[k, line(x)] - u[k, line(x)]
            step = (rho_second * rho_first) * step
            step += (2.0 * rho_second / delta_value) * (inv[k, line(x)] * r[k, line(x)])
            result[k, line(x)] = d[k, line(x)] + step

        copies[-1].start()
    for copy in copies:
        copy.wait()


def body(load, guess, labels, segments, stiffness):
    vmem = pl.BlockSpec(memory_space=pltpu.VMEM)
    hbm = pl.BlockSpec(memory_space=pltpu.HBM)
    shape = load.shape
    field = (3, W * W, 128)
    inputs = (
        load.reshape(field),
        guess.reshape(field),
        labels.reshape(field[1:]),
        segments.reshape(field[1:]),
        stiffness,
    )
    results = pl.pallas_call(
        kernel,
        out_shape=[pltpu.VMEM((3, ROOM, 128), f32)] * 4,
        in_specs=[hbm] * 5,
        out_specs=[vmem] * 4,
        scratch_shapes=[
            pltpu.VMEM(stiffness.shape, f32),
            pltpu.VMEM((8, 128), f32),
            pltpu.VMEM((3, ROOM, 128), f32),
            pltpu.VMEM((ROOM, 128), f32),
            pltpu.VMEM(field[1:], jnp.int32),
            pltpu.VMEM(field[1:], jnp.int32),
            pltpu.VMEM((6,) + field[1:], f32),
            pltpu.VMEM(field, f32),
            pltpu.VMEM((6,) + field[1:], f32),
            pltpu.VMEM((4, LINES, 128), f32),
            pltpu.VMEM((2, 2, VALUES, 2, 128), f32),
            pltpu.VMEM((4, LINES, 128), f32),
            pltpu.VMEM((2, VALUES, 8, 128), f32),
            pltpu.VMEM((2, VALUES, 8, 128), f32),
            pltpu.VMEM((4, 4, 6, RING, 128), f32),
            pltpu.SemaphoreType.DMA((5,)),
            pltpu.SemaphoreType.DMA((8,)),
            pltpu.SemaphoreType.DMA((4,)),
            pltpu.SemaphoreType.DMA((8,)),
            pltpu.SemaphoreType.DMA((4,)),
        ],
        compiler_params=pltpu.CompilerParams(
            collective_id=0, has_side_effects=True, vmem_limit_bytes=40 * 2**20
        ),
    )(*[pltpu.with_memory_space_constraint(x, pltpu.HBM) for x in inputs])
    out_u, out_r = pl.pallas_call(
        finish,
        out_shape=[jax.ShapeDtypeStruct(field, f32)] * 2,
        in_specs=[vmem] * 4,
        out_specs=[hbm] * 2,
        scratch_shapes=[pltpu.VMEM(field, f32), pltpu.SemaphoreType.DMA((4,))],
    )(*[pltpu.with_memory_space_constraint(x, pltpu.VMEM) for x in results])
    return out_u.reshape(shape), out_r.reshape(shape)


def solution(mesh):
    field = P(None, "gx", "gy", None)
    voxel = P("gx", "gy", None)
    return jax.shard_map(
        body,
        mesh=mesh,
        in_specs=(field, field, voxel, voxel, P()),
        out_specs=(field, field),
        check_vma=False,
    )
```

```python
import functools

import jax
import jax.numpy as jnp
from jax import lax
from jax.experimental import pallas as pl
from jax.experimental.pallas import tpu as pltpu
from jax.sharding import PartitionSpec as P

SEGS = 16
MESH = pl.DeviceIdType.MESH
f32 = jnp.float32

theta_value = 1.025
delta_value = 0.975
sigma_value = theta_value / delta_value
rho_first = 1.0 / sigma_value
rho_second = 1.0 / (2.0 * sigma_value - rho_first)

W = 16
RING = W + 8
CELLS = W * W
ROOM = CELLS + W
CODES, ENDS, PART, LINES = 3 * W, 5 * W, 5 * W + 8, 8 * W + 8
VALUES = 11
VECTOR = (-1.0, -1.0, 1.0)
SIGNS = VECTOR * 2 + (1.0, 1.0) + VECTOR


def routes(gx, gy):
    nx, ny = lax.axis_size("gx"), lax.axis_size("gy")
    first, last = gx == 0, gx == nx - 1
    xl = jnp.where(first, 0, gx - 1)
    xh = jnp.where(last, nx - 1, gx + 1)
    down, up = lax.rem(gy + ny - 1, ny), lax.rem(gy + 1, ny)
    mid = ny - 1 - gy
    mid_down, mid_up = lax.rem(mid + ny - 1, ny), lax.rem(mid + 1, ny)
    pick = jnp.where
    return [
        ((gx, down), 1),
        ((gx, up), 0),
        ((xl, pick(first, mid, gy)), pick(first, 2, 3)),
        ((xh, pick(last, mid, gy)), pick(last, 3, 2)),
        ((xl, pick(first, mid_up, down)), (7, 4)),
        ((xl, pick(first, mid_down, up)), (6, 5)),
        ((xh, pick(last, mid_up, down)), (5, 6)),
        ((xh, pick(last, mid_down, up)), (4, 7)),
    ]


def sym_apply(c, u):
    return (
        c[0] * u[0] + c[3] * u[1] + c[4] * u[2],
        c[3] * u[0] + c[1] * u[1] + c[5] * u[2],
        c[4] * u[0] + c[5] * u[1] + c[2] * u[2],
    )


def along_row(h):
    n = h.shape[0]
    return (h + h) + (pltpu.roll(h, 1, 0) + pltpu.roll(h, n - 1, 0))


def along_depth(h, repeat=False):
    lane = lax.broadcasted_iota(jnp.int32, h.shape, 1)
    end = h if repeat else jnp.zeros_like(h)
    below = jnp.where(lane == 0, end, pltpu.roll(h, 1, 1))
    above = jnp.where(lane == 127, end, pltpu.roll(h, 127, 1))
    return (h + h) + (below + above)


def along_open_row(h):
    place = lax.broadcasted_iota(jnp.int32, h.shape, 0)
    n = h.shape[0]
    below = jnp.where(place == 0, 0.0, pltpu.roll(h, 1, 0))
    above = jnp.where(place == n - 1, 0.0, pltpu.roll(h, n - 1, 0))
    return (h + h) + (below + above)


def weigh(h, repeat=False):
    return along_depth(along_row(h), repeat)


def line(x):
    return pl.ds(W * x, W) if isinstance(x, int) else pl.ds(pl.multiple_of(W * x, W), W)


def kernel(
    load, guess, labels, segments, stiffness, u_own, r_own, d_own, inv_own,
    blocks, table, l_own, k_own, lab, seg, c_own, v_own, cs_own, snd, csnd, rcv, t2g, t2o, c_strip,
    local_sem, send_sem, late_send_sem, recv_sem, late_recv_sem,
):
    gx, gy = lax.axis_index("gx"), lax.axis_index("gy")
    first, last = gx == 0, gx == lax.axis_size("gx") - 1
    t2g[...] = jnp.zeros(t2g.shape, f32)

    to = routes(gx, gy)
    here = [None] * 4 + [jnp.logical_and(d[0] == gx, d[1] == gy) for d, _ in to[4:]]
    barrier = pltpu.get_barrier_semaphore()
    expected = 4
    for (device, _), same in zip(to, here):
        if same is None:
            pl.semaphore_signal(barrier, inc=1, device_id=device, device_id_type=MESH)
        else:

            @pl.when(jnp.logical_not(same))
            def _():
                pl.semaphore_signal(barrier, inc=1, device_id=device, device_id_type=MESH)

            expected = expected + jnp.where(same, 0, 1)

    fetch = [
        pltpu.make_async_copy(labels, lab, local_sem.at[0]),
        pltpu.make_async_copy(segments, seg, local_sem.at[1]),
        pltpu.make_async_copy(stiffness, blocks, local_sem.at[4]),
        pltpu.make_async_copy(guess, u_own.at[:, pl.ds(0, CELLS)], local_sem.at[2]),
        pltpu.make_async_copy(load, l_own.at[:, pl.ds(0, CELLS)], local_sem.at[3]),
    ]
    for copy in fetch:
        copy.start()
    t2o[...] = jnp.zeros(t2o.shape, f32)
    fetch[0].wait()
    fetch[1].wait()
    k_own[0:CELLS] = (lab[...] * SEGS + seg[...]).astype(f32)
    fetch[3].wait()
    fetch[4].wait()
    sides = ((0, 1), (W - 1, W - 2))

    def own_rows(s, j):
        if isinstance(s, int):
            return pl.ds(sides[s % 2][j], W, stride=W) if s < 2 else line(sides[s % 2][j])
        return line(jnp.where(s == 2, sides[0][j], sides[1][j]))

    for s in range(4):
        for c in range(3):
            snd[s, line(c)] = u_own[c, own_rows(s, 0)]
            for end in range(2):
                at = sides[s % 2][1]
                at = (W * (W - 1) * end + at) if s < 2 else (W * at + (W - 1) * end)
                snd[s, ENDS + 3 * end + c] = u_own[c, at]
        for j in range(2):
            snd[s, line(3 + j)] = k_own[own_rows(s, j)]
    for s in range(2):
        for end in range(2):
            for j in range(2):
                at = sides[s][j] + W * (W - 2) * end
                for i in range(2):
                    for c in range(3):
                        csnd[s, end, 3 * j + c, i] = u_own[c, at + W * i]
                        if j == 0:
                            csnd[s, end, 8 + c, i] = l_own[c, at + W * i]
                    csnd[s, end, 6 + j, i] = k_own[at + W * i]
    fetch[2].wait()
    table[0:6, 0 : stiffness.shape[1]] = blocks[...]

    def lookup(codes, entry):
        rows = jnp.broadcast_to(table[entry : entry + 1, :], codes.shape)
        return jnp.take_along_axis(rows, codes, axis=1, mode="promise_in_bounds")

    for s in range(4):
        c, u = [], []
        for j in range(2):
            codes = snd[s, line(3 + j)].astype(jnp.int32)
            c.append([lookup(codes, e) for e in range(6)])
            u.append([u_own[k, own_rows(s, j)] for k in range(3)])
            for e in range(6):
                c_strip[s, 2 + j, e, 0:W] = c[j][e]
        v = [sym_apply(c[j], u[j]) for j in range(2)]
        u_sum = [along_depth(along_open_row(2.0 * u[0][k] + u[1][k])) for k in range(3)]
        v_sum = [along_depth(along_open_row(2.0 * v[0][k] + v[1][k])) for k in range(3)]
        near = sym_apply(c[0], [64.0 * u[0][k] - u_sum[k] for k in range(3)])
        for k in range(3):
            part = l_own[k, own_rows(s, 0)] - 0.0625 * (near[k] - v_sum[k])
            snd[s, pl.ds(PART + W * k, W)] = part

    pl.semaphore_wait(barrier, expected)

    early, late = pl.ds(0, PART), pl.ds(PART, LINES - PART)
    parts = ((early, send_sem, recv_sem), (late, late_send_sem, late_recv_sem))

    whole = ((pl.ds(0, LINES), send_sem, recv_sem),)

    def n_is_y(n):
        return not isinstance(n, int) or n < 2

    def edge(n, device, slot):
        return [
            pltpu.make_async_remote_copy(
                src_ref=snd.at[n, values],
                dst_ref=rcv.at[slot, values],
                send_sem=out_sem.at[n],
                recv_sem=in_sem.at[slot],
                device_id=device,
                device_id_type=MESH,
            )
            for values, out_sem, in_sem in (parts if n_is_y(n) else whole)
        ]

    def corner_ref(side, end):
        return t2g.at[side, :, pl.ds(0 if end else 6, 2)]

    def send_x(n):
        for copy in edge(n, *to[n]):
            copy.start()

    def send_y(side):
        for copy in edge(side, (gx, jnp.where(side == 0, to[0][0][1], to[1][0][1])), 1 - side):
            copy.start()

    def send_corners(side):
        for end in range(2):
            low, high = to[4 + 2 * end][0], to[5 + 2 * end][0]
            device = (low[0], jnp.where(side == 0, low[1], high[1]))
            same = jnp.where(side == 0, here[4 + 2 * end], here[5 + 2 * end])
            mirrored = (first, last)[end]
            n = 4 + 2 * end + side
            source = csnd.at[side, end]

            def remote(target, slot):
                return pltpu.make_async_remote_copy(
                    src_ref=source,
                    dst_ref=target,
                    send_sem=send_sem.at[n],
                    recv_sem=recv_sem.at[slot],
                    device_id=device,
                    device_id_type=MESH,
                )

            ahead = remote(corner_ref(1 - side, 1 - end), 4 + 2 * (1 - end) + (1 - side))
            back = remote(corner_ref(side, end), n)
            local = pltpu.make_async_copy(source, corner_ref(side, end), recv_sem.at[n])
            pl.when(jnp.logical_not(mirrored))(ahead.start)
            pl.when(jnp.logical_and(mirrored, jnp.logical_not(same)))(back.start)
            pl.when(same)(local.start)

    group = lax.rem(gy, 4)
    odd = lax.rem(lax.div(gx, 2), 2)
    hasty = jnp.where(group == 0, odd, jnp.where(group == 3, 1, 0))
    mirrors = ((2, first), (3, last))

    @pl.when(group == 0)
    def _():
        upper = lax.rem(gx, 2) == 1
        pl.when(jnp.logical_and(upper, jnp.logical_not(last)))(lambda: send_x(3))
        pl.when(jnp.logical_not(first))(lambda: send_x(2))
        pl.when(jnp.logical_not(jnp.logical_or(upper, last)))(lambda: send_x(3))

    send_corners(hasty)
    send_corners(1 - hasty)

    @pl.when(group == 3)
    def _():
        for n, mirrored in mirrors:
            pl.when(mirrored)(lambda: send_x(n))
    send_y(hasty)

    @pl.when(group == 2)
    def _():
        for n, mirrored in mirrors:
            pl.when(mirrored)(lambda: send_x(n))

    @pl.when(group != 0)
    def _():
        for n, mirrored in mirrors:
            pl.when(jnp.logical_not(mirrored))(lambda: send_x(n))

    send_y(1 - hasty)

    @pl.when(group < 2)
    def _():
        for n, mirrored in mirrors:
            pl.when(mirrored)(lambda: send_x(n))

    def receive(ref, sem):
        pltpu.make_async_copy(ref, ref, sem).wait()

    inner_row = lax.broadcasted_iota(jnp.int32, (W, 128), 0)
    inner_row = jnp.logical_and(inner_row > 0, inner_row < W - 1)
    none = jnp.zeros((W, 128), f32)
    for x in (0, W - 1):
        for c in range(3):
            d_own[c, line(x)] = none
        for e in range(6):
            cs_own[e, line(x)] = none

    @pl.loop(0, W, unroll=4)
    def _(x):
        codes = k_own[line(x)].astype(jnp.int32)
        c = [lookup(codes, e) for e in range(6)]
        for e in range(6):
            c_own[e, line(x)] = c[e]
        v = sym_apply(c, [u_own[k, line(x)] for k in range(3)])
        for k in range(3):
            v_own[k, line(x)] = v[k]

    def three(ref, e, x):
        return (ref[e, line(x - 1)] + ref[e, line(x + 1)]) + 2.0 * ref[e, line(x)]

    @pl.loop(1, W - 1, unroll=2)
    def _(x):
        c = [c_own[e, line(x)] for e in range(6)]
        u = [u_own[k, line(x)] for k in range(3)]
        c_sum = [weigh(three(c_own, e, x), True) for e in range(6)]
        u_sum = [weigh(three(u_own, k, x)) for k in range(3)]
        v_sum = [weigh(three(v_own, k, x)) for k in range(3)]
        near = sym_apply(c, [64.0 * u[k] - u_sum[k] for k in range(3)])
        far = sym_apply(c_sum, u)
        for k in range(3):
            r = l_own[k, line(x)] - 0.0625 * (near[k] + far[k] - v_sum[k])
            inverse = 16.0 / (48.0 * c[k] + c_sum[k])
            d = u[k] + (inverse * r) * (1.0 / theta_value)
            inv_own[k, line(x)] = inverse
            d_own[k, line(x)] = jnp.where(inner_row, d, 0.0)
        for e in range(6):
            cs_own[e, line(x)] = c_sum[e]

    @pl.loop(0, W, unroll=4)
    def _(x):
        v = sym_apply([c_own[e, line(x)] for e in range(6)], [d_own[k, line(x)] for k in range(3)])
        for k in range(3):
            v_own[k, line(x)] = v[k]

    def three_within(ref, e, x):
        below, above = jnp.maximum(x - 1, 0), jnp.minimum(x + 1, W - 1)
        return (ref[e, line(below)] + ref[e, line(above)]) + 2.0 * ref[e, line(x)]

    @pl.loop(0, W, unroll=2)
    def _(x):
        c = [c_own[e, line(x)] for e in range(6)]
        c_sum = [cs_own[e, line(x)] for e in range(6)]
        d = [d_own[k, line(x)] for k in range(3)]
        d_sum = [weigh(three_within(d_own, k, x)) for k in range(3)]
        v_sum = [weigh(three_within(v_own, k, x)) for k in range(3)]
        near = sym_apply(c, [64.0 * d[k] - d_sum[k] for k in range(3)])
        far = sym_apply(c_sum, d)
        for k in range(3):
            r_own[k, line(x)] = l_own[k, line(x)] - 0.0625 * (near[k] + far[k] - v_sum[k])

    turn = 7 - lax.broadcasted_iota(jnp.int32, (8, 128), 0)

    def turned(tile):
        return jnp.take_along_axis(tile, turn, axis=0, mode="promise_in_bounds")

    eight = lax.broadcasted_iota(jnp.int32, (8, 128), 0)
    low_sign = jnp.where(first, -1.0, 1.0)
    high_sign = jnp.where(last, -1.0, 1.0)
    end_sign = jnp.where(eight > 5, low_sign, jnp.where(eight < 2, high_sign, 1.0))

    def strip(s):
        ring = isinstance(s, int)
        n = RING if ring else W

        def ringed(row, index, middle):
            return jnp.concatenate([middle, (t2g if row < 2 else t2o)[s, index]], axis=0)

        place = lax.broadcasted_iota(jnp.int32, (W, 128), 0)
        c, u = [], []
        for row in range(4):
            layer = (1, 0, 0, 1)[row]
            codes = (rcv if row < 2 else snd)[s, line(3 + layer)].astype(jnp.int32)
            if row < 2:
                for e in range(6):
                    entry = lookup(codes, e)
                    if e > 3 and not ring:
                        entry = entry * jnp.where(s == 2, low_sign, high_sign)
                    c_strip[s, row, e, 0:W] = entry
            if ring:
                codes = (t2g if row < 2 else t2o)[s, 6 + layer].astype(jnp.int32)
                for e in range(6):
                    entry = lookup(codes, e)
                    c_strip[s, row, e, W:RING] = entry * end_sign if e > 3 else entry
            c.append([c_strip[s, row, e, 0:n] for e in range(6)])
            u.append([])
            for k in range(3):
                if row == 0:
                    low_end = jnp.broadcast_to(rcv[s, pl.ds(ENDS + k, 1)], (W, 128))
                    high_end = jnp.broadcast_to(rcv[s, pl.ds(ENDS + 3 + k, 1)], (W, 128))
                    middle = jnp.where(place == 0, low_end, 0.0)
                    middle = jnp.where(place == W - 1, high_end, middle)
                elif row == 1:
                    middle = rcv[s, line(k)]
                else:
                    middle = u_own[k, own_rows(s, layer)]
                u[row].append(ringed(row, 3 * layer + k, middle) if ring else middle)
        v = [sym_apply(c[row], u[row]) if ring or row > 0 else None for row in range(4)]

        def three_rows(f, row, k):
            return (f[row - 1][k] + f[row + 1][k]) + 2.0 * f[row][k]

        def sums(f, row, k):
            if not ring:
                return weigh(f[2][k] if row == 1 else three_rows(f, row, k))
            whole = three_rows(f, row, k)
            rest = jnp.concatenate(
                [f[2][k][0:W], whole[W:RING]] if row == 1 else [whole[0:W], f[1][k][W:RING]],
                axis=0,
            )
            middle, ends = (rest, whole) if row == 1 else (whole, rest)
            h = jnp.concatenate([along_row(middle)[0:W], along_row(ends)[W:RING]], axis=0)
            return along_depth(h)

        tail = (lax.broadcasted_iota(jnp.int32, (n, 128), 0) >= W) if ring else None
        raw = {1: jnp.where(tail, 64.0, 0.0) if ring else 0.0, 2: jnp.where(tail, 0.0, 64.0) if ring else 64.0}
        part, inverse, c_sum = {}, {}, {}
        for row in (1, 2):
            c_sum[row] = [weigh(three_rows(c, row, e), True) for e in range(6)]
            u_sum = [sums(u, row, k) for k in range(3)]
            v_sum = [sums(v, row, k) for k in range(3)]
            near = sym_apply(c[row], [raw[row] * u[row][k] - u_sum[k] for k in range(3)])
            far = sym_apply(c_sum[row], u[row])
            part[row] = [0.0625 * (near[k] + far[k] - v_sum[k]) for k in range(3)]
            inverse[row] = [16.0 / (48.0 * c[row][k] + c_sum[row][k]) for k in range(3)]

        def start_of(row, k):
            if row == 1:
                middle = rcv[s, pl.ds(PART + W * k, W)]
            else:
                middle = l_own[k, own_rows(s, 0)]
            return ringed(row, 8 + k, middle) if ring else middle

        if ring:
            receive(rcv.at[s, late], late_recv_sem.at[s])
        d = {}
        for row in (1, 2):
            d[row] = []
            for k in range(3):
                r = start_of(row, k) - part[row][k]
                step = u[row][k] + (inverse[row][k] * r) * (1.0 / theta_value)
                d[row].append(step if ring else jnp.where(inner_row, step, 0.0))
        v = {row: sym_apply(c[row], d[row]) for row in (1, 2)}
        d_sum = [weigh(d[1][k] + 2.0 * d[2][k])[0:W] for k in range(3)]
        v_sum = [weigh(v[1][k] + 2.0 * v[2][k])[0:W] for k in range(3)]
        c2 = [t[0:W] for t in c[2]]
        c3 = [t[0:W] for t in c[3]]
        d2 = [t[0:W] for t in d[2]]
        near = sym_apply(c2, [64.0 * d2[k] - d_sum[k] for k in range(3)])
        far = sym_apply([t[0:W] for t in c_sum[2]], d2)
        outer = [near[k] + far[k] - v_sum[k] for k in range(3)]
        d_sum = [weigh(d[2][k])[0:W] for k in range(3)]
        v_sum = [weigh(v[2][k])[0:W] for k in range(3)]
        near = sym_apply(c3, d_sum)
        if ring:
            nearer, farther = sides[s]
            rows_0, rows_1 = pl.ds(nearer, W, stride=W), pl.ds(farther, W, stride=W)
        else:
            nearer = jnp.where(s == 2, 0, W - 1)
            rows_0, rows_1 = line(nearer), line(jnp.where(s == 2, 1, W - 2))
        for k in range(3):
            r_own[k, rows_0] = r_own[k, rows_0] - 0.0625 * outer[k]
            r_own[k, rows_1] = r_own[k, rows_1] + 0.0625 * (near[k] + v_sum[k])
            d_own[k, rows_0] = d2[k]
            inv_own[k, rows_0] = inverse[2][k][0:W]

    def turn_strip(s):
        @pl.when(jnp.logical_or(first, last))
        def _():
            lines = [W * i for i in range(5)] + [PART + W * k for k in range(3)]
            for at, sign in zip(lines, VECTOR + (1.0, 1.0) + VECTOR):
                head, tail = rcv[s, at : at + 8], rcv[s, at + 8 : at + W]
                rcv[s, at : at + 8] = sign * turned(tail)
                rcv[s, at + 8 : at + W] = sign * turned(head)
            for k in range(3):
                one, two = rcv[s, ENDS + k], rcv[s, ENDS + 3 + k]
                rcv[s, ENDS + k] = VECTOR[k] * two
                rcv[s, ENDS + 3 + k] = VECTOR[k] * one

    def receive_edge(s):
        receive(rcv.at[s], recv_sem.at[s])

    side_a = jnp.where(lax.rem(gx, 2) == 0, 3, 2)
    side_b = 5 - side_a
    receive_edge(side_a)
    strip(side_a)
    receive_edge(side_b)
    turn_strip(side_b)

    for s in range(2):
        for j in range(2):
            at = sides[s][j]
            for side, spot in ((2, (7, 6)), (3, (0, 1))):
                for c in range(3):
                    t2o[s, 3 * j + c, spot[0]] = rcv[side, W * c + at]
                    if j == 0:
                        t2o[s, c, spot[1]] = rcv[side, ENDS + 3 * s + c]
                        t2o[s, 8 + c, spot[0]] = rcv[side, PART + W * c + at]
                for i in range(2):
                    t2o[s, 6 + j, spot[i]] = rcv[side, CODES + W * i + at]

    def receive_y(s):
        receive(rcv.at[s, early], recv_sem.at[s])
        for end in range(2):
            receive(corner_ref(s, end), recv_sem.at[4 + 2 * end + s])
        for mirrored, base in ((first, 6), (last, 0)):

            @pl.when(mirrored)
            def _():
                for i in range(VALUES):
                    one, two = t2g[s, i, base], t2g[s, i, base + 1]
                    t2g[s, i, base] = SIGNS[i] * two
                    t2g[s, i, base + 1] = SIGNS[i] * one

    receive_y(1)
    strip(side_b)
    strip(1)
    receive_y(0)
    strip(0)

    for n in range(4):
        for copy in edge(n, *to[n]):
            copy.wait_send()
    for n in range(4, 8):

        @pl.when(jnp.logical_not(here[n]))
        def _():
            source = csnd.at[n % 2, n // 6]
            pltpu.make_async_copy(source, source, send_sem.at[n]).wait()


def finish(u, r, d, inv, out_u, out_r, result, sem):
    copies = [pltpu.make_async_copy(r.at[:, pl.ds(0, CELLS)], out_r, sem.at[3])]
    copies[0].start()
    for k in range(3):
        copies.append(pltpu.make_async_copy(result.at[k], out_u.at[k], sem.at[k]))

        @pl.loop(0, W, unroll=8)
        def _(x):
            step = d[k, line(x)] - u[k, line(x)]
            step = (rho_second * rho_first) * step
            step += (2.0 * rho_second / delta_value) * (inv[k, line(x)] * r[k, line(x)])
            result[k, line(x)] = d[k, line(x)] + step

        copies[-1].start()
    for copy in copies:
        copy.wait()


def body(load, guess, labels, segments, stiffness):
    vmem = pl.BlockSpec(memory_space=pltpu.VMEM)
    hbm = pl.BlockSpec(memory_space=pltpu.HBM)
    shape = load.shape
    field = (3, W * W, 128)
    inputs = (
        load.reshape(field),
        guess.reshape(field),
        labels.reshape(field[1:]),
        segments.reshape(field[1:]),
        stiffness,
    )
    results = pl.pallas_call(
        kernel,
        out_shape=[pltpu.VMEM((3, ROOM, 128), f32)] * 4,
        in_specs=[hbm] * 5,
        out_specs=[vmem] * 4,
        scratch_shapes=[
            pltpu.VMEM(stiffness.shape, f32),
            pltpu.VMEM((8, 128), f32),
            pltpu.VMEM((3, ROOM, 128), f32),
            pltpu.VMEM((ROOM, 128), f32),
            pltpu.VMEM(field[1:], jnp.int32),
            pltpu.VMEM(field[1:], jnp.int32),
            pltpu.VMEM((6,) + field[1:], f32),
            pltpu.VMEM(field, f32),
            pltpu.VMEM((6,) + field[1:], f32),
            pltpu.VMEM((4, LINES, 128), f32),
            pltpu.VMEM((2, 2, VALUES, 2, 128), f32),
            pltpu.VMEM((4, LINES, 128), f32),
            pltpu.VMEM((2, VALUES, 8, 128), f32),
            pltpu.VMEM((2, VALUES, 8, 128), f32),
            pltpu.VMEM((4, 4, 6, RING, 128), f32),
            pltpu.SemaphoreType.DMA((5,)),
            pltpu.SemaphoreType.DMA((8,)),
            pltpu.SemaphoreType.DMA((4,)),
            pltpu.SemaphoreType.DMA((8,)),
            pltpu.SemaphoreType.DMA((4,)),
        ],
        compiler_params=pltpu.CompilerParams(
            collective_id=0, has_side_effects=True, vmem_limit_bytes=40 * 2**20
        ),
    )(*[pltpu.with_memory_space_constraint(x, pltpu.HBM) for x in inputs])
    out_u, out_r = pl.pallas_call(
        finish,
        out_shape=[jax.ShapeDtypeStruct(field, f32)] * 2,
        in_specs=[vmem] * 4,
        out_specs=[hbm] * 2,
        scratch_shapes=[pltpu.VMEM(field, f32), pltpu.SemaphoreType.DMA((4,))],
    )(*[pltpu.with_memory_space_constraint(x, pltpu.VMEM) for x in results])
    return out_u.reshape(shape), out_r.reshape(shape)


def solution(mesh):
    field = P(None, "gx", "gy", None)
    voxel = P("gx", "gy", None)
    return jax.shard_map(
        body,
        mesh=mesh,
        in_specs=(field, field, voxel, voxel, P()),
        out_specs=(field, field),
        check_vma=False,
    )
```
